32 devices in a mesh: stream: 2 (over y), dp: 16 (over z, x, core).
Axes of the slice: x: 2, y: 2, z: 4, core: 2. Of those that a mesh axis runs over, the one named last changes fastest.
Arguments:
- tokens: bfloat16 [2, 256, 36, 768], P('stream', 'dp'), may hold values from -6 to 6
- region_mask: int32 [256, 36], P('dp'), may hold values from 0 to 1, as said below
- cotangent: bfloat16 [2, 256, 36, 768], P('stream', 'dp'), may hold values from -6 to 6
- cross_qkv: bfloat16 [768, 2304], replicated, may hold values from -0.21875 to 0.21875
- cross_q_bias: float32 [768], replicated, may hold values from -1.75 to 1.75
- cross_v_bias: float32 [768], replicated, may hold values from -1.75 to 1.75
- cross_out: bfloat16 [768, 768], replicated, may hold values from -0.875 to 0.875
- cross_out_bias: float32 [768], replicated, may hold values from -1.75 to 1.75
- cross_gain: float32 [768], replicated, may hold values from 0.5 to 1.5
- cross_shift: float32 [768], replicated, may hold values from -1.75 to 1.75
- self_qkv: bfloat16 [2, 768, 2304], P('stream'), may hold values from -0.21875 to 0.21875
- self_q_bias: float32 [2, 768], P('stream'), may hold values from -1.75 to 1.75
- self_v_bias: float32 [2, 768], P('stream'), may hold values from -1.75 to 1.75
- self_out: bfloat16 [2, 768, 768], P('stream'), may hold values from -0.875 to 0.875
- self_out_bias: float32 [2, 768], P('stream'), may hold values from -1.75 to 1.75
- self_gain: float32 [2, 768], P('stream'), may hold values from 0.5 to 1.5
- self_shift: float32 [2, 768], P('stream'), may hold values from -1.75 to 1.75
- ffn_in: bfloat16 [2, 768, 3072], P('stream'), may hold values from -0.21875 to 0.21875
- ffn_in_bias: float32 [2, 3072], P('stream'), may hold values from -1.75 to 1.75
- ffn_out: bfloat16 [2, 3072, 768], P('stream'), may hold values from -0.21875 to 0.21875
- ffn_out_bias: float32 [2, 768], P('stream'), may hold values from -1.75 to 1.75
- ffn_gain: float32 [2, 768], P('stream'), may hold values from 0.5 to 1.5
- ffn_shift: float32 [2, 768], P('stream'), may hold values from -1.75 to 1.75
Outputs:
- stream_out: bfloat16 [2, 256, 36, 768], P('stream', 'dp')
- tokens_grad: float32 [2, 256, 36, 768], P('stream', 'dp')
- cross_qkv_grad: float32 [768, 2304], P('dp')
- cross_q_bias_grad: float32 [768], P('dp')
- cross_v_bias_grad: float32 [768], P('dp')
- cross_out_grad: float32 [768, 768], P('dp')
- cross_out_bias_grad: float32 [768], P('dp')
- cross_gain_grad: float32 [768], P('dp')
- cross_shift_grad: float32 [768], P('dp')
- self_qkv_grad: float32 [2, 768, 2304], P('stream', 'dp')
- self_q_bias_grad: float32 [2, 768], P('stream', 'dp')
- self_v_bias_grad: float32 [2, 768], P('stream', 'dp')
- self_out_grad: float32 [2, 768, 768], P('stream', 'dp')
- self_out_bias_grad: float32 [2, 768], P('stream', 'dp')
- self_gain_grad: float32 [2, 768], P('stream', 'dp')
- self_shift_grad: float32 [2, 768], P('stream', 'dp')
- ffn_in_grad: float32 [2, 768, 3072], P('stream', 'dp')
- ffn_in_bias_grad: float32 [2, 3072], P('stream', 'dp')
- ffn_out_grad: float32 [2, 3072, 768], P('stream', 'dp')
- ffn_out_bias_grad: float32 [2, 768], P('stream', 'dp')
- ffn_gain_grad: float32 [2, 768], P('stream', 'dp')
- ffn_shift_grad: float32 [2, 768], P('stream', 'dp')
The draws below stay inside these ranges and needn't reach their ends.
Inputs may be any that keep to these rules, and one draw needn't show every extreme that they name: `region_mask`: each row is ones in its first positions and zeros after, with 10 to 36 ones; in every block of 16 items one item, drawn from the seed, has 36.
All inputs are finite; a program needn't handle non-finite values.
Results may differ from the reference program's by a relative error of at most 0.023.
Values may be sent and summed in bfloat16 or wider, within the bound.
A program may use at most 192 MiB of HBM per device.

```python
import jax
import jax.numpy as jnp
from jax import lax

D = 768
H = 12
HD = 64
FF = 3072
LW = 20
LR = 36
ITEMS_DEV = 16
ITEMS = 256


def draw_region_mask(key, part):
    key = jax.random.fold_in(key, 11)
    count_key, pick_key = jax.random.split(key)
    counts = jax.random.randint(count_key, (ITEMS,), 10, LR + 1)
    picked = jax.random.randint(pick_key, (ITEMS // ITEMS_DEV,), 0, ITEMS_DEV)
    place = jnp.arange(ITEMS) % ITEMS_DEV
    chosen = jnp.repeat(picked, ITEMS_DEV, total_repeat_length=ITEMS)
    counts = jnp.where(place == chosen, LR, counts)
    return (jnp.arange(LR)[None, :] < counts[:, None]).astype(jnp.int32)


def block_levels(stream_key, extent, cuts, least, largest):
    loudness = 1.0
    for dim, shards_of in cuts:
        steps = jax.random.uniform(jax.random.fold_in(jax.random.fold_in(stream_key, 6), dim), (shards_of,), jnp.float32, least / len(cuts), largest / len(cuts))
        loudness = loudness * jnp.repeat(jnp.exp(steps), extent[dim] // shards_of).reshape((-1,) + (1,) * (len(extent) - 1 - dim))
    return loudness


def normal_values(stream_key, dims, width, limit, cuts=(), kind=jnp.bfloat16):
    values = jax.random.normal(stream_key, dims, jnp.float32) * width
    if len(cuts) > 0:
        values = block_levels(stream_key, dims, cuts, -0.22, 0.18) * values
    return jnp.clip(values, min=-limit, max=limit).astype(kind)


def setup_inputs(seed: int = 0) -> dict:
    key_of = jax.random.split(jax.random.key(seed), 24)
    return {
        "tokens": normal_values(key_of[0], (2, ITEMS, LR, D), 1.0, 6.0, ((0, 2), (1, 16))),
        "region_mask": draw_region_mask(jax.random.fold_in(key_of[23], 71), 0),
        "cotangent": normal_values(key_of[2], (2, ITEMS, LR, D), 1.0, 6.0, ((0, 2), (1, 16))),
        "cross_qkv": normal_values(key_of[3], (D, 3 * D), D ** -0.5, 0.21875),
        "cross_q_bias": normal_values(key_of[4], (D,), 0.3, 1.75, (), jnp.float32),
        "cross_v_bias": normal_values(key_of[5], (D,), 0.3, 1.75, (), jnp.float32),
        "cross_out": normal_values(key_of[6], (D, D), (D // 16) ** -0.5, 0.875),
        "cross_out_bias": normal_values(key_of[7], (D,), 0.3, 1.75, (), jnp.float32),
        "cross_gain": jnp.clip(1.0 + 0.1 * jax.random.normal(key_of[8], (D,), jnp.float32), 0.5, 1.5),
        "cross_shift": normal_values(key_of[9], (D,), 0.3, 1.75, (), jnp.float32),
        "self_qkv": normal_values(key_of[10], (2, D, 3 * D), D ** -0.5, 0.21875, ((0, 2),)),
        "self_q_bias": normal_values(key_of[11], (2, D), 0.3, 1.75, ((0, 2),), jnp.float32),
        "self_v_bias": normal_values(key_of[12], (2, D), 0.3, 1.75, ((0, 2),), jnp.float32),
        "self_out": normal_values(key_of[13], (2, D, D), (D // 16) ** -0.5, 0.875, ((0, 2),)),
        "self_out_bias": normal_values(key_of[14], (2, D), 0.3, 1.75, ((0, 2),), jnp.float32),
        "self_gain": jnp.clip(1.0 + 0.1 * jax.random.normal(key_of[15], (2, D), jnp.float32), 0.5, 1.5),
        "self_shift": normal_values(key_of[16], (2, D), 0.3, 1.75, ((0, 2),), jnp.float32),
        "ffn_in": normal_values(key_of[17], (2, D, FF), D ** -0.5, 0.21875, ((0, 2),)),
        "ffn_in_bias": normal_values(key_of[18], (2, FF), 0.3, 1.75, ((0, 2),), jnp.float32),
        "ffn_out": normal_values(key_of[19], (2, FF, D), (FF // 4) ** -0.5, 0.21875, ((0, 2),)),
        "ffn_out_bias": normal_values(key_of[20], (2, D), 0.3, 1.75, ((0, 2),), jnp.float32),
        "ffn_gain": jnp.clip(1.0 + 0.1 * jax.random.normal(key_of[21], (2, D), jnp.float32), 0.5, 1.5),
        "ffn_shift": normal_values(key_of[22], (2, D), 0.3, 1.75, ((0, 2),), jnp.float32),
    }


@jax.custom_vjp
def low(v):
    return lax.optimization_barrier(v.astype(jnp.bfloat16)).astype(jnp.float32)

@jax.custom_vjp
def low_back(v):
    return v

def low_keep(v):
    return (low(v), None)

def low_pass(kept, grad):
    return (grad,)

def back_keep(v):
    return (v, None)

def back_low(kept, grad):
    return (low(grad),)
low.defvjp(low_keep, low_pass)
low_back.defvjp(back_keep, back_low)

def round_both(value_in):
    return low_back(low(value_in))

def matmul(left, right):
    return jnp.dot(left, right, precision=lax.Precision.HIGHEST)

def layer_norm(row_block, norm_gain, norm_shift):
    centre = row_block - lax.optimization_barrier(jnp.mean(row_block, axis=-1, keepdims=True))
    spread = lax.optimization_barrier(jnp.mean(centre * centre, axis=-1, keepdims=True))
    return centre * lax.rsqrt(spread + 1e-12) * norm_gain + norm_shift

def project(row_block, weight, q_bias, v_bias):
    projected = matmul(low(row_block), weight)
    query_rows = round_both(projected[..., :D] + q_bias)
    key_rows = round_both(projected[..., D:2 * D])
    value_rows = round_both(projected[..., 2 * D:] + v_bias)
    return (query_rows, key_rows, value_rows)

def attend(query_rows, key_rows, value_rows, key_mask):
    item_count, query_len, row_width = query_rows.shape
    key_len = key_rows.shape[1]
    query_heads = query_rows.reshape(item_count, query_len, H, HD)
    key_heads = key_rows.reshape(item_count, key_len, H, HD)
    value_heads = value_rows.reshape(item_count, key_len, H, HD)
    scores = jnp.einsum('bqhd,bkhd->bhqk', query_heads, key_heads, precision=lax.Precision.HIGHEST) * (1.0 / HD ** 0.5)
    scores = low_back(scores)
    scores = jnp.where(key_mask[:, None, None, :] > 0, scores, -1000000000.0)
    probability = low(jax.nn.softmax(scores, axis=-1))
    attended = jnp.einsum('bhqk,bkhd->bqhd', probability, value_heads, precision=lax.Precision.HIGHEST)
    return round_both(attended.reshape(item_count, query_len, row_width))

def forward(tok_in, param_set, word_mask, region_group):
    cross_qkv, cross_q_bias, cross_v_bias, cross_out, cross_out_bias, cross_gain, cross_shift, self_qkv, self_q_bias, self_v_bias, self_out, self_out_bias, self_gain, self_shift, ffn_in, ffn_in_bias, ffn_out, ffn_out_bias, ffn_gain, ffn_shift = param_set
    mask_pair = (word_mask, region_group)
    projected = [project(tok_in[0], cross_qkv, cross_q_bias, cross_v_bias), project(tok_in[1], cross_qkv, cross_q_bias, cross_v_bias)]
    results = []
    for stream_idx in range(2):
        far_idx = 1 - stream_idx
        attended = attend(projected[stream_idx][0], projected[far_idx][1], projected[far_idx][2], mask_pair[far_idx])
        branch = low_back(matmul(attended, cross_out) + cross_out_bias)
        joined = layer_norm(tok_in[stream_idx] + branch, cross_gain, cross_shift)
        query_rows, key_rows, value_rows = project(joined, self_qkv[stream_idx], self_q_bias[stream_idx], self_v_bias[stream_idx])
        attended = attend(query_rows, key_rows, value_rows, mask_pair[stream_idx])
        branch = low_back(matmul(attended, self_out[stream_idx]) + self_out_bias[stream_idx])
        settled = layer_norm(joined + branch, self_gain[stream_idx], self_shift[stream_idx])
        ffn_inner = low_back(matmul(low(settled), ffn_in[stream_idx]) + ffn_in_bias[stream_idx])
        active = low(jax.nn.gelu(ffn_inner, approximate=False))
        branch = low_back(matmul(active, ffn_out[stream_idx]) + ffn_out_bias[stream_idx])
        normed = layer_norm(settled + branch, ffn_gain[stream_idx], ffn_shift[stream_idx])
        results.append(normed * mask_pair[stream_idx][..., None].astype(normed.dtype))
    return jnp.stack(results)

def reference(tokens, region_mask, cotangent, cross_qkv, cross_q_bias, cross_v_bias, cross_out, cross_out_bias, cross_gain, cross_shift, self_qkv, self_q_bias, self_v_bias, self_out, self_out_bias, self_gain, self_shift, ffn_in, ffn_in_bias, ffn_out, ffn_out_bias, ffn_gain, ffn_shift):
    param_set = tuple((weight.astype(jnp.float32) for weight in (cross_qkv, cross_q_bias, cross_v_bias, cross_out, cross_out_bias, cross_gain, cross_shift, self_qkv, self_q_bias, self_v_bias, self_out, self_out_bias, self_gain, self_shift, ffn_in, ffn_in_bias, ffn_out, ffn_out_bias, ffn_gain, ffn_shift)))
    group_size = 64 if ITEMS % 64 == 0 else ITEMS
    groups = ITEMS // group_size
    tok_groups = tokens.astype(jnp.float32).reshape(2, groups, group_size, LR, D).transpose(1, 0, 2, 3, 4)
    cot_groups = cotangent.astype(jnp.float32).reshape(2, groups, group_size, LR, D).transpose(1, 0, 2, 3, 4)
    mask_groups = region_mask.reshape(groups, group_size, LR)
    word_row = (jnp.arange(LR) < LW).astype(jnp.int32)

    def group_step(grad_sums, group_slab):
        tok_group, cot_group, region_group = group_slab
        word_mask = jnp.broadcast_to(word_row, region_group.shape)

        def forward_run(tok_in, params_in):
            return forward(tok_in, params_in, word_mask, region_group)
        result, pullback = jax.vjp(forward_run, tok_group, param_set)
        grad_tok, grad_params = pullback(cot_group)
        grad_sums = jax.tree.map(jnp.add, grad_sums, grad_params)
        return (grad_sums, (result.astype(jnp.bfloat16), grad_tok))
    zero_grads = jax.tree.map(jnp.zeros_like, param_set)
    grad_sums, (out_groups, grad_groups) = lax.scan(group_step, zero_grads, (tok_groups, cot_groups, mask_groups))
    stream_out = out_groups.transpose(1, 0, 2, 3, 4).reshape(2, ITEMS, LR, D)
    tokens_grad = grad_groups.transpose(1, 0, 2, 3, 4).reshape(2, ITEMS, LR, D)
    g_cqkv, g_cqb, g_cvb, g_cout, g_coutb, g_cgain, g_cshift, g_sqkv, g_sqb, g_svb, g_sout, g_soutb, g_sgain, g_sshift, g_fin, g_finb, g_fout, g_foutb, g_fgain, g_fshift = grad_sums
    return (stream_out, tokens_grad, g_cqkv, g_cqb, g_cvb, g_cout, g_coutb, g_cgain, g_cshift, g_sqkv, g_sqb, g_svb, g_sout, g_soutb, g_sgain, g_sshift, g_fin, g_finb, g_fout, g_foutb, g_fgain, g_fshift)
```

```python
from functools import partial

import jax
import jax.numpy as jnp
from jax import lax
from jax.experimental import pallas as pl
from jax.experimental.pallas import tpu as pltpu
from jax.sharding import PartitionSpec as P

D = 768
H = 12
HD = 64
FF = 3072
LW = 20
LR = 36
BF = jnp.bfloat16
F32 = jnp.float32
GROUP = 4
GR = GROUP * LR
TILE = 256
BLK = 48
FGAIN, FSHIFT, FOUTB, SGAIN, SSHIFT, SOUTB, SQB, SVB, FINB = 0, 1, 2, 3, 4, 5, 6, 7, 8
CGAIN, CSHIFT, COUTB, CQB, CVB = 12, 13, 14, 15, 16
NV = 24


def nn(a, b):
    return lax.dot_general(a, b, (((1,), (0,)), ((), ())), preferred_element_type=F32)


def nt(a, b):
    return lax.dot_general(a, b, (((1,), (1,)), ((), ())), preferred_element_type=F32)


def tn(a, b):
    return lax.dot_general(a, b, (((0,), (0,)), ((), ())), preferred_element_type=F32)


def tile_at(i, size=TILE):
    return pl.ds(pl.multiple_of(i * size, size), size)


def total(x):
    return jnp.sum(x.astype(F32), axis=0, keepdims=True)


def norm_forward(res, gain, shift, hat, rstd, y_low):
    rows = res.shape[0]

    @pl.loop(0, rows // BLK)
    def _(i):
        at = tile_at(i, BLK)
        r = res[at, :]
        centre = r - jnp.mean(r, axis=-1, keepdims=True)
        rs = lax.rsqrt(jnp.mean(centre * centre, axis=-1, keepdims=True) + 1e-12)
        xh = centre * rs
        y = xh * gain[...] + shift[...]
        hat[at, :] = xh.astype(BF)
        rstd[at, :] = rs
        res[at, :] = y
        y_low[at, :] = y.astype(BF)


def norm_grad(dy, xh, rs, gain):
    dx = dy * gain
    return rs * (
        dx - jnp.mean(dx, axis=-1, keepdims=True) - xh * jnp.mean(dx * xh, axis=-1, keepdims=True)
    )


def norm_backward(res, gain, hat, rstd, g_low, vec, at_gain, at_shift, at_bias):
    rows = res.shape[0]

    @pl.loop(0, rows // BLK)
    def _(i):
        at = tile_at(i, BLK)
        dy = res[at, :]
        xh = hat[at, :].astype(F32)
        g = norm_grad(dy, xh, rstd[at, :], gain[...])
        low = g.astype(BF)
        res[at, :] = g
        g_low[at, :] = low
        vec[at_gain : at_gain + 1, :] += total(dy * xh)
        vec[at_shift : at_shift + 1, :] += total(dy)
        vec[at_bias : at_bias + 1, :] += total(low)


def head_masks():
    lane = lax.broadcasted_iota(jnp.int32, (1, 128), 1)
    first = (lane < HD).astype(BF)
    return first, (1 - first).astype(BF)


def stack_heads(x, masks):
    return jnp.concatenate([x * masks[0], x * masks[1]], axis=0)


def pick_heads(x):
    lane = lax.broadcasted_iota(jnp.int32, (GR, 128), 1)
    return jnp.where(lane < HD, x[:GR], x[GR:])


def probabilities(q2, k, rid, kid):
    s = nt(q2, k) * (1.0 / HD**0.5)
    s = jnp.where(rid == kid, s, -1000000000.0)
    e = jnp.exp(s - jnp.max(s, axis=-1, keepdims=True))
    return e * (1.0 / jnp.sum(e, axis=-1, keepdims=True))


def attention_forward(qr, qo, kr, ko, vr, vo, rid, kids, out):
    groups = out.shape[0] // GR

    @pl.loop(0, groups)
    def _(g):
        rows = pl.ds(pl.multiple_of(g * GR, GR), GR)
        kid = kids[g]
        masks = head_masks()

        for p in range(H // 2):
            def cols(o):
                return pl.ds(o + p * 128, 128)

            q2 = stack_heads(qr[rows, cols(qo)], masks)
            prob = probabilities(q2, kr[rows, cols(ko)], rid[...], kid)
            o = nn(prob.astype(BF), vr[rows, cols(vo)])
            out[rows, cols(0)] = pick_heads(o).astype(BF)


def attention_backward(qkv, grad_out, rid, kids):
    groups = grad_out.shape[0] // GR

    @pl.loop(0, groups)
    def _(g):
        rows = pl.ds(pl.multiple_of(g * GR, GR), GR)
        kid = kids[g]
        masks = head_masks()

        for p in range(H // 2):
            def cols(o):
                return pl.ds(o + p * 128, 128)

            q2 = stack_heads(qkv[rows, cols(0)], masks)
            k = qkv[rows, cols(D)]
            v = qkv[rows, cols(2 * D)]
            g2 = stack_heads(grad_out[rows, cols(0)], masks)
            prob = probabilities(q2, k, rid[...], kid)
            gp = nt(g2, v)
            gv = tn(prob.astype(BF), g2)
            s = prob * (gp - jnp.sum(gp * prob, axis=-1, keepdims=True))
            s = s.astype(BF)
            gq = pick_heads(nn(s, k)) * (1.0 / HD**0.5)
            gk = tn(s, q2) * (1.0 / HD**0.5)
            qkv[rows, cols(0)] = gq.astype(BF)
            qkv[rows, cols(D)] = gk.astype(BF)
            qkv[rows, cols(2 * D)] = gv.astype(BF)


SMALL = (
    "cross_q_bias", "cross_v_bias", "cross_out_bias", "cross_gain", "cross_shift",
    "self_q_bias", "self_v_bias", "self_out_bias", "self_gain", "self_shift",
    "ffn_in_bias", "ffn_out_bias", "ffn_gain", "ffn_shift",
)
NS = len(SMALL)
PARTS = (
    [(4 * BLK, TILE)] * 3 + [(BLK, 1024)] * 3 + [(BLK, D)] * 8
)


def body(*refs):
    tok_h, far_h, cot_h, cqkv_h, cout_h, sqkv_h, sout_h, fin_h, fout_h = refs[:9]
    kid_own, kid_far, row_ok = refs[9:12]
    sm = dict(zip(SMALL, refs[12 : 12 + NS]))
    refs = refs[12 + NS :]
    out_o, grad_o, back_o, vec = refs[:4]
    parts_o = refs[4 : 4 + len(PARTS)]
    refs = refs[4 + len(PARTS) :]
    (tok, far, cot, wp, wq, xqkv, xatt, joined, hat1, sqkv, satt, settled, hat2, active, inner,
     res, g_low, g_att, rid, rstd1, rstd2, slot_a, slot_b, sems, part_sems) = refs
    rows = tok.shape[0]

    def fetch(i, src, dst):
        c = pltpu.make_async_copy(src, dst, sems.at[i])
        c.start()
        return c

    c_tok = fetch(0, tok_h, tok)
    c_cqkv = fetch(1, cqkv_h, wp.at[:, 0 : 3 * D])
    c_far = fetch(2, far_h, far)
    c_cout = fetch(3, cout_h, wp.at[:, 3 * D :])
    c_sqkv = [fetch(4 + j, sqkv_h.at[:, j * D : (j + 1) * D], wq.at[j * D : (j + 1) * D, :]) for j in range(3)]
    c_sout = fetch(7, sout_h, wq.at[3 * D :, :])
    c_cot = fetch(8, cot_h, cot)

    vec[...] = jnp.zeros_like(vec)
    row_item = lax.broadcasted_iota(jnp.int32, (2 * GR, GR), 0)
    item = jnp.zeros((2 * GR, GR), F32)
    for edge in range(1, 2 * GROUP):
        if edge == GROUP:
            continue
        item += (row_item >= edge * LR).astype(F32)
    item -= jnp.where(row_item >= GR, float(GROUP - 1), 0.0)
    rid[...] = item

    c_tok.wait()
    c_cqkv.wait()

    @pl.loop(0, 3)
    def _(j):
        at = tile_at(j)
        xqkv[:, at] = (nn(tok[...], wp[:, at]) + sm["cross_q_bias"][:, at]).astype(BF)

    c_far.wait()

    @pl.loop(3, 6)
    def _(j):
        at = tile_at(j)
        xqkv[:, at] = nn(far[...], wp[:, at]).astype(BF)

    @pl.loop(6, 9)
    def _(j):
        at = tile_at(j)
        xqkv[:, at] = (nn(far[...], wp[:, at]) + sm["cross_v_bias"][:, tile_at(j - 6)]).astype(BF)

    attention_forward(xqkv, 0, xqkv, D, xqkv, 2 * D, rid, kid_far, xatt)
    c_cout.wait()

    @pl.loop(0, 3)
    def _(j):
        at = tile_at(j)
        w_at = pl.ds(pl.multiple_of(3 * D + j * TILE, TILE), TILE)
        res[:, at] = tok[:, at].astype(F32) + nn(xatt[...], wp[:, w_at]) + sm["cross_out_bias"][:, at]

    c_fin = fetch(1, fin_h, wp)
    norm_forward(res, sm["cross_gain"], sm["cross_shift"], hat1, rstd1, joined)

    for c in c_sqkv:
        c.wait()
    for part in range(3):
        @pl.loop(0, 3)
        def _(j):
            at = tile_at(j)
            x = nn(joined[...], wq[part * D : (part + 1) * D, at])
            if part == 0:
                x = x + sm["self_q_bias"][:, at]
            if part == 2:
                x = x + sm["self_v_bias"][:, at]
            sqkv[:, pl.ds(pl.multiple_of(part * D + j * TILE, TILE), TILE)] = x.astype(BF)

    attention_forward(sqkv, 0, sqkv, D, sqkv, 2 * D, rid, kid_own, satt)
    c_sout.wait()

    @pl.loop(0, 3)
    def _(j):
        at = tile_at(j)
        res[:, at] += nn(satt[...], wq[3 * D :, at]) + sm["self_out_bias"][:, at]

    c_fout = fetch(3, fout_h, wq)
    norm_forward(res, sm["self_gain"], sm["self_shift"], hat2, rstd2, settled)

    c_fin.wait()

    @pl.loop(0, FF // TILE)
    def _(j):
        at = tile_at(j)
        x = nn(settled[...], wp[:, at]) + sm["ffn_in_bias"][:, at]
        half = 0.5 * (1.0 + lax.erf(x * (0.5**0.5)))
        active[:, at] = (x * half).astype(BF)
        inner[:, at] = (half + x * jnp.exp(-0.5 * x * x) * 0.3989422804014327).astype(BF)

    c_fout.wait()

    @pl.loop(0, 3)
    def _(j):
        at = tile_at(j)
        res[:, at] += nn(active[...], wq[:, at]) + sm["ffn_out_bias"][:, at]

    c_cot.wait()

    @pl.loop(0, rows // BLK)
    def _(i):
        at = tile_at(i, BLK)
        r = res[at, :]
        ok = row_ok[at, :]
        gain = sm["ffn_gain"][...]
        centre = r - jnp.mean(r, axis=-1, keepdims=True)
        rs = lax.rsqrt(jnp.mean(centre * centre, axis=-1, keepdims=True) + 1e-12)
        xh = centre * rs
        y = xh * gain + sm["ffn_shift"][...]
        g_low[at, :] = (y * ok).astype(BF)
        dy = cot[at, :].astype(F32) * ok
        g = norm_grad(dy, xh, rs, gain)
        low = g.astype(BF)
        res[at, :] = g
        cot[at, :] = low
        vec[FGAIN : FGAIN + 1, :] += total(dy * xh)
        vec[FSHIFT : FSHIFT + 1, :] += total(dy)
        vec[FOUTB : FOUTB + 1, :] += total(low)

    c_out = fetch(8, g_low, out_o)

    used = {0: [], 1: []}

    def slot_for(i):
        kind = 1 if PARTS[i][0] != BLK else 0
        held = used[kind]
        if len(held) >= 2:
            held[-2].wait()
        place = len(held) % 2
        ref = (slot_b if kind else slot_a).at[place]
        if not kind and PARTS[i][1] != 1024:
            ref = ref.at[:, :, :, 0 : PARTS[i][1]]
        return kind, ref

    def push(i, kind, ref):
        c = pltpu.make_async_copy(ref, parts_o[i], part_sems.at[i])
        c.start()
        used[kind].append(c)

    def weight_part(i, left, right, col0, bias=None):
        kind, ref = slot_for(i)
        width = PARTS[i][1]

        @pl.loop(0, width // TILE)
        def _(j):
            src = right[:, pl.ds(pl.multiple_of(col0 + j * TILE, TILE), TILE)]
            w = tn(left[...], src).astype(BF)
            for d in range(16):
                ref[d % 2, d // 2, :, tile_at(j)] = w[d * BLK : (d + 1) * BLK, :]
            if bias is not None:
                vec[bias : bias + 1, tile_at(j)] += total(src)

        push(i, kind, ref)

    for col in range(3):
        kind, ref = slot_for(col)

        @pl.loop(0, 4)
        def _(t):
            w = tn(active[:, tile_at(t, D)], cot[:, col * TILE : (col + 1) * TILE]).astype(BF)
            for d in range(4):
                ref[d % 2, t * 2 + d // 2, :, :] = w[d * 4 * BLK : (d + 1) * 4 * BLK, :]

        push(col, kind, ref)

    @pl.loop(0, FF // TILE)
    def _(j):
        at = tile_at(j)
        ga = nt(cot[...], wq[at, :])
        gi = (ga * inner[:, at].astype(F32)).astype(BF)
        inner[:, at] = gi

    for r in range(4):
        vec[FINB + r : FINB + r + 1, :] = total(inner[:, r * D : (r + 1) * D])

    c_sqkv = [fetch(4 + j, sqkv_h.at[:, j * D : (j + 1) * D], wq.at[j * D : (j + 1) * D, :]) for j in range(3)]
    c_sout = fetch(7, sout_h, wq.at[3 * D :, :])

    for col in range(3):
        weight_part(3 + col, settled, inner, col * 1024)

    @pl.loop(0, 3)
    def _(j):
        at = tile_at(j)
        res[:, at] += nt(inner[...], wp[at, :])

    c_cqkv = fetch(1, cqkv_h, wp.at[:, 0 : 3 * D])
    c_cout = fetch(3, cout_h, wp.at[:, 3 * D :])
    c_out.wait()
    norm_backward(res, sm["self_gain"], hat2, rstd2, g_low, vec, SGAIN, SSHIFT, SOUTB)
    weight_part(6, satt, g_low, 0)
    for c in c_sqkv:
        c.wait()
    c_sout.wait()

    @pl.loop(0, 3)
    def _(j):
        at = tile_at(j)
        w_at = pl.ds(pl.multiple_of(3 * D + j * TILE, TILE), TILE)
        g_att[:, at] = nt(g_low[...], wq[w_at, :]).astype(BF)

    attention_backward(sqkv, g_att, rid, kid_own)
    for part in range(3):
        weight_part(7 + part, joined, sqkv, part * D, (SQB, None, SVB)[part])

    @pl.loop(0, 3)
    def _(j):
        at = tile_at(j)
        g = res[:, at]
        for part in range(3):
            w_at = pl.ds(pl.multiple_of(part * D + j * TILE, TILE), TILE)
            g += nt(sqkv[:, part * D : (part + 1) * D], wq[w_at, :])
        res[:, at] = g

    norm_backward(res, sm["cross_gain"], hat1, rstd1, g_low, vec, CGAIN, CSHIFT, COUTB)
    weight_part(10, xatt, g_low, 0)
    c_cqkv.wait()
    c_cout.wait()

    @pl.loop(0, 3)
    def _(j):
        at = tile_at(j)
        g_att[:, at] = nt(g_low[...], wp[at, 3 * D :]).astype(BF)

    attention_backward(xqkv, g_att, rid, kid_far)

    @pl.loop(0, 3)
    def _(j):
        at = tile_at(j)
        g_att[:, at] = nt(xqkv[:, D:], wp[at, D : 3 * D]).astype(BF)
        res[:, at] += nt(xqkv[:, 0:D], wp[at, 0:D])

    c_back = fetch(8, g_att, back_o)
    c_grad = fetch(0, res, grad_o)
    weight_part(11, tok, xqkv, 0, CQB)
    weight_part(12, far, xqkv, D)
    weight_part(13, far, xqkv, 2 * D, CVB)
    for held in used.values():
        for c in held[-2:]:
            c.wait()
    c_back.wait()
    c_grad.wait()


def compute(rows, arrays):
    any_space = pl.BlockSpec(memory_space=pl.ANY)
    vmem = pl.BlockSpec(memory_space=pltpu.VMEM)
    part_shapes = [jax.ShapeDtypeStruct((2, 8, r, n), BF) for r, n in PARTS]
    low = lambda n=D: pltpu.VMEM((rows, n), BF)
    return pl.pallas_call(
        body,
        out_shape=[
            jax.ShapeDtypeStruct((rows, D), BF),
            jax.ShapeDtypeStruct((rows, D), F32),
            jax.ShapeDtypeStruct((rows, D), BF),
            jax.ShapeDtypeStruct((NV, D), F32),
            *part_shapes,
        ],
        in_specs=[any_space] * 9 + [vmem] * (3 + NS),
        out_specs=[any_space] * 3 + [vmem] + [any_space] * len(PARTS),
        scratch_shapes=[
            low(), low(), low(),
            pltpu.VMEM((D, FF), BF), pltpu.VMEM((FF, D), BF),
            low(3 * D), low(), low(), low(),
            low(3 * D), low(), low(), low(),
            low(FF), low(FF),
            pltpu.VMEM((rows, D), F32), low(), low(),
            pltpu.VMEM((2 * GR, GR), F32),
            pltpu.VMEM((rows, 1), F32), pltpu.VMEM((rows, 1), F32),
            pltpu.VMEM((2, 2, 8, BLK, 1024), BF), pltpu.VMEM((2, 2, 8, 4 * BLK, TILE), BF),
            pltpu.SemaphoreType.DMA((9,)), pltpu.SemaphoreType.DMA((len(PARTS),)),
        ],
        compiler_params=pltpu.CompilerParams(vmem_limit_bytes=62 * 2**20),
    )(*arrays)


NAMES = (
    "tokens", "region_mask", "cotangent", "cross_qkv", "cross_q_bias", "cross_v_bias",
    "cross_out", "cross_out_bias", "cross_gain", "cross_shift", "self_qkv", "self_q_bias",
    "self_v_bias", "self_out", "self_out_bias", "self_gain", "self_shift", "ffn_in",
    "ffn_in_bias", "ffn_out", "ffn_out_bias", "ffn_gain", "ffn_shift",
)


def partner(block):
    return lax.ppermute(block, "stream", [(0, 1), (1, 0)])


def local(*args):
    a = dict(zip(NAMES, args))
    side = lax.axis_index("stream")
    tokens = a["tokens"]
    tok = tokens[0].reshape(-1, D)
    cot = a["cotangent"][0].reshape(-1, D)
    rows = tok.shape[0]
    far = partner(tok)
    mask = a["region_mask"]
    word = jnp.broadcast_to((jnp.arange(LR) < LW).astype(jnp.int32), mask.shape)
    own = jnp.where(side == 0, word, mask)
    other = jnp.where(side == 0, mask, word)
    place = (jnp.arange(rows) // LR) % GROUP

    def key_ids(m):
        return jnp.where(m.reshape(-1) > 0, place, -1).astype(F32).reshape(rows // GR, 1, GR)

    row_ok = own.reshape(-1, 1).astype(F32)
    small = [a[n].reshape(1, -1) for n in SMALL]
    outs = compute(
        rows,
        [tok, far, cot, a["cross_qkv"], a["cross_out"], a["self_qkv"][0], a["self_out"][0],
         a["ffn_in"][0], a["ffn_out"][0], key_ids(own), key_ids(other), row_ok, *small],
    )
    stream_out, grad_tok, back, vec = outs[:4]
    parts = outs[4:]
    tokens_grad = (grad_tok + partner(back).astype(F32)).reshape(tokens.shape)

    def natural(some):
        done = []
        for p in some:
            r, n = p.shape[2:]
            done.append(p.transpose(1, 0, 2, 3).reshape(16 * r, n))
        return jnp.concatenate(done, axis=1)

    def scatter(x, axes=("dp",)):
        if len(axes) > 1:
            x = lax.psum(x, "stream")
        return lax.psum_scatter(x, "dp", scatter_dimension=0, tiled=True).astype(F32)

    fout = scatter(natural(parts[0:3]))
    fin = scatter(natural(parts[3:6]))
    sout = scatter(natural(parts[6:7]))
    sqkv = scatter(natural(parts[7:10]))
    cout = scatter(natural(parts[10:11]), ("stream", "dp"))
    cqkv = scatter(natural(parts[11:14]), ("stream", "dp"))
    own_vec = lax.psum(vec[:12], "dp")
    cross_vec = lax.psum(vec[12:], ("stream", "dp"))
    n = lax.axis_size("dp")
    me = lax.axis_index("dp")

    def mine(v, r):
        return lax.dynamic_slice_in_dim(v[r], me * (D // n), D // n)

    def own_v(r):
        return mine(own_vec, r)[None]

    def cross_v(r):
        return mine(cross_vec, r - 12)

    finb = lax.dynamic_slice_in_dim(own_vec[FINB : FINB + 4].reshape(-1), me * (FF // n), FF // n)[None]
    return (
        stream_out.reshape(tokens.shape), tokens_grad,
        cqkv, cross_v(CQB), cross_v(CVB), cout, cross_v(COUTB), cross_v(CGAIN), cross_v(CSHIFT),
        sqkv[None], own_v(SQB), own_v(SVB), sout[None], own_v(SOUTB), own_v(SGAIN), own_v(SSHIFT),
        fin[None], finb, fout[None], own_v(FOUTB), own_v(FGAIN), own_v(FSHIFT),
    )


def solution(mesh):
    both = P("stream", "dp")
    one = P("stream")
    specs = {n: one for n in NAMES}
    specs.update({n: P() for n in NAMES if n.startswith("cross")})
    specs.update(tokens=both, cotangent=both, region_mask=P("dp"))
    return jax.shard_map(
        local,
        mesh=mesh,
        in_specs=tuple(specs[n] for n in NAMES),
        out_specs=(both, both) + (P("dp"),) * 7 + (both,) * 13,
        check_vma=False,
    )
```

```python
from functools import partial
from types import SimpleNamespace

import jax
import jax.numpy as jnp
from jax import lax
from jax.experimental import pallas as pl
from jax.experimental.pallas import tpu as pltpu
from jax.sharding import PartitionSpec as P

D = 768
H = 12
HD = 64
FF = 3072
LW = 20
LR = 36
BF = jnp.bfloat16
F32 = jnp.float32
GROUP = 4
GR = GROUP * LR
PAIR = 2 * LR
PAD = 80
TILE = 256
BLK = 48
FGAIN, FSHIFT, FOUTB, SGAIN, SSHIFT, SOUTB, SQB, SVB, FINB = 0, 1, 2, 3, 4, 5, 6, 7, 8
CGAIN, CSHIFT, COUTB, CQB, CVB = 12, 13, 14, 15, 16
NV = 24


def nn(a, b):
    return lax.dot_general(a, b, (((1,), (0,)), ((), ())), preferred_element_type=F32)


def nt(a, b):
    return lax.dot_general(a, b, (((1,), (1,)), ((), ())), preferred_element_type=F32)


def tn(a, b):
    return lax.dot_general(a, b, (((0,), (0,)), ((), ())), preferred_element_type=F32)


def tile_at(i, size=TILE):
    return pl.ds(pl.multiple_of(i * size, size), size)


def total(x):
    return jnp.sum(x.astype(F32), axis=0, keepdims=True)


def norm_forward(res, gain, shift, hat, columns, col, y_low):
    rows = res.shape[0]

    @pl.loop(0, rows // BLK)
    def _(i):
        at = tile_at(i, BLK)
        r = res[at, :]
        centre = r - jnp.mean(r, axis=-1, keepdims=True)
        rs = lax.rsqrt(jnp.mean(centre * centre, axis=-1, keepdims=True) + 1e-12)
        xh = centre * rs
        y = xh * gain[...] + shift[...]
        hat[at, :] = xh.astype(BF)
        columns[at, col : col + 1] = rs
        res[at, :] = y
        y_low[at, :] = y.astype(BF)


def norm_grad(dy, xh, rs, gain):
    dx = dy * gain
    return rs * (
        dx - jnp.mean(dx, axis=-1, keepdims=True) - xh * jnp.mean(dx * xh, axis=-1, keepdims=True)
    )


def norm_backward(res, gain, hat, columns, col, g_low, vec, at_gain, at_shift, at_bias):
    rows = res.shape[0]

    @pl.loop(0, rows // BLK)
    def _(i):
        at = tile_at(i, BLK)
        dy = res[at, :]
        xh = hat[at, :].astype(F32)
        g = norm_grad(dy, xh, columns[at, col : col + 1], gain[...])
        low = g.astype(BF)
        res[at, :] = g
        g_low[at, :] = low
        vec[at_gain : at_gain + 1, :] += total(dy * xh)
        vec[at_shift : at_shift + 1, :] += total(dy)
        vec[at_bias : at_bias + 1, :] += total(low)


def head_masks():
    lane = lax.broadcasted_iota(jnp.int32, (1, 128), 1)
    first = (lane < HD).astype(BF)
    return first, (1 - first).astype(BF)


def stack_heads(x, masks):
    return jnp.concatenate([x * masks[0], x * masks[1]], axis=0)


def pick_heads(x):
    lane = lax.broadcasted_iota(jnp.int32, (PAIR, 128), 1)
    return jnp.where(lane < HD, x[:PAIR], x[PAD : PAD + PAIR])


def store_pairs(dst, x, at, first=0):
    zeros = jnp.zeros((PAD - PAIR, x.shape[1]), F32)
    for p in range(x.shape[0] // PAIR):
        block = jnp.concatenate([x[p * PAIR : (p + 1) * PAIR], zeros], axis=0)
        dst[pl.ds(pl.multiple_of((first + p) * PAD, 16), PAD), at] = block.astype(BF)


def probabilities(q2, k, rid, kid):
    s = nt(q2, k) * (1.0 / HD**0.5)
    s = jnp.where(rid == kid, s, -1000000000.0)
    e = jnp.exp(s - jnp.max(s, axis=-1, keepdims=True))
    return e * (1.0 / jnp.sum(e, axis=-1, keepdims=True))


def attention_forward(g, qkv, rid, kids, out):
    masks = head_masks()
    group = pl.ds(pl.multiple_of(g * GR, GR), GR)
    for p in range(H // 2):
        done = []
        for half in range(2):
            rows = pl.ds(pl.multiple_of((2 * g + half) * PAD, 16), PAD)
            q2 = stack_heads(qkv[rows, p * 128 : p * 128 + 128], masks)
            prob = probabilities(q2, qkv[rows, D + p * 128 : D + p * 128 + 128], rid[...], kids[2 * g + half])
            done.append(pick_heads(nn(prob.astype(BF), qkv[rows, 2 * D + p * 128 : 2 * D + p * 128 + 128])))
        out[group, p * 128 : p * 128 + 128] = jnp.concatenate(done, axis=0).astype(BF)


def attention_backward(g, qkv, grad_out, rid, kids, out):
    masks = head_masks()
    group = pl.ds(pl.multiple_of(g * GR, GR), GR)
    for p in range(H // 2):
        done = [[], [], []]
        for half in range(2):
            rows = pl.ds(pl.multiple_of((2 * g + half) * PAD, 16), PAD)
            q2 = stack_heads(qkv[rows, p * 128 : p * 128 + 128], masks)
            k = qkv[rows, D + p * 128 : D + p * 128 + 128]
            v = qkv[rows, 2 * D + p * 128 : 2 * D + p * 128 + 128]
            g2 = stack_heads(grad_out[rows, p * 128 : p * 128 + 128], masks)
            prob = probabilities(q2, k, rid[...], kids[2 * g + half])
            gp = nt(g2, v)
            gv = tn(prob.astype(BF), g2)
            s = prob * (gp - jnp.sum(gp * prob, axis=-1, keepdims=True))
            s = s.astype(BF)
            done[0].append(pick_heads(nn(s, k)) * (1.0 / HD**0.5))
            done[1].append(tn(s, q2)[:PAIR] * (1.0 / HD**0.5))
            done[2].append(gv[:PAIR])
        for part in range(3):
            at = part * D + p * 128
            out[group, at : at + 128] = jnp.concatenate(done[part], axis=0).astype(BF)


def by_item(wide, dst, g):
    items = wide.shape[1] // LR
    for j in range(D // 128):
        got = [wide[j, pl.ds(g * GROUP + i, LR, stride=items), :] for i in range(GROUP)]
        dst[g * GR : (g + 1) * GR, j * 128 : (j + 1) * 128] = jnp.concatenate(got, axis=0).astype(BF)


def widen(src, wide):
    @pl.loop(0, src.shape[0] // BLK)
    def _(i):
        at = tile_at(i, BLK)
        for j in range(D // 128):
            wide[j, at, :] = src[at, j * 128 : (j + 1) * 128].astype(F32)


NAMES = (
    "tokens", "region_mask", "cotangent", "cross_qkv", "cross_q_bias", "cross_v_bias",
    "cross_out", "cross_out_bias", "cross_gain", "cross_shift", "self_qkv", "self_q_bias",
    "self_v_bias", "self_out", "self_out_bias", "self_gain", "self_shift", "ffn_in",
    "ffn_in_bias", "ffn_out", "ffn_out_bias", "ffn_gain", "ffn_shift",
)
SMALL = tuple(n for n in NAMES if n.endswith(("bias", "gain", "shift")))
NS = len(SMALL)
KINDS = ((4 * BLK, TILE), (BLK, 1024), (BLK, D))
PARTS = (
    *((0, TILE * i, 0) for i in range(3)),
    *((1, 1024 * i, 1) for i in range(3)),
    (2, 0, 2),
    *((3, D * i, 2) for i in range(3)),
    (4, 0, 2),
    *((5, D * i, 2) for i in range(3)),
)
NP = len(PARTS)
FIRST_CROSS = 10
OUTS = ((4 * BLK, D), (BLK, FF), (BLK, D), (BLK, 3 * D), (BLK, D), (BLK, 3 * D))
HALF = D // 2
BY_Y = (10, 12)
IN_KIND = [sum(p[2] == PARTS[i][2] for p in PARTS[:i]) for i in range(NP)]
COUNT = [sum(p[2] == k for p in PARTS) for k in range(3)]


SERVE = {
    -3: (100,),
    20: (101,),
    21: (102,),
    4: (200,),
    -6: (103,),
    30: (104, 201, 105, 300,),
    40: (202, 301, 106,),
    41: (400,),
    43: (203, 302,),
    7: (401,),
    -10: (107,),
    9: (204,),
    33: (108, 303, 109, 402,),
    10: (304, 205,),
    35: (403,),
    50: (110, 206, 404,),
    51: (305,),
    52: (207, 306,),
    53: (405,),
    11: (208,),
    12: (307, 510,),
    -14: (111,),
    13: (406,),
    36: (112, 209,),
    60: (308, 113, 210, 407, 309,),
    61: (211, 408, 310, 409, 311, 512,),
    62: (213, 410, 411, 610, 212, 313,),
    63: (312, 611, 413, 412, 613, 612,),
}


def body(fused, *refs):
    refs = list(refs)

    def take(n):
        got = refs[:n]
        del refs[:n]
        return got

    tok_h, far_h, cot_h, cqkv_h, cout_h, sqkv_h, sout_h, fin_h, fout_h = take(9)
    (mask_in,) = take(1)
    given = dict(zip(SMALL, take(NS)))
    out_o, grad_o, back_o, vec_o = take(4)
    parts_o = take(len(OUTS) if fused else NP)
    (tok, far, cot, wp, wq, xqkv, xatt, joined, hat1, sqkv, satt, settled, hat2, active, inner,
     res, g_low, gpad, rid, columns, slot_a, slot_b, kid_own, kid_far, sv,
     out_f, sems, part_sems) = take(28)
    rows = tok.shape[0]
    groups = rows // GR
    gx = active
    side = lax.axis_index("stream")

    def fetch(i, src, dst):
        c = pltpu.make_async_copy(src, dst, sems.at[i])
        c.start()
        return c

    if fused:
        acc, xr, za, zb, fin = take(3), take(3), take(3), take(3), take(3)
        yr, back, vbuf, ybf = take(4)
        s_core, r_core, s_x, r_x, s_za, r_za, s_zb, r_zb, s_y, r_y, s_yf, r_yf, s_m, r_m = take(14)
        me = lax.axis_index("dp")
        core, x = lax.rem(me, 2), lax.rem(lax.div(me, 2), 2)
        zl, zh = lax.rem(lax.div(me, 4), 2), lax.div(me, 8)
        to_y, to_core = (1 - side, me), (side, me + 1 - 2 * core)
        to_x, to_zl, to_zh = (side, me + 2 - 4 * x), (side, me + 4 - 8 * zl), (side, me + 8 - 16 * zh)
        peers = (to_y, to_core, to_x, to_zl, to_zh)
        def remote(src, dst, send, recv, peer):
            return pltpu.make_async_remote_copy(
                src_ref=src, dst_ref=dst, send_sem=send, recv_sem=recv,
                device_id=peer, device_id_type=pl.DeviceIdType.MESH,
            )

    c_tok = fetch(0, tok_h, g_low)
    c_cqkv = fetch(1, cqkv_h, wp.at[:, 0 : 3 * D])
    c_cot = fetch(8, cot_h, settled)
    c_cout = fetch(3, cout_h, wp.at[:, 3 * D :])
    if not fused:
        c_far = fetch(2, far_h, satt)

    def fetch_self():
        return [
            *(fetch(4 + j, sqkv_h.at[:, j * D : (j + 1) * D], wq.at[j * D : (j + 1) * D, :]) for j in range(3)),
            fetch(7, sout_h, wq.at[3 * D :, :]),
        ]

    c_self = fetch_self()
    c_tok.wait()
    widen(g_low, out_f)
    if fused:
        barrier = pltpu.get_barrier_semaphore()
        for p in peers:
            pl.semaphore_signal(barrier, inc=1, device_id=p, device_id_type=pl.DeviceIdType.MESH)
        pl.semaphore_wait(barrier, len(peers))

        def tokens_to(g):
            at = pl.ds(pl.multiple_of(g * GR, GR), GR)
            return remote(tok.at[at, :], far.at[at, :], s_m.at[g], r_m.at[g], to_y)

    for g in range(groups):
        by_item(out_f, tok, g)
        if fused:
            tokens_to(g).start()

    sm = SimpleNamespace()
    for i, n in enumerate(SMALL):
        row_of = given[n]
        if len(given[n].shape) == 1:
            sv[i : i + 1, :] = given[n][...].reshape(1, D)
            row_of = sv.at[i : i + 1, :]
        setattr(sm, n, row_of)
    vec = vbuf.at[0] if fused else vec_o
    vec[...] = jnp.zeros(vec.shape, F32)
    edge = lax.broadcasted_iota(jnp.int32, (2 * PAD, PAD), 0)
    second = ((edge >= LR) & (edge < PAD)) | (edge >= PAD + LR)
    rid[...] = second.astype(F32)
    items = rows // LR
    present = (mask_in[...] > 0).astype(F32)
    word = (lax.broadcasted_iota(jnp.int32, (items, LR), 1) < LW).astype(F32)
    slot = lax.broadcasted_iota(jnp.int32, (LR, GR), 0)
    lane = lax.broadcasted_iota(jnp.int32, (1, GR), 1)
    lane_item = sum((lane >= LR * i).astype(jnp.int32) for i in range(1, GROUP))
    spread_slots = (slot == lane - LR * lane_item).astype(BF)
    row = lax.broadcasted_iota(jnp.int32, (GR, GR), 0)
    diagonal = row == lax.broadcasted_iota(jnp.int32, (GR, GR), 1)

    def lay_masks(mask, kid, own):
        spread = nn(mask.astype(BF), spread_slots)
        for g in range(groups):
            line = jnp.zeros((1, GR), F32)
            for i in range(GROUP):
                line += jnp.where(lane_item == i, spread[g * GROUP + i : g * GROUP + i + 1, :], 0.0)
            ids = jnp.where(line > 0.5, (lane_item % 2).astype(F32), -1.0)
            for half in range(2):
                kid[2 * g + half, :, 0:PAIR] = ids[:, half * PAIR : (half + 1) * PAIR]
                kid[2 * g + half, :, PAIR:] = jnp.full((1, PAD - PAIR), -1.0, F32)
            if own:
                column = jnp.sum(jnp.where(diagonal, line, 0.0), axis=-1, keepdims=True)
                columns[g * GR : (g + 1) * GR, 0:1] = column

    lay_masks(jnp.where(side == 0, word, present), kid_own, True)
    lay_masks(jnp.where(side == 0, present, word), kid_far, False)

    c_cqkv.wait()

    @pl.loop(0, 3)
    def _(j):
        at = tile_at(j)
        store_pairs(xqkv, nn(tok[...], wp[:, at]) + sm.cross_q_bias[:, at], at)

    c_cot.wait()
    widen(settled, out_f)
    for g in range(groups):
        by_item(out_f, cot, g)
    if not fused:
        c_far.wait()
        widen(satt, out_f)
        for g in range(groups):
            by_item(out_f, far, g)

    @pl.loop(0, groups)
    def _(g):
        at_g = pl.ds(pl.multiple_of(g * GR, GR), GR)
        if fused:
            tokens_to(g).wait_recv()
        x = far[at_g, :]
        for j in range(3, 9):
            y = nn(x, wp[:, j * TILE : (j + 1) * TILE])
            if j >= 6:
                y = y + sm.cross_v_bias[:, (j - 6) * TILE : (j - 5) * TILE]
            store_pairs(xqkv, y, slice(j * TILE, (j + 1) * TILE), 2 * g)
        attention_forward(g, xqkv, rid, kid_far, xatt)

    c_cout.wait()

    @pl.loop(0, 3)
    def _(j):
        at = tile_at(j)
        w_at = pl.ds(pl.multiple_of(3 * D + j * TILE, TILE), TILE)
        res[:, at] = tok[:, at].astype(F32) + nn(xatt[...], wp[:, w_at]) + sm.cross_out_bias[:, at]

    c_fin = fetch(1, fin_h, wp)
    norm_forward(res, sm.cross_gain, sm.cross_shift, hat1, columns, 1, joined)

    for c in c_self:
        c.wait()
    for part in range(3):
        @pl.loop(0, 3)
        def _(j):
            at = tile_at(j)
            x = nn(joined[...], wq[part * D : (part + 1) * D, at])
            if part == 0:
                x = x + sm.self_q_bias[:, at]
            if part == 2:
                x = x + sm.self_v_bias[:, at]
            store_pairs(sqkv, x, pl.ds(pl.multiple_of(part * D + j * TILE, TILE), TILE))

    @pl.loop(0, groups)
    def _(g):
        attention_forward(g, sqkv, rid, kid_own, satt)

    @pl.loop(0, 3)
    def _(j):
        at = tile_at(j)
        res[:, at] += nn(satt[...], wq[3 * D :, at]) + sm.self_out_bias[:, at]

    c_fout = fetch(3, fout_h, wq)
    norm_forward(res, sm.self_gain, sm.self_shift, hat2, columns, 2, settled)

    c_fin.wait()

    @pl.loop(0, FF // TILE)
    def _(j):
        at = tile_at(j)
        x = nn(settled[...], wp[:, at]) + sm.ffn_in_bias[:, at]
        half = 0.5 * (1.0 + lax.erf(x * (0.5**0.5)))
        active[:, at] = (x * half).astype(BF)
        inner[:, at] = (half + x * jnp.exp(-0.5 * x * x) * 0.3989422804014327).astype(BF)

    c_fout.wait()

    @pl.loop(0, 3)
    def _(j):
        at = tile_at(j)
        res[:, at] += nn(active[...], wq[:, at]) + sm.ffn_out_bias[:, at]

    @pl.loop(0, rows // BLK)
    def _(i):
        at = tile_at(i, BLK)
        r = res[at, :]
        ok = columns[at, 0:1]
        gain = sm.ffn_gain[...]
        centre = r - jnp.mean(r, axis=-1, keepdims=True)
        rs = lax.rsqrt(jnp.mean(centre * centre, axis=-1, keepdims=True) + 1e-12)
        xh = centre * rs
        y = xh * gain + sm.ffn_shift[...]
        for j in range(D // 128):
            out_f[j, at, :] = y[:, j * 128 : (j + 1) * 128] * ok
        dy = cot[at, :].astype(F32) * ok
        g = norm_grad(dy, xh, rs, gain)
        low = g.astype(BF)
        res[at, :] = g
        cot[at, :] = low
        vec[FGAIN : FGAIN + 1, :] += total(dy * xh)
        vec[FSHIFT : FSHIFT + 1, :] += total(dy)
        vec[FOUTB : FOUTB + 1, :] += total(low)

    c_out = fetch(8, out_f, out_o)

    def slot_of(i):
        kind = PARTS[i][2]
        if kind == 0:
            return slot_b.at[i % 2]
        ref = slot_a.at[i % 2]
        return ref if kind == 1 else ref.at[:, :, :, :, :, 0:D]

    mv = SimpleNamespace(
        core={}, y={}, x={}, zl={}, zh={}, yf={}, out={}, acc={}, rx={}, rza={}, rzb={}, fin={}
    )
    out_going, far_going = [], []
    if fused:
        for i in range(NP):
            out, col, kind = PARTS[i]
            n = IN_KIND[i]
            a, width = acc[kind].at[n], KINDS[kind][1]
            mv.core[i] = remote(slot_of(i).at[1 - core], a, s_core.at[i], r_core.at[i], to_core)
            r_xi, r_zai, r_zbi = xr[kind].at[n], za[kind].at[n], zb[kind].at[n]
            if i in BY_Y:
                c = i - FIRST_CROSS
                mine = pl.ds(pl.multiple_of(side * HALF, HALF), HALF)
                other = pl.ds(pl.multiple_of((1 - side) * HALF, HALF), HALF)
                mv.y[i] = remote(a.at[:, :, :, :, other], yr.at[c], s_y.at[c], r_y.at[c], to_y)
                a = a.at[:, :, :, :, mine]
                cut = pl.ds(0, HALF)
                r_xi, r_zai, r_zbi = r_xi.at[:, :, :, cut], r_zai.at[:, :, cut], r_zbi.at[:, cut]
                width = HALF
            mv.acc[i], mv.rx[i], mv.rza[i], mv.rzb[i] = a, r_xi, r_zai, r_zbi
            mv.x[i] = remote(a.at[:, :, 1 - x], r_xi, s_x.at[i], r_x.at[i], to_x)
            mv.zl[i] = remote(a.at[:, 1 - zl, x], r_zai, s_za.at[i], r_za.at[i], to_zl)
            mv.zh[i] = remote(a.at[1 - zh, zl, x], r_zbi, s_zb.at[i], r_zb.at[i], to_zh)
            f = fin[kind].at[n % 2]
            if i in BY_Y:
                f = f.at[:, 0:HALF]
                col0 = pl.ds(pl.multiple_of(col + side * HALF, HALF), HALF)
            else:
                col0 = pl.ds(col, width)
            mv.fin[i] = f
            mv.out[i] = pltpu.make_async_copy(f, parts_o[out].at[:, col0], part_sems.at[i])
            if i in BY_Y:
                mv.yf[i] = remote(f, parts_o[out].at[:, col0], s_yf.at[c], r_yf.at[c], to_y)
            elif i >= FIRST_CROSS:
                c = i - FIRST_CROSS
                mv.yf[i] = remote(ybf.at[c // 2, 0], ybf.at[c // 2, 1], s_yf.at[c], r_yf.at[c], to_y)

        def t1(i):
            mv.core[i].wait_recv()
            out, col, kind = PARTS[i]
            a, own = acc[kind].at[IN_KIND[i]], slot_of(i)

            @pl.loop(0, 8)
            def _(d):
                p, q, r = lax.div(d, 4), lax.rem(lax.div(d, 2), 2), lax.rem(d, 2)
                a[p, q, r] = a[p, q, r] + own[core, p, q, r]

            (mv.y if i in BY_Y else mv.x)[i].start()

        def ty(i):
            mv.y[i].wait_recv()
            a, c = mv.acc[i], i - FIRST_CROSS

            @pl.loop(0, 8)
            def _(d):
                p, q, r = lax.div(d, 4), lax.rem(lax.div(d, 2), 2), lax.rem(d, 2)
                a[p, q, r] = a[p, q, r] + yr[c, p, q, r]

            mv.x[i].start()

        def t2(i):
            mv.x[i].wait_recv()
            a, r = mv.acc[i], mv.rx[i]

            @pl.loop(0, 4)
            def _(d):
                p, q = lax.div(d, 2), lax.rem(d, 2)
                a[p, q, x] = a[p, q, x] + r[p, q]

            mv.zl[i].start()

        def t3(i):
            mv.zl[i].wait_recv()
            a, r = mv.acc[i], mv.rza[i]
            for p in range(2):
                a[p, zl, x] = a[p, zl, x] + r[p]
            mv.zh[i].start()

        def room(i):
            before = [j for j in range(i) if PARTS[j][2] == PARTS[i][2] and IN_KIND[j] == IN_KIND[i] - 2]
            for j in before:
                mv.out[j].wait()
                out_going.remove(j)
                if j in BY_Y:
                    mv.yf[j].wait_send()
                    far_going.remove(j)

        def t4(i):
            mv.zh[i].wait_recv()
            whole = mv.acc[i][zh, zl, x].astype(F32) + mv.rzb[i][...].astype(F32)
            if i >= FIRST_CROSS and i not in BY_Y:
                ybf[(i - FIRST_CROSS) // 2, 0] = whole.astype(BF)
                mv.yf[i].start()
                far_going.append(i)
                return
            room(i)
            mv.fin[i][...] = whole
            mv.out[i].start()
            out_going.append(i)
            if i in BY_Y:
                mv.yf[i].start()
                far_going.append(i)

        def tf(i):
            mv.yf[i].wait_recv()
            if i not in BY_Y:
                room(i)
                c = i - FIRST_CROSS
                mv.fin[i][...] = ybf[c // 2, 0].astype(F32) + ybf[c // 2, 1].astype(F32)
                mv.out[i].start()
                out_going.append(i)

        steps = (t1, t2, t3, t4, ty, tf)
    left = []
    for i in range(NP):
        left += [n * 100 + i for n in (1, 2, 3, 4) + (5,) * (i in BY_Y) + (6,) * (i >= FIRST_CROSS)]
    core_free = {}

    def serve(place):
        if fused:
            for t in SERVE.get(place, ()):
                left.remove(t)
                steps[t // 100 - 1](t % 100)

    def free_slot(i):
        if i in core_free:
            core_free.pop(i)()

    def push(i):
        if fused:
            mv.core[i].start()
            core_free[i] = mv.core[i].wait_send
        else:
            c = pltpu.make_async_copy(slot_of(i), parts_o[i], part_sems.at[i])
            c.start()
            core_free[i] = c.wait

    def same_slot(i):
        for j in range(i - 1, -1, -1):
            if (PARTS[j][2] == 0) == (PARTS[i][2] == 0) and j % 2 == i % 2:
                return j
        return None

    def weight_part(i, left, right, col0):
        serve(-1 - i)
        free_slot(same_slot(i))
        ref = slot_of(i)
        width = KINDS[PARTS[i][2]][1]

        @pl.loop(0, width // TILE)
        def _(j):
            src = right[:, pl.ds(pl.multiple_of(col0 + j * TILE, TILE), TILE)]
            w = tn(left[...], src).astype(BF)
            for d in range(16):
                ref[d % 2, d // 8, (d // 4) % 2, (d // 2) % 2, :, tile_at(j)] = w[d * BLK : (d + 1) * BLK, :]

        push(i)
        serve(i)

    for col in range(3):
        serve(-1 - col)
        free_slot(same_slot(col))
        ref = slot_of(col)

        @pl.loop(0, 4)
        def _(t):
            w = tn(active[:, tile_at(t, D)], cot[:, col * TILE : (col + 1) * TILE]).astype(BF)
            for d in range(4):
                ref[d % 2, lax.div(t, 2), lax.rem(t, 2), d // 2, :, :] = w[d * 4 * BLK : (d + 1) * 4 * BLK, :]

        push(col)
        serve(col)

    for r in range(3):
        @pl.loop(4 * r, 4 * r + 4)
        def _(j):
            at = tile_at(j)
            ga = nt(cot[...], wq[at, :])
            gi = (ga * inner[:, at].astype(F32)).astype(BF)
            inner[:, at] = gi

        serve(20 + r)
    for r in range(4):
        vec[FINB + r : FINB + r + 1, :] = total(inner[:, r * D : (r + 1) * D])
    c_self = fetch_self()

    for col in range(3):
        weight_part(3 + col, settled, inner, col * 1024)

    @pl.loop(0, 3)
    def _(j):
        at = tile_at(j)
        res[:, at] += nt(inner[...], wp[at, :])

    serve(30)
    c_cqkv = fetch(1, cqkv_h, wp.at[:, 0 : 3 * D])
    c_cout = fetch(3, cout_h, wp.at[:, 3 * D :])
    norm_backward(res, sm.self_gain, hat2, columns, 2, g_low, vec, SGAIN, SSHIFT, SOUTB)
    serve(31)
    weight_part(6, satt, g_low, 0)
    for c in c_self:
        c.wait()

    @pl.loop(0, 3)
    def _(j):
        at = tile_at(j)
        w_at = pl.ds(pl.multiple_of(3 * D + j * TILE, TILE), TILE)
        store_pairs(gpad, nt(g_low[...], wq[w_at, :]), at)

    serve(32)

    def serve_each(place, g):
        for k in range(groups):
            if fused and SERVE.get(place + k):
                @pl.when(g == k)
                def _():
                    serve(place + k)

    @pl.loop(0, groups)
    def _(g):
        attention_backward(g, sqkv, gpad, rid, kid_own, gx)
        serve_each(40, g)

    for part in range(3):
        weight_part(7 + part, joined, gx, part * D)
    vec[SQB : SQB + 1, :] = total(gx[:, 0:D])
    vec[SVB : SVB + 1, :] = total(gx[:, 2 * D : 3 * D])

    @pl.loop(0, 3)
    def _(j):
        at = tile_at(j)
        g = res[:, at]
        for part in range(3):
            w_at = pl.ds(pl.multiple_of(part * D + j * TILE, TILE), TILE)
            g += nt(gx[:, part * D : (part + 1) * D], wq[w_at, :])
        res[:, at] = g

    serve(33)
    norm_backward(res, sm.cross_gain, hat1, columns, 1, g_low, vec, CGAIN, CSHIFT, COUTB)
    serve(34)
    weight_part(10, xatt, g_low, 0)
    c_cqkv.wait()
    c_cout.wait()

    @pl.loop(0, 3)
    def _(j):
        at = tile_at(j)
        store_pairs(gpad, nt(g_low[...], wp[at, 3 * D :]), at)

    serve(35)
    if fused:

        def back_to(g):
            at = pl.ds(pl.multiple_of(g * GR, GR), GR)
            return remote(g_low.at[at, :], back.at[at, :], s_m.at[groups + g], r_m.at[groups + g], to_y)

    @pl.loop(0, groups)
    def _(g):
        attention_backward(g, xqkv, gpad, rid, kid_far, gx)
        at = pl.ds(pl.multiple_of(g * GR, GR), GR)
        pair = gx[at, D : 3 * D]
        for j in range(3):
            w_at = slice(j * TILE, (j + 1) * TILE)
            g_low[at, w_at] = nt(pair, wp[w_at, D : 3 * D]).astype(BF)
        if fused:
            back_to(g).start()
        serve_each(50, g)

    vec[CQB : CQB + 1, :] = total(gx[:, 0:D])
    vec[CVB : CVB + 1, :] = total(gx[:, 2 * D : 3 * D])
    if fused:
        v_at = [
            remote(vbuf.at[j], vbuf.at[4 + j], s_m.at[2 * groups + j], r_m.at[2 * groups + j], p)
            for j, p in enumerate((to_core, to_x, to_zl, to_zh))
        ]
        v_y = remote(vbuf.at[8], vbuf.at[9], s_m.at[2 * groups + 4], r_m.at[2 * groups + 4], to_y)

        def vec_step(j):
            v_at[j].wait_recv()
            if j < 3:
                vbuf[j + 1] = vbuf[j] + vbuf[4 + j]
                v_at[j + 1].start()
            else:
                vbuf[8] = vbuf[3] + vbuf[7]
                v_y.start()

        v_at[0].start()
    weight_part(11, tok, gx, 0)
    weight_part(12, far, gx, D)
    if fused:
        vec_step(0)
    weight_part(13, far, gx, 2 * D)

    @pl.loop(0, 3)
    def _(j):
        at = tile_at(j)
        res[:, at] += nt(gx[:, 0:D], wp[at, 0:D])

    if not fused:
        c_back = fetch(2, g_low, back_o)
        c_grad = fetch(0, res, grad_o)
        for done in core_free.values():
            done()
        c_back.wait()
        c_grad.wait()
        c_out.wait()
        return

    serve(36)
    vec_step(1)
    serve(60)
    for g in range(groups):
        back_to(g).wait()

    @pl.loop(0, rows // BLK)
    def _(i):
        at = tile_at(i, BLK)
        res[at, :] = res[at, :] + back[at, :].astype(F32)

    c_grad = fetch(0, res, grad_o)
    serve(61)
    vec_step(2)
    serve(62)
    vec_step(3)
    serve(63)
    v_y.wait_recv()
    vec_o[...] = vbuf[8]
    vec_o[12:, :] = vbuf[8, 12:, :] + vbuf[9, 12:, :]
    for done in core_free.values():
        done()
    for i in range(NP):
        if i in BY_Y:
            mv.y[i].wait_send()
        for m in (mv.x, mv.zl, mv.zh):
            m[i].wait_send()
    for i in out_going:
        mv.out[i].wait()
    for i in far_going:
        mv.yf[i].wait_send()
    for v in v_at:
        v.wait_send()
    v_y.wait_send()
    for g in range(groups):
        tokens_to(g).wait_send()
    c_out.wait()
    c_grad.wait()
    assert not left


def compute(rows, fused, arrays):
    any_space = pl.BlockSpec(memory_space=pl.ANY)
    vmem = pl.BlockSpec(memory_space=pltpu.VMEM)
    if fused:
        out_parts = [jax.ShapeDtypeStruct(o, F32) for o in OUTS]
    else:
        out_parts = [jax.ShapeDtypeStruct((2, 2, 2, 2, *KINDS[k]), BF) for _, _, k in PARTS]
    low = lambda n=D: pltpu.VMEM((rows, n), BF)
    wide = lambda n: pltpu.VMEM((rows // PAIR * PAD, n), BF)
    dma = lambda n: pltpu.SemaphoreType.DMA((n,))
    scratch = [
        low(), low(), low(),
        pltpu.VMEM((D, FF), BF), pltpu.VMEM((FF, D), BF),
        wide(3 * D), low(), low(), low(),
        wide(3 * D), low(), low(), low(),
        low(FF), low(FF),
        pltpu.VMEM((rows, D), F32), low(), wide(D),
        pltpu.VMEM((2 * PAD, PAD), F32),
        pltpu.VMEM((rows, 128), F32),
        pltpu.VMEM((2, 2, 2, 2, 2, BLK, 1024), BF), pltpu.VMEM((2, 2, 2, 2, 2, 4 * BLK, TILE), BF),
        pltpu.VMEM((rows // PAIR, 1, PAD), F32), pltpu.VMEM((rows // PAIR, 1, PAD), F32),
        pltpu.VMEM((8, D), F32),
        pltpu.VMEM((D // 128, rows, 128), F32),
        dma(9), dma(NP),
    ]
    params = dict(vmem_limit_bytes=int(63.9 * 2**20))
    if fused:
        for lead in ((2, 2, 2), (2, 2), (2,), ()):
            scratch += [pltpu.VMEM((COUNT[k], *lead, *KINDS[k]), BF) for k in range(3)]
        scratch += [pltpu.VMEM((2, *KINDS[k]), F32) for k in range(3)]
        cross = NP - FIRST_CROSS
        scratch += [
            pltpu.VMEM((cross, 2, 2, 2, BLK, HALF), BF), low(), pltpu.VMEM((10, NV, D), F32),
            pltpu.VMEM((cross // 2, 2, BLK, D), BF),
            *([dma(NP)] * 8), *([dma(cross)] * 4), dma(2 * rows // GR + 5), dma(2 * rows // GR + 5),
        ]
        params.update(collective_id=0, has_side_effects=True)
    return pl.pallas_call(
        partial(body, fused),
        out_shape=[
            jax.ShapeDtypeStruct((D // 128, rows, 128), F32),
            jax.ShapeDtypeStruct((rows, D), F32),
            jax.ShapeDtypeStruct((8, 128) if fused else (rows, D), BF),
            jax.ShapeDtypeStruct((NV, D), F32),
            *out_parts,
        ],
        in_specs=[any_space] * 9 + [vmem] * (1 + NS),
        out_specs=[any_space] * 3 + [vmem] + [any_space] * len(out_parts),
        scratch_shapes=scratch,
        compiler_params=pltpu.CompilerParams(**params),
    )(*arrays)


VECTORS = (CQB, CVB, COUTB, CGAIN, CSHIFT, SQB, SVB, SOUTB, SGAIN, SSHIFT, FOUTB, FGAIN, FSHIFT)


def finish_body(n, copies, *refs):
    refs = list(refs)

    def take(count):
        got = refs[:count]
        del refs[:count]
        return got

    stream_h, grad_h, vec = take(3)
    sums = take(copies)
    stream_o, grad_o = take(2)
    vectors = take(len(VECTORS))
    (finb,) = take(1)
    sums_o = take(copies)
    stream, grad, wide, stream_t, grad_t, sems = take(6)
    held = take(copies)
    items = grad.shape[0] // LR
    c_grad = pltpu.make_async_copy(grad_h, grad, sems.at[0])
    c_stream = pltpu.make_async_copy(stream_h, stream, sems.at[1])
    c_grad.start()
    c_stream.start()
    into = [pltpu.make_async_copy(a, b, sems.at[2 + i]) for i, (a, b) in enumerate(zip(sums, held))]
    out = [pltpu.make_async_copy(a, b, sems.at[2 + i]) for i, (a, b) in enumerate(zip(held, sums_o))]
    for c in into:
        c.start()
    me = lax.axis_index("dp")
    share = D // n
    mine = pltpu.roll(vec[...], lax.rem(D - me * share, D), 1)
    for r, v in zip(VECTORS, vectors):
        v[...] = mine[r : r + 1, 0:share].reshape(v.shape)
    share = FF // n
    a_row = D // share
    v = vec[FINB : FINB + 8, :]
    at = lax.broadcasted_iota(jnp.int32, v.shape, 0) == lax.div(me, a_row)
    line = jnp.broadcast_to(jnp.sum(jnp.where(at, v, 0.0), axis=0, keepdims=True), v.shape)
    finb[...] = pltpu.roll(line, lax.rem(D - lax.rem(me, a_row) * share, D), 1)[0:1, 0:share]
    c_grad.wait()
    for j in range(D // 128):
        cols = slice(j * 128, (j + 1) * 128)
        for i in range(items):
            wide[0, j, pl.ds(i, LR, stride=items), :] = grad[i * LR : (i + 1) * LR, cols]
        grad_t[:, cols] = wide[0, j]
    c_grad = pltpu.make_async_copy(grad_t, grad_o, sems.at[0])
    c_grad.start()
    for a, b in zip(into, out):
        a.wait()
        b.start()
    c_stream.wait()
    for j in range(D // 128):
        cols = slice(j * 128, (j + 1) * 128)
        for i in range(items):
            wide[1, j, pl.ds(i, LR, stride=items), :] = stream[j, i * LR : (i + 1) * LR, :]
        stream_t[:, cols] = wide[1, j].astype(BF)
    c_stream = pltpu.make_async_copy(stream_t, stream_o, sems.at[1])
    c_stream.start()
    for c in out:
        c.wait()
    c_grad.wait()
    c_stream.wait()


def finish(n, stream, grad, vec, sums):
    any_space = pl.BlockSpec(memory_space=pl.ANY)
    vmem = pl.BlockSpec(memory_space=pltpu.VMEM)
    share = D // n
    shapes = [(share,)] * 5 + [(1, share)] * 8 + [(1, FF // n)]
    return pl.pallas_call(
        partial(finish_body, n, len(sums)),
        out_shape=[
            jax.ShapeDtypeStruct(grad.shape, BF),
            jax.ShapeDtypeStruct(grad.shape, F32),
            *(jax.ShapeDtypeStruct(s, F32) for s in shapes),
            *(jax.ShapeDtypeStruct(x.shape, F32) for x in sums),
        ],
        in_specs=[any_space] * 2 + [vmem] + [any_space] * len(sums),
        out_specs=[any_space] * 2 + [vmem] * len(shapes) + [any_space] * len(sums),
        scratch_shapes=[
            pltpu.VMEM(stream.shape, F32), pltpu.VMEM(grad.shape, F32), pltpu.VMEM((2, *stream.shape), F32),
            pltpu.VMEM(grad.shape, BF), pltpu.VMEM(grad.shape, F32),
            pltpu.SemaphoreType.DMA((2 + len(sums),)),
            *(pltpu.VMEM(x.shape, F32) for x in sums),
        ],
        compiler_params=pltpu.CompilerParams(vmem_limit_bytes=int(63.9 * 2**20)),
    )(stream, grad, vec, *sums)


def partner(block):
    return lax.ppermute(block, "stream", [(0, 1), (1, 0)])


def reduce_parts(parts, vec):
    def natural(some):
        done = []
        for p in some:
            r, n = p.shape[-2:]
            done.append(p.transpose(1, 2, 3, 0, 4, 5).reshape(16 * r, n))
        return jnp.concatenate(done, axis=1)

    def scatter(some, shared=False):
        x = natural(some)
        if shared:
            x = lax.psum(x, "stream")
        return lax.psum_scatter(x, "dp", scatter_dimension=0, tiled=True).astype(F32)

    sums = [
        scatter(parts[0:3]), scatter(parts[3:6]), scatter(parts[6:7]), scatter(parts[7:10]),
        scatter(parts[10:11], True), scatter(parts[11:14], True),
    ]
    own = lax.psum(vec[:CGAIN], "dp")
    return sums, jnp.concatenate([own, lax.psum(vec[CGAIN:], ("stream", "dp"))])


def local(*args):
    a = dict(zip(NAMES, args))
    n = lax.axis_size("dp")
    fused = n == 16
    shape = a["tokens"].shape
    items = shape[1]

    def by_slot(v):
        return v[0].transpose(1, 0, 2).reshape(items * LR, D)

    def back_to_items(v):
        return v.reshape(LR, items, D).transpose(1, 0, 2).reshape(shape)

    tok, cot = by_slot(a["tokens"]), by_slot(a["cotangent"])
    far = tok if fused else partner(tok)
    outs = compute(
        items * LR,
        fused,
        [tok, far, cot, a["cross_qkv"], a["cross_out"], a["self_qkv"][0], a["self_out"][0],
         a["ffn_in"][0], a["ffn_out"][0], a["region_mask"], *(a[k] for k in SMALL)],
    )
    stream, grad, back, vec = outs[:4]
    sums = outs[4:]
    if not fused:
        grad = grad + partner(back).astype(F32)
        sums, vec = reduce_parts(sums, vec)
    done = finish(n, stream, grad, vec, sums if fused else [])
    if fused:
        sums = done[16:]
    fout, fin, sout, sqkv, cout, cqkv = sums
    cqb, cvb, coutb, cgain, cshift, sqb, svb, soutb, sgain, sshift, foutb, fgain, fshift, finb = done[2:16]
    return (
        back_to_items(done[0]), back_to_items(done[1]),
        cqkv, cqb, cvb, cout, coutb, cgain, cshift,
        sqkv[None], sqb, svb, sout[None], soutb, sgain, sshift,
        fin[None], finb, fout[None], foutb, fgain, fshift,
    )


def solution(mesh):
    both = P("stream", "dp")
    one = P("stream")
    specs = {n: one for n in NAMES}
    specs.update({n: P() for n in NAMES if n.startswith("cross")})
    specs.update(tokens=both, cotangent=both, region_mask=P("dp"))
    return jax.shard_map(
        local,
        mesh=mesh,
        in_specs=tuple(specs[n] for n in NAMES),
        out_specs=(both, both) + (P("dp"),) * 7 + (both,) * 13,
        check_vma=False,
    )
```

```python
from functools import partial
from types import SimpleNamespace

import jax
import jax.numpy as jnp
from jax import lax
from jax.experimental import pallas as pl
from jax.experimental.pallas import tpu as pltpu
from jax.sharding import PartitionSpec as P

D = 768
H = 12
HD = 64
FF = 3072
LW = 20
LR = 36
BF = jnp.bfloat16
F32 = jnp.float32
GROUP = 4
GR = GROUP * LR
PAIR = 2 * LR
PAD = 80
TILE = 256
BLK = 48
NH = 2
LNB = 144
FGAIN, FSHIFT, FOUTB, SGAIN, SSHIFT, SOUTB, SQB, SVB, FINB = 0, 1, 2, 3, 4, 5, 6, 7, 8
CGAIN, CSHIFT, COUTB, CQB, CVB = 12, 13, 14, 15, 16
NV = 24


def nn(a, b):
    return lax.dot_general(a, b, (((1,), (0,)), ((), ())), preferred_element_type=F32)


def nt(a, b):
    return lax.dot_general(a, b, (((1,), (1,)), ((), ())), preferred_element_type=F32)


def tn(a, b):
    return lax.dot_general(a, b, (((0,), (0,)), ((), ())), preferred_element_type=F32)


def tile_at(i, size=TILE):
    return pl.ds(pl.multiple_of(i * size, size), size)


def total(x):
    return jnp.sum(x.astype(F32), axis=0, keepdims=True)


def norm_forward(res, gain, shift, hat, columns, col, y_low, first, count):
    @pl.loop(0, count // LNB)
    def _(i):
        at = pl.ds(pl.multiple_of(first + i * LNB, 16), LNB)
        r = res[at, :]
        centre = r - jnp.mean(r, axis=-1, keepdims=True)
        rs = lax.rsqrt(jnp.mean(centre * centre, axis=-1, keepdims=True) + 1e-12)
        xh = centre * rs
        y = xh * gain[...] + shift[...]
        hat[at, :] = xh.astype(BF)
        columns[at, col : col + 1] = rs
        res[at, :] = y
        y_low[at, :] = y.astype(BF)


def norm_grad(dy, xh, rs, gain):
    dx = dy * gain
    return rs * (
        dx - jnp.mean(dx, axis=-1, keepdims=True) - xh * jnp.mean(dx * xh, axis=-1, keepdims=True)
    )


def norm_backward(res, gain, hat, columns, col, g_low, vec, at_gain, at_shift, at_bias):
    rows = res.shape[0]

    @pl.loop(0, rows // LNB)
    def _(i):
        at = tile_at(i, LNB)
        dy = res[at, :]
        xh = hat[at, :].astype(F32)
        g = norm_grad(dy, xh, columns[at, col : col + 1], gain[...])
        low = g.astype(BF)
        res[at, :] = g
        g_low[at, :] = low
        vec[at_gain : at_gain + 1, :] += total(dy * xh)
        vec[at_shift : at_shift + 1, :] += total(dy)
        vec[at_bias : at_bias + 1, :] += total(low)


def head_masks():
    lane = lax.broadcasted_iota(jnp.int32, (1, 128), 1)
    first = (lane < HD).astype(BF)
    return first, (1 - first).astype(BF)


def stack_heads(x, masks):
    return jnp.concatenate([x * masks[0], x * masks[1]], axis=0)


def pick_heads(x):
    lane = lax.broadcasted_iota(jnp.int32, (PAIR, 128), 1)
    return jnp.where(lane < HD, x[:PAIR], x[PAD : PAD + PAIR])


def store_pairs(dst, x, at, first=0):
    zeros = jnp.zeros((PAD - PAIR, x.shape[1]), F32)
    for p in range(x.shape[0] // PAIR):
        block = jnp.concatenate([x[p * PAIR : (p + 1) * PAIR], zeros], axis=0)
        dst[pl.ds(pl.multiple_of((first + p) * PAD, 16), PAD), at] = block.astype(BF)


def probabilities(q2, k, rid, kid):
    s = nt(q2, k) * (1.0 / HD**0.5)
    s = jnp.where(rid == kid, s, -1000000000.0)
    e = jnp.exp(s - jnp.max(s, axis=-1, keepdims=True))
    return e * (1.0 / jnp.sum(e, axis=-1, keepdims=True))


def attention_forward(g, qkv, rid, kids, out):
    masks = head_masks()
    group = pl.ds(pl.multiple_of(g * GR, GR), GR)
    for p in range(H // 2):
        done = []
        for half in range(2):
            rows = pl.ds(pl.multiple_of((2 * g + half) * PAD, 16), PAD)
            q2 = stack_heads(qkv[rows, p * 128 : p * 128 + 128], masks)
            prob = probabilities(q2, qkv[rows, D + p * 128 : D + p * 128 + 128], rid[...], kids[2 * g + half])
            done.append(pick_heads(nn(prob.astype(BF), qkv[rows, 2 * D + p * 128 : 2 * D + p * 128 + 128])))
        out[group, p * 128 : p * 128 + 128] = jnp.concatenate(done, axis=0).astype(BF)


def attention_backward(g, qkv, grad_out, columns, col, out):
    masks = head_masks()
    group = pl.ds(pl.multiple_of(g * GR, GR), GR)
    query = lax.broadcasted_iota(jnp.int32, (1, 2 * PAD), 1)
    second = ((query >= LR) & (query < PAD)) | (query >= PAD + LR)
    query_item = second.astype(F32)
    for p in range(H // 2):
        done = [[], [], []]
        for half in range(2):
            rows = pl.ds(pl.multiple_of((2 * g + half) * PAD, 16), PAD)
            q2 = stack_heads(qkv[rows, p * 128 : p * 128 + 128], masks)
            k = qkv[rows, D + p * 128 : D + p * 128 + 128]
            v = qkv[rows, 2 * D + p * 128 : 2 * D + p * 128 + 128]
            g2 = stack_heads(grad_out[rows, p * 128 : p * 128 + 128], masks)
            s = nt(k, q2) * (1.0 / HD**0.5)
            s = jnp.where(columns[rows, col : col + 1] == query_item, s, -1000000000.0)
            e = jnp.exp(s - jnp.max(s, axis=0, keepdims=True))
            prob = e * (1.0 / jnp.sum(e, axis=0, keepdims=True))
            gp = nt(v, g2)
            gv = nn(prob.astype(BF), g2)
            s = prob * (gp - jnp.sum(gp * prob, axis=0, keepdims=True))
            s = s.astype(BF)
            done[0].append(pick_heads(tn(s, k)) * (1.0 / HD**0.5))
            done[1].append(nn(s, q2)[:PAIR] * (1.0 / HD**0.5))
            done[2].append(gv[:PAIR])
        for part in range(3):
            at = part * D + p * 128
            out[group, at : at + 128] = jnp.concatenate(done[part], axis=0).astype(BF)


def by_item(wide, dst, g):
    items = wide.shape[1] // LR
    for j in range(D // 128):
        got = [wide[j, pl.ds(g * GROUP + i, LR, stride=items), :] for i in range(GROUP)]
        dst[g * GR : (g + 1) * GR, j * 128 : (j + 1) * 128] = jnp.concatenate(got, axis=0).astype(BF)


def by_slot(value, wide, j):
    items = value.shape[0] // LR
    for i in range(items):
        wide[j, pl.ds(i, LR, stride=items), :] = value[i * LR : (i + 1) * LR]


def widen(src, wide):
    @pl.loop(0, src.shape[0] // BLK)
    def _(i):
        at = tile_at(i, BLK)
        for j in range(D // 128):
            wide[j, at, :] = src[at, j * 128 : (j + 1) * 128].astype(F32)


NAMES = (
    "tokens", "region_mask", "cotangent", "cross_qkv", "cross_q_bias", "cross_v_bias",
    "cross_out", "cross_out_bias", "cross_gain", "cross_shift", "self_qkv", "self_q_bias",
    "self_v_bias", "self_out", "self_out_bias", "self_gain", "self_shift", "ffn_in",
    "ffn_in_bias", "ffn_out", "ffn_out_bias", "ffn_gain", "ffn_shift",
)
SMALL = tuple(n for n in NAMES if n.endswith(("bias", "gain", "shift")))
NS = len(SMALL)
KINDS = ((4 * BLK, TILE), (BLK, 1024), (BLK, D))
PARTS = (
    *((0, TILE * i, 0) for i in range(3)),
    *((1, 1024 * i, 1) for i in range(3)),
    (2, 0, 2),
    *((3, D * i, 2) for i in range(3)),
    (4, 0, 2),
    *((5, D * i, 2) for i in range(3)),
)
NP = len(PARTS)
FIRST_CROSS = 10
OUTS = ((4 * BLK, D), (BLK, FF), (BLK, D), (BLK, 3 * D), (BLK, D), (BLK, 3 * D))
HALF = D // 2
IN_KIND = [sum(p[2] == PARTS[i][2] for p in PARTS[:i]) for i in range(NP)]
COUNT = [sum(p[2] == k for p in PARTS) for k in range(3)]


BY_Y = (10, 12,)
ORDER = (
    (2, 1, 0),
    (1, 2, 0),
    (2, 1, 0),
    (1, 0, 2),
    (2, 1, 0),
    (2, 1, 0),
    (2, 1, 0),
    (2, 1, 0),
    (2, 1, 0),
    (2, 1, 0),
    (2, 1, 0),
    (2, 1, 0),
    (2, 1, 0),
    (2, 1, 0),
)
SERVE = {
    -3: (100,),
    20: (101,),
    21: (102,),
    -6: (103,),
    5: (200,),
    30: (104, 201,),
    31: (105,),
    6: (202,),
    40: (106, 203,),
    42: (300, 204,),
    43: (302,),
    7: (301,),
    -10: (107,),
    33: (108, 303,),
    34: (109, 205, 400,),
    50: (304, 110, 206,),
    51: (402, 401,),
    52: (207, 305,),
    11: (404,),
    12: (306, 208,),
    -14: (111,),
    36: (510, 403, 307, 112,),
    60: (113, 405, 209, 406, 308, 407,),
    61: (211, 309, 210, 408, 311, 512, 213,),
    62: (409, 310, 411, 212, 313, 611,),
    63: (410, 312, 413, 610, 412, 613, 612,),
}


def body(fused, *refs):
    refs = list(refs)

    def take(n):
        got = refs[:n]
        del refs[:n]
        return got

    tok_h, far_h, cot_h, cqkv_h, cout_h, sqkv_h, sout_h, fin_h, fout_h = take(9)
    (mask_in,) = take(1)
    given = dict(zip(SMALL, take(NS)))
    out_o, grad_o, back_o, vec_o = take(4)
    parts_o = take(len(OUTS) if fused else NP)
    (tok, far, cot, wp, wq, xqkv, xatt, joined, hat1, sqkv, satt, settled, hat2, active, inner,
     res, g_low, gpad, rid, columns, slot_a, slot_b, kid_own, kid_far, sv,
     out_f, sems, part_sems) = take(28)
    rows = tok.shape[0]
    groups = rows // GR
    gx = active
    side = lax.axis_index("stream")

    def fetch(i, src, dst):
        c = pltpu.make_async_copy(src, dst, sems.at[i])
        c.start()
        return c

    if fused:
        acc, xr, za, zb, fin = take(3), take(3), take(3), take(3), take(3)
        yr, back, vbuf, ybf = take(4)
        s_core, r_core, s_x, r_x, s_za, r_za, s_zb, r_zb, s_y, r_y, s_yf, r_yf, s_m, r_m = take(14)
        me = lax.axis_index("dp")
        core, x = lax.rem(me, 2), lax.rem(lax.div(me, 2), 2)
        zl, zh = lax.rem(lax.div(me, 4), 2), lax.div(me, 8)
        to_y, to_core = (1 - side, me), (side, me + 1 - 2 * core)
        to_x, to_zl, to_zh = (side, me + 2 - 4 * x), (side, me + 4 - 8 * zl), (side, me + 8 - 16 * zh)
        peers = (to_y, to_core, to_x, to_zl, to_zh)
        barrier = pltpu.get_barrier_semaphore()
        for p in peers:
            pl.semaphore_signal(barrier, inc=1, device_id=p, device_id_type=pl.DeviceIdType.MESH)

        def remote(src, dst, send, recv, peer):
            return pltpu.make_async_remote_copy(
                src_ref=src, dst_ref=dst, send_sem=send, recv_sem=recv,
                device_id=peer, device_id_type=pl.DeviceIdType.MESH,
            )

    c_tok = fetch(0, tok_h, g_low)
    def fetch_self():
        return [
            *(fetch(4 + j, sqkv_h.at[:, j * D : (j + 1) * D], wq.at[j * D : (j + 1) * D, :]) for j in range(3)),
            fetch(7, sout_h, wq.at[3 * D :, :]),
        ]

    c_tok.wait()
    c_cqkv = fetch(1, cqkv_h, wp.at[:, 0 : 3 * D])
    c_cot = fetch(8, cot_h, settled)
    c_cout = fetch(3, cout_h, wp.at[:, 3 * D :])
    if not fused:
        c_far = fetch(2, far_h, satt)

    c_self = fetch_self()
    widen(g_low, out_f)
    if fused:
        pl.semaphore_wait(barrier, len(peers))

        def tokens_to(g):
            at = pl.ds(pl.multiple_of(g * GR, GR), GR)
            return remote(tok.at[at, :], far.at[at, :], s_m.at[g], r_m.at[g], to_y)

    for g in range(groups):
        by_item(out_f, tok, g)
        if fused:
            tokens_to(g).start()

    sm = SimpleNamespace()
    for i, n in enumerate(SMALL):
        row_of = given[n]
        if len(given[n].shape) == 1:
            sv[i : i + 1, :] = given[n][...].reshape(1, D)
            row_of = sv.at[i : i + 1, :]
        setattr(sm, n, row_of)
    vec = vbuf.at[0] if fused else vec_o
    vec[...] = jnp.zeros(vec.shape, F32)
    edge = lax.broadcasted_iota(jnp.int32, (2 * PAD, PAD), 0)
    second = ((edge >= LR) & (edge < PAD)) | (edge >= PAD + LR)
    rid[...] = second.astype(F32)
    items = rows // LR
    present = (mask_in[...] > 0).astype(F32)
    word = (lax.broadcasted_iota(jnp.int32, (items, LR), 1) < LW).astype(F32)
    slot = lax.broadcasted_iota(jnp.int32, (LR, GR), 0)
    lane = lax.broadcasted_iota(jnp.int32, (1, GR), 1)
    lane_item = sum((lane >= LR * i).astype(jnp.int32) for i in range(1, GROUP))
    spread_slots = (slot == lane - LR * lane_item).astype(BF)
    row = lax.broadcasted_iota(jnp.int32, (GR, GR), 0)
    diagonal = row == lax.broadcasted_iota(jnp.int32, (GR, GR), 1)

    def lay_masks(mask, kid, col, own):
        spread = nn(mask.astype(BF), spread_slots)
        for g in range(groups):
            line = jnp.zeros((1, GR), F32)
            for i in range(GROUP):
                line += jnp.where(lane_item == i, spread[g * GROUP + i : g * GROUP + i + 1, :], 0.0)
            ids = jnp.where(line > 0.5, (lane_item % 2).astype(F32), -1.0)
            for half in range(2):
                kid[2 * g + half, :, 0:PAIR] = ids[:, half * PAIR : (half + 1) * PAIR]
                kid[2 * g + half, :, PAIR:] = jnp.full((1, PAD - PAIR), -1.0, F32)
            if own:
                column = jnp.sum(jnp.where(diagonal, line, 0.0), axis=-1, keepdims=True)
                columns[g * GR : (g + 1) * GR, 0:1] = column
            column = jnp.sum(jnp.where(diagonal, ids, 0.0), axis=-1, keepdims=True)
            none = jnp.full((PAD - PAIR, 1), -1.0, F32)
            for half in range(2):
                padded = jnp.concatenate([column[half * PAIR : (half + 1) * PAIR], none], axis=0)
                columns[(2 * g + half) * PAD : (2 * g + half + 1) * PAD, col : col + 1] = padded

    lay_masks(jnp.where(side == 0, word, present), kid_own, 3, True)
    lay_masks(jnp.where(side == 0, present, word), kid_far, 4, False)

    c_cqkv.wait()

    @pl.loop(0, 3)
    def _(j):
        at = tile_at(j)
        store_pairs(xqkv, nn(tok[...], wp[:, at]) + sm.cross_q_bias[:, at], at)

    c_cot.wait()
    widen(settled, out_f)
    for g in range(groups):
        by_item(out_f, cot, g)
    if not fused:
        c_far.wait()
        widen(satt, out_f)
        for g in range(groups):
            by_item(out_f, far, g)

    c_cout.wait()
    for c in c_self:
        c.wait()
    part_rows, part_groups = rows // NH, groups // NH

    @pl.loop(0, NH)
    def _(h):
        first = h * part_rows
        at_h = pl.ds(pl.multiple_of(first, 16), part_rows)

        @pl.loop(h * part_groups, (h + 1) * part_groups)
        def _(g):
            at_g = pl.ds(pl.multiple_of(g * GR, GR), GR)
            if fused:
                tokens_to(g).wait_recv()
            far_g = far[at_g, :]
            for j in range(3, 9):
                y = nn(far_g, wp[:, j * TILE : (j + 1) * TILE])
                if j >= 6:
                    y = y + sm.cross_v_bias[:, (j - 6) * TILE : (j - 5) * TILE]
                store_pairs(xqkv, y, slice(j * TILE, (j + 1) * TILE), 2 * g)
            attention_forward(g, xqkv, rid, kid_far, xatt)

        @pl.loop(0, 3)
        def _(j):
            at = tile_at(j)
            w_at = pl.ds(pl.multiple_of(3 * D + j * TILE, TILE), TILE)
            res[at_h, at] = tok[at_h, at].astype(F32) + nn(xatt[at_h, :], wp[:, w_at]) + sm.cross_out_bias[:, at]

        @pl.when(h == NH - 1)
        def _():
            fetch(1, fin_h, wp)

        norm_forward(res, sm.cross_gain, sm.cross_shift, hat1, columns, 1, joined, first, part_rows)
        for part in range(3):
            @pl.loop(0, 3)
            def _(j):
                at = tile_at(j)
                y = nn(joined[at_h, :], wq[part * D : (part + 1) * D, at])
                if part == 0:
                    y = y + sm.self_q_bias[:, at]
                if part == 2:
                    y = y + sm.self_v_bias[:, at]
                store_pairs(sqkv, y, pl.ds(pl.multiple_of(part * D + j * TILE, TILE), TILE), 2 * part_groups * h)

        @pl.loop(h * part_groups, (h + 1) * part_groups)
        def _(g):
            attention_forward(g, sqkv, rid, kid_own, satt)

        @pl.loop(0, 3)
        def _(j):
            at = tile_at(j)
            res[at_h, at] += nn(satt[at_h, :], wq[3 * D :, at]) + sm.self_out_bias[:, at]

        @pl.when(h == NH - 1)
        def _():
            fetch(3, fout_h, wq)

        norm_forward(res, sm.self_gain, sm.self_shift, hat2, columns, 2, settled, first, part_rows)

    pltpu.make_async_copy(fin_h, wp, sems.at[1]).wait()

    @pl.loop(0, FF // TILE)
    def _(j):
        at = tile_at(j)
        x = nn(settled[...], wp[:, at]) + sm.ffn_in_bias[:, at]
        half = 0.5 * (1.0 + lax.erf(x * (0.5**0.5)))
        active[:, at] = (x * half).astype(BF)
        inner[:, at] = x.astype(BF)

    pltpu.make_async_copy(fout_h, wq, sems.at[3]).wait()

    @pl.loop(0, 3)
    def _(j):
        at = tile_at(j)
        res[:, at] += nn(active[...], wq[:, at]) + sm.ffn_out_bias[:, at]

    @pl.loop(0, rows // LNB)
    def _(i):
        at = tile_at(i, LNB)
        r = res[at, :]
        ok = columns[at, 0:1]
        gain = sm.ffn_gain[...]
        centre = r - jnp.mean(r, axis=-1, keepdims=True)
        rs = lax.rsqrt(jnp.mean(centre * centre, axis=-1, keepdims=True) + 1e-12)
        xh = centre * rs
        y = xh * gain + sm.ffn_shift[...]
        for j in range(D // 128):
            out_f[j, at, :] = y[:, j * 128 : (j + 1) * 128] * ok
        dy = cot[at, :].astype(F32) * ok
        g = norm_grad(dy, xh, rs, gain)
        low = g.astype(BF)
        res[at, :] = g
        cot[at, :] = low
        vec[FGAIN : FGAIN + 1, :] += total(dy * xh)
        vec[FSHIFT : FSHIFT + 1, :] += total(dy)
        vec[FOUTB : FOUTB + 1, :] += total(low)

    def slot_of(i):
        kind = PARTS[i][2]
        if kind == 0:
            return slot_b.at[i % 2]
        ref = slot_a.at[i % 2]
        return ref if kind == 1 else ref.at[:, :, :, :, :, 0:D]

    mv = SimpleNamespace(core={}, y={}, cut={}, yf={}, out={}, acc={}, got={}, fin={})
    if fused:
        here = (zh, zl, x)

        def late(i):
            return [j for j in range(FIRST_CROSS, NP) if j not in BY_Y].index(i)

        over = (to_zh, to_zl, to_x)

        def cut(ref, places, *after):
            return ref.at[(*(places.get(d, slice(None)) for d in range(3)), *after)]

        for i in range(NP):
            out, col, kind = PARTS[i]
            n, width = IN_KIND[i], KINDS[kind][1]
            a = acc[kind].at[n]
            mv.core[i] = remote(slot_of(i).at[1 - core], a, s_core.at[i], r_core.at[i], to_core)
            got = [xr[kind].at[n], za[kind].at[n], zb[kind].at[n]]
            c = i - FIRST_CROSS
            if i in BY_Y:
                mine = pl.ds(pl.multiple_of(side * HALF, HALF), HALF)
                other = pl.ds(pl.multiple_of((1 - side) * HALF, HALF), HALF)
                mv.y[i] = remote(a.at[:, :, :, :, other], yr.at[BY_Y.index(i)], s_y.at[c], r_y.at[c], to_y)
                a = a.at[:, :, :, :, mine]
                short = pl.ds(0, HALF)
                got = [got[0].at[:, :, :, short], got[1].at[:, :, short], got[2].at[:, short]]
                width = HALF
            mv.acc[i], mv.got[i] = a, got
            places = {}
            sems_of = ((s_x, r_x), (s_za, r_za), (s_zb, r_zb))
            for step, d in enumerate(ORDER[i]):
                send, recv = sems_of[step]
                src = cut(a, {**places, d: 1 - here[d]})
                mv.cut[step, i] = remote(src, got[step], send.at[i], recv.at[i], over[d])
                places[d] = here[d]
            if i in BY_Y:
                col0 = pl.ds(pl.multiple_of(col + side * HALF, HALF), HALF)
            else:
                col0 = pl.ds(col, width)
            for place in range(2):
                f = fin[kind].at[place]
                if i in BY_Y:
                    f = f.at[:, 0:HALF]
                    mv.yf[i, place] = remote(f, parts_o[out].at[:, col0], s_yf.at[c], r_yf.at[c], to_y)
                mv.fin[i, place] = f
                mv.out[i, place] = pltpu.make_async_copy(f, parts_o[out].at[:, col0], part_sems.at[i])
            if i >= FIRST_CROSS and i not in BY_Y:
                mv.yf[i, 0] = remote(ybf.at[late(i), 0], ybf.at[late(i), 1], s_yf.at[c], r_yf.at[c], to_y)
        leaving = ([], [], [])


        def leave(i, value):
            before = leaving[PARTS[i][2]]
            place = len(before) % 2
            if len(before) > 1:
                gone(before[-2])
            before.append((i, place))
            mv.fin[i, place][...] = value
            mv.out[i, place].start()
            if i in BY_Y:
                mv.yf[i, place].start()

        def gone(what):
            mv.out[what].wait()
            if what[0] in BY_Y:
                mv.yf[what].wait_send()

        def t1(i):
            mv.core[i].wait_recv()
            out, col, kind = PARTS[i]
            a, own = acc[kind].at[IN_KIND[i]], slot_of(i)

            @pl.loop(0, 8)
            def _(d):
                p, q, r = lax.div(d, 4), lax.rem(lax.div(d, 2), 2), lax.rem(d, 2)
                a[p, q, r] = a[p, q, r] + own[core, p, q, r]

            (mv.y[i] if i in BY_Y else mv.cut[0, i]).start()

        def ty(i):
            mv.y[i].wait_recv()
            a, c = mv.acc[i], BY_Y.index(i)

            @pl.loop(0, 8)
            def _(d):
                p, q, r = lax.div(d, 4), lax.rem(lax.div(d, 2), 2), lax.rem(d, 2)
                a[p, q, r] = a[p, q, r] + yr[c, p, q, r]

            mv.cut[0, i].start()

        def t2(i):
            mv.cut[0, i].wait_recv()
            a, r = mv.acc[i], mv.got[i][0]
            first = ORDER[i][0]

            @pl.loop(0, 4)
            def _(d):
                p, q = lax.div(d, 2), lax.rem(d, 2)
                at = [p, q]
                at.insert(first, here[first])
                at = tuple(at)
                a[at] = a[at] + r[p, q]

            mv.cut[1, i].start()

        def t3(i):
            mv.cut[1, i].wait_recv()
            a, r = mv.acc[i], mv.got[i][1]
            for p in range(2):
                at = list(here)
                at[ORDER[i][2]] = p
                at = tuple(at)
                a[at] = a[at] + r[p]
            mv.cut[2, i].start()

        def t4(i):
            mv.cut[2, i].wait_recv()
            whole = mv.acc[i][zh, zl, x].astype(F32) + mv.got[i][2][...].astype(F32)
            if i >= FIRST_CROSS and i not in BY_Y:
                ybf[late(i), 0] = whole.astype(BF)
                mv.yf[i, 0].start()
            else:
                leave(i, whole)

        def tf(i):
            mv.yf[i, 0].wait_recv()
            if i not in BY_Y:
                leave(i, ybf[late(i), 0].astype(F32) + ybf[late(i), 1].astype(F32))

        steps = (t1, t2, t3, t4, ty, tf)
    left = []
    for i in range(NP):
        left += [n * 100 + i for n in (1, 2, 3, 4) + (5,) * (i in BY_Y) + (6,) * (i >= FIRST_CROSS)]
    core_free = {}

    def serve(place):
        if fused:
            for t in SERVE.get(place, ()):
                left.remove(t)
                steps[t // 100 - 1](t % 100)

    def free_slot(i):
        if i in core_free:
            core_free.pop(i)()

    def push(i):
        if fused:
            mv.core[i].start()
            core_free[i] = mv.core[i].wait_send
        else:
            c = pltpu.make_async_copy(slot_of(i), parts_o[i], part_sems.at[i])
            c.start()
            core_free[i] = c.wait

    def same_slot(i):
        for j in range(i - 1, -1, -1):
            if (PARTS[j][2] == 0) == (PARTS[i][2] == 0) and j % 2 == i % 2:
                return j
        return None

    def weight_part(i, left, right, col0):
        serve(-1 - i)
        free_slot(same_slot(i))
        ref = slot_of(i)
        width = KINDS[PARTS[i][2]][1]

        @pl.loop(0, width // TILE)
        def _(j):
            src = right[:, pl.ds(pl.multiple_of(col0 + j * TILE, TILE), TILE)]
            w = tn(left[...], src).astype(BF)
            for d in range(16):
                ref[d % 2, d // 8, (d // 4) % 2, (d // 2) % 2, :, tile_at(j)] = w[d * BLK : (d + 1) * BLK, :]

        push(i)
        serve(i)

    for col in range(3):
        serve(-1 - col)
        free_slot(same_slot(col))
        ref = slot_of(col)

        @pl.loop(0, 4)
        def _(t):
            w = tn(active[:, tile_at(t, D)], cot[:, col * TILE : (col + 1) * TILE]).astype(BF)
            for d in range(4):
                ref[d % 2, lax.div(t, 2), lax.rem(t, 2), d // 2, :, :] = w[d * 4 * BLK : (d + 1) * 4 * BLK, :]

        push(col)
        serve(col)

    for r in range(3):
        @pl.loop(4 * r, 4 * r + 4)
        def _(j):
            at = tile_at(j)
            ga = nt(cot[...], wq[at, :])
            y = inner[:, at].astype(F32)
            slope = 0.5 * (1.0 + lax.erf(y * (0.5**0.5))) + y * jnp.exp(-0.5 * y * y) * 0.3989422804014327
            gi = (ga * slope).astype(BF)
            inner[:, at] = gi

        serve(20 + r)
    for r in range(4):
        vec[FINB + r : FINB + r + 1, :] = total(inner[:, r * D : (r + 1) * D])
    c_self = fetch_self()

    for col in range(3):
        weight_part(3 + col, settled, inner, col * 1024)

    @pl.loop(0, 3)
    def _(j):
        at = tile_at(j)
        res[:, at] += nt(inner[...], wp[at, :])

    serve(30)
    c_cqkv = fetch(1, cqkv_h, wp.at[:, 0 : 3 * D])
    c_cout = fetch(3, cout_h, wp.at[:, 3 * D :])
    norm_backward(res, sm.self_gain, hat2, columns, 2, g_low, vec, SGAIN, SSHIFT, SOUTB)
    serve(31)
    weight_part(6, satt, g_low, 0)
    for j in range(D // 128):
        by_slot(out_f[j], out_f, j)
        satt[:, j * 128 : (j + 1) * 128] = out_f[j].astype(BF)
    c_out = fetch(8, satt, out_o)
    for c in c_self:
        c.wait()

    @pl.loop(0, 3)
    def _(j):
        at = tile_at(j)
        w_at = pl.ds(pl.multiple_of(3 * D + j * TILE, TILE), TILE)
        store_pairs(gpad, nt(g_low[...], wq[w_at, :]), at)

    serve(32)

    def serve_each(place, g):
        for k in range(groups):
            if fused and SERVE.get(place + k):
                @pl.when(g == k)
                def _():
                    serve(place + k)

    @pl.loop(0, groups)
    def _(g):
        attention_backward(g, sqkv, gpad, columns, 3, gx)
        serve_each(40, g)

    for part in range(3):
        weight_part(7 + part, joined, gx, part * D)
    vec[SQB : SQB + 1, :] = total(gx[:, 0:D])
    vec[SVB : SVB + 1, :] = total(gx[:, 2 * D : 3 * D])

    @pl.loop(0, 3)
    def _(j):
        at = tile_at(j)
        g = res[:, at]
        for part in range(3):
            w_at = pl.ds(pl.multiple_of(part * D + j * TILE, TILE), TILE)
            g += nt(gx[:, part * D : (part + 1) * D], wq[w_at, :])
        res[:, at] = g

    serve(33)
    norm_backward(res, sm.cross_gain, hat1, columns, 1, g_low, vec, CGAIN, CSHIFT, COUTB)
    serve(34)
    weight_part(10, xatt, g_low, 0)
    c_cqkv.wait()
    c_cout.wait()

    @pl.loop(0, 3)
    def _(j):
        at = tile_at(j)
        store_pairs(gpad, nt(g_low[...], wp[at, 3 * D :]), at)

    serve(35)
    if fused:

        def back_to(g):
            at = pl.ds(pl.multiple_of(g * GR, GR), GR)
            return remote(g_low.at[at, :], back.at[at, :], s_m.at[groups + g], r_m.at[groups + g], to_y)

    @pl.loop(0, groups)
    def _(g):
        attention_backward(g, xqkv, gpad, columns, 4, gx)
        at = pl.ds(pl.multiple_of(g * GR, GR), GR)
        pair = gx[at, D : 3 * D]
        for j in range(3):
            w_at = slice(j * TILE, (j + 1) * TILE)
            g_low[at, w_at] = nt(pair, wp[w_at, D : 3 * D]).astype(BF)
        if fused:
            back_to(g).start()
        serve_each(50, g)

    vec[CQB : CQB + 1, :] = total(gx[:, 0:D])
    vec[CVB : CVB + 1, :] = total(gx[:, 2 * D : 3 * D])
    if fused:
        v_at = [
            remote(vbuf.at[j], vbuf.at[4 + j], s_m.at[2 * groups + j], r_m.at[2 * groups + j], p)
            for j, p in enumerate((to_core, to_x, to_zl, to_zh))
        ]
        v_y = remote(vbuf.at[8], vbuf.at[9], s_m.at[2 * groups + 4], r_m.at[2 * groups + 4], to_y)

        def vec_step(j):
            v_at[j].wait_recv()
            if j < 3:
                vbuf[j + 1] = vbuf[j] + vbuf[4 + j]
                v_at[j + 1].start()
            else:
                vbuf[8] = vbuf[3] + vbuf[7]
                v_y.start()

        v_at[0].start()
    weight_part(11, tok, gx, 0)
    weight_part(12, far, gx, D)
    if fused:
        vec_step(0)
    weight_part(13, far, gx, 2 * D)

    @pl.loop(0, 3)
    def _(j):
        at = tile_at(j)
        res[:, at] += nt(gx[:, 0:D], wp[at, 0:D])

    if not fused:
        for src, dst in ((g_low, back_o), (res, grad_o)):
            for j in range(D // 128):
                by_slot(src[:, j * 128 : (j + 1) * 128].astype(F32), out_f, j)
                fetch(0, out_f.at[j], dst.at[:, j * 128 : (j + 1) * 128]).wait()
        for done in core_free.values():
            done()
        c_out.wait()
        return

    serve(36)
    vec_step(1)
    serve(60)
    for g in range(groups):
        back_to(g).wait()

    c_grad = []
    for j in range(D // 128):
        cols = slice(j * 128, (j + 1) * 128)
        by_slot(res[:, cols] + back[:, cols].astype(F32), out_f, j)
        c_grad.append(pltpu.make_async_copy(out_f.at[j], grad_o.at[:, cols], sems.at[j]))
        c_grad[-1].start()
    serve(61)
    vec_step(2)
    serve(62)
    vec_step(3)
    serve(63)
    v_y.wait_recv()
    vec_o[...] = vbuf[8]
    vec_o[12:, :] = vbuf[8, 12:, :] + vbuf[9, 12:, :]
    for done in core_free.values():
        done()
    for i in range(NP):
        if i in BY_Y:
            mv.y[i].wait_send()
        for step in range(3):
            mv.cut[step, i].wait_send()
    for before in leaving:
        for what in before[-2:]:
            gone(what)
    for i in range(FIRST_CROSS, NP):
        if i not in BY_Y:
            mv.yf[i, 0].wait_send()
    for v in v_at:
        v.wait_send()
    v_y.wait_send()
    for g in range(groups):
        tokens_to(g).wait_send()
    c_out.wait()
    for c in c_grad:
        c.wait()
    assert not left


def compute(rows, fused, arrays):
    any_space = pl.BlockSpec(memory_space=pl.ANY)
    vmem = pl.BlockSpec(memory_space=pltpu.VMEM)
    if fused:
        out_parts = [jax.ShapeDtypeStruct(o, F32) for o in OUTS]
    else:
        out_parts = [jax.ShapeDtypeStruct((2, 2, 2, 2, *KINDS[k]), BF) for _, _, k in PARTS]
    low = lambda n=D: pltpu.VMEM((rows, n), BF)
    wide = lambda n: pltpu.VMEM((rows // PAIR * PAD, n), BF)
    dma = lambda n: pltpu.SemaphoreType.DMA((n,))
    scratch = [
        low(), low(), low(),
        pltpu.VMEM((D, FF), BF), pltpu.VMEM((FF, D), BF),
        wide(3 * D), low(), low(), low(),
        wide(3 * D), low(), low(), low(),
        low(FF), low(FF),
        pltpu.VMEM((rows, D), F32), low(), wide(D),
        pltpu.VMEM((2 * PAD, PAD), F32),
        pltpu.VMEM((rows // PAIR * PAD, 128), F32),
        pltpu.VMEM((2, 2, 2, 2, 2, BLK, 1024), BF), pltpu.VMEM((2, 2, 2, 2, 2, 4 * BLK, TILE), BF),
        pltpu.VMEM((rows // PAIR, 1, PAD), F32), pltpu.VMEM((rows // PAIR, 1, PAD), F32),
        pltpu.VMEM((8, D), F32),
        pltpu.VMEM((D // 128, rows, 128), F32),
        dma(9), dma(NP),
    ]
    params = dict(vmem_limit_bytes=int(63.9 * 2**20))
    if fused:
        for lead in ((2, 2, 2), (2, 2), (2,), ()):
            scratch += [pltpu.VMEM((COUNT[k], *lead, *KINDS[k]), BF) for k in range(3)]
        scratch += [pltpu.VMEM((2, *KINDS[k]), F32) for k in range(3)]
        cross = NP - FIRST_CROSS
        scratch += [
            pltpu.VMEM((max(len(BY_Y), 1), 2, 2, 2, BLK, HALF), BF), low(), pltpu.VMEM((10, NV, D), F32),
            pltpu.VMEM((max(cross - len(BY_Y), 1), 2, BLK, D), BF),
            *([dma(NP)] * 8), *([dma(cross)] * 4), dma(2 * rows // GR + 5), dma(2 * rows // GR + 5),
        ]
        params.update(collective_id=0, has_side_effects=True)
    return pl.pallas_call(
        partial(body, fused),
        out_shape=[
            jax.ShapeDtypeStruct((rows, D), BF),
            jax.ShapeDtypeStruct((rows, D), F32),
            jax.ShapeDtypeStruct((8, 128) if fused else (rows, D), F32),
            jax.ShapeDtypeStruct((NV, D), F32),
            *out_parts,
        ],
        in_specs=[any_space] * 9 + [vmem] * (1 + NS),
        out_specs=[any_space] * 3 + [vmem] + [any_space] * len(out_parts),
        scratch_shapes=scratch,
        compiler_params=pltpu.CompilerParams(**params),
    )(*arrays)


VECTORS = (CQB, CVB, COUTB, CGAIN, CSHIFT, SQB, SVB, SOUTB, SGAIN, SSHIFT, FOUTB, FGAIN, FSHIFT)


def finish_body(n, *refs):
    vec, refs = refs[0], refs[1:]
    count = (len(refs) - len(VECTORS) - 2) // 3
    given, refs = refs[:count], refs[count:]
    vectors, finb, refs = refs[: len(VECTORS)], refs[len(VECTORS)], refs[len(VECTORS) + 1 :]
    out, sems, held = refs[:count], refs[count], refs[count + 1 :]
    into = [pltpu.make_async_copy(a, b, sems.at[i]) for i, (a, b) in enumerate(zip(given, held))]
    away = [pltpu.make_async_copy(a, b, sems.at[i]) for i, (a, b) in enumerate(zip(held, out))]
    for c in into:
        c.start()
    me = lax.axis_index("dp")
    share = D // n
    mine = pltpu.roll(vec[...], lax.rem(D - me * share, D), 1)
    for r, v in zip(VECTORS, vectors):
        v[...] = mine[r : r + 1, 0:share].reshape(v.shape)
    share = FF // n
    a_row = D // share
    v = vec[FINB : FINB + 8, :]
    at = lax.broadcasted_iota(jnp.int32, v.shape, 0) == lax.div(me, a_row)
    line = jnp.broadcast_to(jnp.sum(jnp.where(at, v, 0.0), axis=0, keepdims=True), v.shape)
    finb[...] = pltpu.roll(line, lax.rem(D - lax.rem(me, a_row) * share, D), 1)[0:1, 0:share]
    for a, b in zip(into, away):
        a.wait()
        b.start()
    for b in away:
        b.wait()


def finish(n, vec, arrays):
    any_space = pl.BlockSpec(memory_space=pl.ANY)
    vmem = pl.BlockSpec(memory_space=pltpu.VMEM)
    share = D // n
    shapes = [(share,)] * 5 + [(1, share)] * 8 + [(1, FF // n)]
    return pl.pallas_call(
        partial(finish_body, n),
        out_shape=[
            *(jax.ShapeDtypeStruct(s, F32) for s in shapes),
            *(jax.ShapeDtypeStruct(x.shape, x.dtype) for x in arrays),
        ],
        in_specs=[vmem] + [any_space] * len(arrays),
        out_specs=[vmem] * len(shapes) + [any_space] * len(arrays),
        scratch_shapes=[
            pltpu.SemaphoreType.DMA((max(len(arrays), 1),)),
            *(pltpu.VMEM(x.shape, x.dtype) for x in arrays),
        ],
        compiler_params=pltpu.CompilerParams(vmem_limit_bytes=int(63.9 * 2**20)),
    )(vec, *arrays)


def partner(block):
    return lax.ppermute(block, "stream", [(0, 1), (1, 0)])


def reduce_parts(parts, vec):
    def natural(some):
        done = []
        for p in some:
            r, n = p.shape[-2:]
            done.append(p.transpose(1, 2, 3, 0, 4, 5).reshape(16 * r, n))
        return jnp.concatenate(done, axis=1)

    def scatter(some, shared=False):
        x = natural(some)
        if shared:
            x = lax.psum(x, "stream")
        return lax.psum_scatter(x, "dp", scatter_dimension=0, tiled=True).astype(F32)

    sums = [
        scatter(parts[0:3]), scatter(parts[3:6]), scatter(parts[6:7]), scatter(parts[7:10]),
        scatter(parts[10:11], True), scatter(parts[11:14], True),
    ]
    own = lax.psum(vec[:CGAIN], "dp")
    return sums, jnp.concatenate([own, lax.psum(vec[CGAIN:], ("stream", "dp"))])


def local(*args):
    a = dict(zip(NAMES, args))
    n = lax.axis_size("dp")
    fused = n == 16
    shape = a["tokens"].shape
    items = shape[1]

    def to_slots(v):
        return v[0].transpose(1, 0, 2).reshape(items * LR, D)

    def back_to_items(v):
        return v.reshape(LR, items, D).transpose(1, 0, 2).reshape(shape)

    tok, cot = to_slots(a["tokens"]), to_slots(a["cotangent"])
    far = tok if fused else partner(tok)
    outs = compute(
        items * LR,
        fused,
        [tok, far, cot, a["cross_qkv"], a["cross_out"], a["self_qkv"][0], a["self_out"][0],
         a["ffn_in"][0], a["ffn_out"][0], a["region_mask"], *(a[k] for k in SMALL)],
    )
    stream, grad, back, vec = outs[:4]
    sums = outs[4:]
    if not fused:
        grad = grad + partner(back.astype(BF)).astype(F32)
        sums, vec = reduce_parts(sums, vec)
    done = finish(n, vec, [stream, grad, *sums] if fused else [])
    if fused:
        stream, grad, *sums = done[14:]
    fout, fin, sout, sqkv, cout, cqkv = sums
    cqb, cvb, coutb, cgain, cshift, sqb, svb, soutb, sgain, sshift, foutb, fgain, fshift, finb = done[:14]
    return (
        back_to_items(stream), back_to_items(grad),
        cqkv, cqb, cvb, cout, coutb, cgain, cshift,
        sqkv[None], sqb, svb, sout[None], soutb, sgain, sshift,
        fin[None], finb, fout[None], foutb, fgain, fshift,
    )


def solution(mesh):
    both = P("stream", "dp")
    one = P("stream")
    specs = {n: one for n in NAMES}
    specs.update({n: P() for n in NAMES if n.startswith("cross")})
    specs.update(tokens=both, cotangent=both, region_mask=P("dp"))
    return jax.shard_map(
        local,
        mesh=mesh,
        in_specs=tuple(specs[n] for n in NAMES),
        out_specs=(both, both) + (P("dp"),) * 7 + (both,) * 13,
        check_vma=False,
    )
```

```python
from functools import partial
from types import SimpleNamespace

import jax
import jax.numpy as jnp
from jax import lax
from jax.experimental import pallas as pl
from jax.experimental.pallas import tpu as pltpu
from jax.sharding import PartitionSpec as P

D = 768
H = 12
HD = 64
FF = 3072
LW = 20
LR = 36
BF = jnp.bfloat16
F32 = jnp.float32
GROUP = 4
GR = GROUP * LR
PAIR = 2 * LR
PAD = 80
TILE = 256
BLK = 48
NH = 2
LNB = 144
FGAIN, FSHIFT, FOUTB, SGAIN, SSHIFT, SOUTB, SQB, SVB, FINB = 0, 1, 2, 3, 4, 5, 6, 7, 8
CGAIN, CSHIFT, COUTB, CQB, CVB = 12, 13, 14, 15, 16
NV = 24


def nn(a, b):
    return lax.dot_general(a, b, (((1,), (0,)), ((), ())), preferred_element_type=F32)


def nt(a, b):
    return lax.dot_general(a, b, (((1,), (1,)), ((), ())), preferred_element_type=F32)


def tn(a, b):
    return lax.dot_general(a, b, (((0,), (0,)), ((), ())), preferred_element_type=F32)


def tile_at(i, size=TILE):
    return pl.ds(pl.multiple_of(i * size, size), size)


def total(x):
    return jnp.sum(x.astype(F32), axis=0, keepdims=True)


def norm_forward(res, gain, shift, hat, columns, col, y_low, first, count):
    @pl.loop(0, count // LNB)
    def _(i):
        at = pl.ds(pl.multiple_of(first + i * LNB, 16), LNB)
        r = res[at, :]
        centre = r - jnp.mean(r, axis=-1, keepdims=True)
        rs = lax.rsqrt(jnp.mean(centre * centre, axis=-1, keepdims=True) + 1e-12)
        xh = centre * rs
        y = xh * gain[...] + shift[...]
        hat[at, :] = xh.astype(BF)
        columns[at, col : col + 1] = rs
        res[at, :] = y
        y_low[at, :] = y.astype(BF)


def norm_grad(dy, xh, rs, gain):
    dx = dy * gain
    return rs * (
        dx - jnp.mean(dx, axis=-1, keepdims=True) - xh * jnp.mean(dx * xh, axis=-1, keepdims=True)
    )


def norm_backward(res, gain, hat, columns, col, g_low, vec, at_gain, at_shift, at_bias):
    rows = res.shape[0]

    @pl.loop(0, rows // LNB)
    def _(i):
        at = tile_at(i, LNB)
        dy = res[at, :]
        xh = hat[at, :].astype(F32)
        g = norm_grad(dy, xh, columns[at, col : col + 1], gain[...])
        low = g.astype(BF)
        res[at, :] = g
        g_low[at, :] = low
        vec[at_gain : at_gain + 1, :] += total(dy * xh)
        vec[at_shift : at_shift + 1, :] += total(dy)
        vec[at_bias : at_bias + 1, :] += total(low)


def head_masks():
    lane = lax.broadcasted_iota(jnp.int32, (1, 128), 1)
    first = (lane < HD).astype(BF)
    return first, (1 - first).astype(BF)


def stack_heads(x, masks):
    return jnp.concatenate([x * masks[0], x * masks[1]], axis=0)


def pick_heads(x):
    lane = lax.broadcasted_iota(jnp.int32, (PAIR, 128), 1)
    return jnp.where(lane < HD, x[:PAIR], x[PAD : PAD + PAIR])


def store_pairs(dst, x, at, first=0):
    zeros = jnp.zeros((PAD - PAIR, x.shape[1]), F32)
    for p in range(x.shape[0] // PAIR):
        block = jnp.concatenate([x[p * PAIR : (p + 1) * PAIR], zeros], axis=0)
        dst[pl.ds(pl.multiple_of((first + p) * PAD, 16), PAD), at] = block.astype(BF)


def probabilities(q2, k, rid, kid):
    s = nt(q2, k) * (1.0 / HD**0.5)
    s = jnp.where(rid == kid, s, -1000000000.0)
    e = jnp.exp(s - jnp.max(s, axis=-1, keepdims=True))
    return e * (1.0 / jnp.sum(e, axis=-1, keepdims=True))


def attention_forward(g, qkv, rid, kids, out):
    masks = head_masks()
    group = pl.ds(pl.multiple_of(g * GR, GR), GR)
    for p in range(H // 2):
        done = []
        for half in range(2):
            rows = pl.ds(pl.multiple_of((2 * g + half) * PAD, 16), PAD)
            q2 = stack_heads(qkv[rows, p * 128 : p * 128 + 128], masks)
            prob = probabilities(q2, qkv[rows, D + p * 128 : D + p * 128 + 128], rid[...], kids[2 * g + half])
            done.append(pick_heads(nn(prob.astype(BF), qkv[rows, 2 * D + p * 128 : 2 * D + p * 128 + 128])))
        out[group, p * 128 : p * 128 + 128] = jnp.concatenate(done, axis=0).astype(BF)


def attention_backward(g, qkv, grad_out, columns, col, out):
    masks = head_masks()
    group = pl.ds(pl.multiple_of(g * GR, GR), GR)
    query = lax.broadcasted_iota(jnp.int32, (1, 2 * PAD), 1)
    second = ((query >= LR) & (query < PAD)) | (query >= PAD + LR)
    query_item = second.astype(F32)
    for p in range(H // 2):
        done = [[], [], []]
        for half in range(2):
            rows = pl.ds(pl.multiple_of((2 * g + half) * PAD, 16), PAD)
            q2 = stack_heads(qkv[rows, p * 128 : p * 128 + 128], masks)
            k = qkv[rows, D + p * 128 : D + p * 128 + 128]
            v = qkv[rows, 2 * D + p * 128 : 2 * D + p * 128 + 128]
            g2 = stack_heads(grad_out[rows, p * 128 : p * 128 + 128], masks)
            s = nt(k, q2) * (1.0 / HD**0.5)
            s = jnp.where(columns[rows, col : col + 1] == query_item, s, -1000000000.0)
            e = jnp.exp(s - jnp.max(s, axis=0, keepdims=True))
            prob = e * (1.0 / jnp.sum(e, axis=0, keepdims=True))
            gp = nt(v, g2)
            gv = nn(prob.astype(BF), g2)
            s = prob * (gp - jnp.sum(gp * prob, axis=0, keepdims=True))
            s = s.astype(BF)
            done[0].append(pick_heads(tn(s, k)) * (1.0 / HD**0.5))
            done[1].append(nn(s, q2)[:PAIR] * (1.0 / HD**0.5))
            done[2].append(gv[:PAIR])
        for part in range(3):
            at = part * D + p * 128
            out[group, at : at + 128] = jnp.concatenate(done[part], axis=0).astype(BF)


def by_item(wide, dst, g):
    items = wide.shape[1] // LR
    for j in range(D // 128):
        got = [wide[j, pl.ds(g * GROUP + i, LR, stride=items), :] for i in range(GROUP)]
        dst[g * GR : (g + 1) * GR, j * 128 : (j + 1) * 128] = jnp.concatenate(got, axis=0).astype(BF)


def by_slot(value, wide, j):
    items = value.shape[0] // LR
    for i in range(items):
        wide[j, pl.ds(i, LR, stride=items), :] = value[i * LR : (i + 1) * LR]


def widen(src, wide):
    @pl.loop(0, src.shape[0] // BLK)
    def _(i):
        at = tile_at(i, BLK)
        for j in range(D // 128):
            wide[j, at, :] = src[at, j * 128 : (j + 1) * 128].astype(F32)


NAMES = (
    "tokens", "region_mask", "cotangent", "cross_qkv", "cross_q_bias", "cross_v_bias",
    "cross_out", "cross_out_bias", "cross_gain", "cross_shift", "self_qkv", "self_q_bias",
    "self_v_bias", "self_out", "self_out_bias", "self_gain", "self_shift", "ffn_in",
    "ffn_in_bias", "ffn_out", "ffn_out_bias", "ffn_gain", "ffn_shift",
)
SMALL = tuple(n for n in NAMES if n.endswith(("bias", "gain", "shift")))
NS = len(SMALL)
KINDS = ((4 * BLK, TILE), (BLK, 1024), (BLK, D))
PARTS = (
    *((0, TILE * i, 0) for i in range(3)),
    *((1, 1024 * i, 1) for i in range(3)),
    (2, 0, 2),
    *((3, D * i, 2) for i in range(3)),
    (4, 0, 2),
    *((5, D * i, 2) for i in range(3)),
)
NP = len(PARTS)
FIRST_CROSS = 10
OUTS = ((4 * BLK, D), (BLK, FF), (BLK, D), (BLK, 3 * D), (BLK, D), (BLK, 3 * D))
HALF = D // 2
IN_KIND = [sum(p[2] == PARTS[i][2] for p in PARTS[:i]) for i in range(NP)]
COUNT = [sum(p[2] == k for p in PARTS) for k in range(3)]


BY_Y = (10, 12,)
ORDER = (
    (2, 1, 0),
    (1, 2, 0),
    (2, 1, 0),
    (1, 0, 2),
    (2, 1, 0),
    (2, 1, 0),
    (2, 1, 0),
    (2, 1, 0),
    (2, 1, 0),
    (2, 1, 0),
    (2, 1, 0),
    (2, 1, 0),
    (2, 1, 0),
    (2, 1, 0),
)
SERVE = {
    -3: (100,),
    20: (101,),
    21: (102,),
    -6: (103,),
    5: (200,),
    30: (104, 201,),
    31: (105,),
    6: (202,),
    40: (106, 203,),
    42: (300, 204,),
    43: (302,),
    7: (301,),
    -10: (107,),
    33: (108, 303,),
    34: (109, 205, 400,),
    50: (304, 110, 206,),
    51: (402, 401,),
    52: (207, 305,),
    11: (404,),
    12: (306, 208,),
    -14: (111,),
    36: (510, 403, 307, 112,),
    60: (113, 405, 209, 406, 308, 407,),
    61: (211, 309, 210, 408, 311, 512, 213,),
    62: (409, 310, 411, 212, 313, 611,),
    63: (410, 312, 413, 610, 412, 613, 612,),
}


def body(fused, *refs):
    refs = list(refs)

    def take(n):
        got = refs[:n]
        del refs[:n]
        return got

    tok_h, far_h, cot_h, cqkv_h, cout_h, sqkv_h, sout_h, fin_h, fout_h = take(9)
    (mask_in,) = take(1)
    given = dict(zip(SMALL, take(NS)))
    out_o, grad_o, back_o, vec_o = take(4)
    parts_o = take(len(OUTS) if fused else NP)
    (tok, far, cot, wp, wq, xqkv, xatt, joined, hat1, sqkv, satt, settled, hat2, active, inner,
     res, g_low, gpad, rid, columns, slot_a, slot_b, kid_own, kid_far, sv,
     out_f, sems, part_sems) = take(28)
    rows = tok.shape[0]
    groups = rows // GR
    gx = active
    side = lax.axis_index("stream")

    def fetch(i, src, dst):
        c = pltpu.make_async_copy(src, dst, sems.at[i])
        c.start()
        return c

    if fused:
        acc, xr, za, zb, fin = take(3), take(3), take(3), take(3), take(3)
        yr, back, vbuf, ybf = take(4)
        s_core, r_core, s_x, r_x, s_za, r_za, s_zb, r_zb, s_y, r_y, s_yf, r_yf, s_m, r_m = take(14)
        me = lax.axis_index("dp")
        core, x = lax.rem(me, 2), lax.rem(lax.div(me, 2), 2)
        zl, zh = lax.rem(lax.div(me, 4), 2), lax.div(me, 8)
        to_y, to_core = (1 - side, me), (side, me + 1 - 2 * core)
        to_x, to_zl, to_zh = (side, me + 2 - 4 * x), (side, me + 4 - 8 * zl), (side, me + 8 - 16 * zh)
        peers = (to_y, to_core, to_x, to_zl, to_zh)
        barrier = pltpu.get_barrier_semaphore()
        for p in peers:
            pl.semaphore_signal(barrier, inc=1, device_id=p, device_id_type=pl.DeviceIdType.MESH)

        def remote(src, dst, send, recv, peer):
            return pltpu.make_async_remote_copy(
                src_ref=src, dst_ref=dst, send_sem=send, recv_sem=recv,
                device_id=peer, device_id_type=pl.DeviceIdType.MESH,
            )

    c_tok = fetch(0, tok_h, g_low)
    def fetch_self():
        return [
            *(fetch(4 + j, sqkv_h.at[:, j * D : (j + 1) * D], wq.at[j * D : (j + 1) * D, :]) for j in range(3)),
            fetch(7, sout_h, wq.at[3 * D :, :]),
        ]

    c_tok.wait()
    c_cqkv = fetch(1, cqkv_h, wp.at[:, 0 : 3 * D])
    c_cot = fetch(8, cot_h, settled)
    c_cout = fetch(3, cout_h, wp.at[:, 3 * D :])
    if not fused:
        c_far = fetch(2, far_h, satt)

    c_self = fetch_self()
    widen(g_low, out_f)
    if fused:
        pl.semaphore_wait(barrier, len(peers))

        def tokens_to(g):
            at = pl.ds(pl.multiple_of(g * GR, GR), GR)
            return remote(tok.at[at, :], far.at[at, :], s_m.at[g], r_m.at[g], to_y)

    for g in range(groups):
        by_item(out_f, tok, g)
        if fused:
            tokens_to(g).start()

    sm = SimpleNamespace()
    for i, n in enumerate(SMALL):
        row_of = given[n]
        if len(given[n].shape) == 1:
            sv[i : i + 1, :] = given[n][...].reshape(1, D)
            row_of = sv.at[i : i + 1, :]
        setattr(sm, n, row_of)
    vec = vbuf.at[0] if fused else vec_o
    vec[...] = jnp.zeros(vec.shape, F32)
    edge = lax.broadcasted_iota(jnp.int32, (2 * PAD, PAD), 0)
    second = ((edge >= LR) & (edge < PAD)) | (edge >= PAD + LR)
    rid[...] = second.astype(F32)
    items = rows // LR
    present = (mask_in[...] > 0).astype(F32)
    word = (lax.broadcasted_iota(jnp.int32, (items, LR), 1) < LW).astype(F32)
    slot = lax.broadcasted_iota(jnp.int32, (LR, GR), 0)
    lane = lax.broadcasted_iota(jnp.int32, (1, GR), 1)
    lane_item = sum((lane >= LR * i).astype(jnp.int32) for i in range(1, GROUP))
    spread_slots = (slot == lane - LR * lane_item).astype(BF)
    row = lax.broadcasted_iota(jnp.int32, (GR, GR), 0)
    diagonal = row == lax.broadcasted_iota(jnp.int32, (GR, GR), 1)

    def lay_masks(mask, kid, col, own):
        spread = nn(mask.astype(BF), spread_slots)
        for g in range(groups):
            line = jnp.zeros((1, GR), F32)
            for i in range(GROUP):
                line += jnp.where(lane_item == i, spread[g * GROUP + i : g * GROUP + i + 1, :], 0.0)
            ids = jnp.where(line > 0.5, (lane_item % 2).astype(F32), -1.0)
            for half in range(2):
                kid[2 * g + half, :, 0:PAIR] = ids[:, half * PAIR : (half + 1) * PAIR]
                kid[2 * g + half, :, PAIR:] = jnp.full((1, PAD - PAIR), -1.0, F32)
            if own:
                column = jnp.sum(jnp.where(diagonal, line, 0.0), axis=-1, keepdims=True)
                columns[g * GR : (g + 1) * GR, 0:1] = column
            column = jnp.sum(jnp.where(diagonal, ids, 0.0), axis=-1, keepdims=True)
            none = jnp.full((PAD - PAIR, 1), -1.0, F32)
            for half in range(2):
                padded = jnp.concatenate([column[half * PAIR : (half + 1) * PAIR], none], axis=0)
                columns[(2 * g + half) * PAD : (2 * g + half + 1) * PAD, col : col + 1] = padded

    lay_masks(jnp.where(side == 0, word, present), kid_own, 3, True)
    lay_masks(jnp.where(side == 0, present, word), kid_far, 4, False)

    c_cqkv.wait()

    @pl.loop(0, 3)
    def _(j):
        at = tile_at(j)
        store_pairs(xqkv, nn(tok[...], wp[:, at]) + sm.cross_q_bias[:, at], at)

    c_cot.wait()
    widen(settled, out_f)
    for g in range(groups):
        by_item(out_f, cot, g)
    if not fused:
        c_far.wait()
        widen(satt, out_f)
        for g in range(groups):
            by_item(out_f, far, g)

    c_cout.wait()
    for c in c_self:
        c.wait()
    part_rows, part_groups = rows // NH, groups // NH

    @pl.loop(0, NH)
    def _(h):
        first = h * part_rows
        at_h = pl.ds(pl.multiple_of(first, 16), part_rows)

        @pl.loop(h * part_groups, (h + 1) * part_groups)
        def _(g):
            at_g = pl.ds(pl.multiple_of(g * GR, GR), GR)
            if fused:
                tokens_to(g).wait_recv()
            far_g = far[at_g, :]
            for j in range(3, 9):
                y = nn(far_g, wp[:, j * TILE : (j + 1) * TILE])
                if j >= 6:
                    y = y + sm.cross_v_bias[:, (j - 6) * TILE : (j - 5) * TILE]
                store_pairs(xqkv, y, slice(j * TILE, (j + 1) * TILE), 2 * g)
            attention_forward(g, xqkv, rid, kid_far, xatt)

        res[at_h, :] = tok[at_h, :].astype(F32) + nn(xatt[at_h, :], wp[:, 3 * D :]) + sm.cross_out_bias[...]

        @pl.when(h == NH - 1)
        def _():
            fetch(1, fin_h, wp)

        norm_forward(res, sm.cross_gain, sm.cross_shift, hat1, columns, 1, joined, first, part_rows)
        for part in range(3):
            y = nn(joined[at_h, :], wq[part * D : (part + 1) * D, :])
            if part == 0:
                y = y + sm.self_q_bias[...]
            if part == 2:
                y = y + sm.self_v_bias[...]
            store_pairs(sqkv, y, slice(part * D, (part + 1) * D), 2 * part_groups * h)

        for q in range(part_groups):
            attention_forward(h * part_groups + q, sqkv, rid, kid_own, satt)

        res[at_h, :] += nn(satt[at_h, :], wq[3 * D :, :]) + sm.self_out_bias[...]

        @pl.when(h == NH - 1)
        def _():
            fetch(3, fout_h, wq)

        norm_forward(res, sm.self_gain, sm.self_shift, hat2, columns, 2, settled, first, part_rows)

    pltpu.make_async_copy(fin_h, wp, sems.at[1]).wait()

    @pl.loop(0, FF // TILE)
    def _(j):
        at = tile_at(j)
        x = nn(settled[...], wp[:, at]) + sm.ffn_in_bias[:, at]
        half = 0.5 * (1.0 + lax.erf(x * (0.5**0.5)))
        active[:, at] = (x * half).astype(BF)
        inner[:, at] = x.astype(BF)

    pltpu.make_async_copy(fout_h, wq, sems.at[3]).wait()

    for j in range(3):
        at = slice(j * TILE, (j + 1) * TILE)
        res[:, at] += nn(active[...], wq[:, at]) + sm.ffn_out_bias[:, at]

    @pl.loop(0, rows // LNB)
    def _(i):
        at = tile_at(i, LNB)
        r = res[at, :]
        ok = columns[at, 0:1]
        gain = sm.ffn_gain[...]
        centre = r - jnp.mean(r, axis=-1, keepdims=True)
        rs = lax.rsqrt(jnp.mean(centre * centre, axis=-1, keepdims=True) + 1e-12)
        xh = centre * rs
        y = xh * gain + sm.ffn_shift[...]
        for j in range(D // 128):
            out_f[j, at, :] = y[:, j * 128 : (j + 1) * 128] * ok
        dy = cot[at, :].astype(F32) * ok
        g = norm_grad(dy, xh, rs, gain)
        low = g.astype(BF)
        res[at, :] = g
        cot[at, :] = low
        vec[FGAIN : FGAIN + 1, :] += total(dy * xh)
        vec[FSHIFT : FSHIFT + 1, :] += total(dy)
        vec[FOUTB : FOUTB + 1, :] += total(low)

    def slot_of(i):
        kind = PARTS[i][2]
        if kind == 0:
            return slot_b.at[i % 2]
        ref = slot_a.at[i % 2]
        return ref if kind == 1 else ref.at[:, :, :, :, :, 0:D]

    mv = SimpleNamespace(core={}, y={}, cut={}, yf={}, out={}, acc={}, got={}, fin={})
    if fused:
        here = (zh, zl, x)

        def late(i):
            return [j for j in range(FIRST_CROSS, NP) if j not in BY_Y].index(i)

        over = (to_zh, to_zl, to_x)

        def cut(ref, places, *after):
            return ref.at[(*(places.get(d, slice(None)) for d in range(3)), *after)]

        for i in range(NP):
            out, col, kind = PARTS[i]
            n, width = IN_KIND[i], KINDS[kind][1]
            a = acc[kind].at[n]
            mv.core[i] = remote(slot_of(i).at[1 - core], a, s_core.at[i], r_core.at[i], to_core)
            got = [xr[kind].at[n], za[kind].at[n], zb[kind].at[n]]
            c = i - FIRST_CROSS
            if i in BY_Y:
                mine = pl.ds(pl.multiple_of(side * HALF, HALF), HALF)
                other = pl.ds(pl.multiple_of((1 - side) * HALF, HALF), HALF)
                mv.y[i] = remote(a.at[:, :, :, :, other], yr.at[BY_Y.index(i)], s_y.at[c], r_y.at[c], to_y)
                a = a.at[:, :, :, :, mine]
                short = pl.ds(0, HALF)
                got = [got[0].at[:, :, :, short], got[1].at[:, :, short], got[2].at[:, short]]
                width = HALF
            mv.acc[i], mv.got[i] = a, got
            places = {}
            sems_of = ((s_x, r_x), (s_za, r_za), (s_zb, r_zb))
            for step, d in enumerate(ORDER[i]):
                send, recv = sems_of[step]
                src = cut(a, {**places, d: 1 - here[d]})
                mv.cut[step, i] = remote(src, got[step], send.at[i], recv.at[i], over[d])
                places[d] = here[d]
            if i in BY_Y:
                col0 = pl.ds(pl.multiple_of(col + side * HALF, HALF), HALF)
            else:
                col0 = pl.ds(col, width)
            for place in range(2):
                f = fin[kind].at[place]
                if i in BY_Y:
                    f = f.at[:, 0:HALF]
                    mv.yf[i, place] = remote(f, parts_o[out].at[:, col0], s_yf.at[c], r_yf.at[c], to_y)
                mv.fin[i, place] = f
                mv.out[i, place] = pltpu.make_async_copy(f, parts_o[out].at[:, col0], part_sems.at[i])
            if i >= FIRST_CROSS and i not in BY_Y:
                mv.yf[i, 0] = remote(ybf.at[late(i), 0], ybf.at[late(i), 1], s_yf.at[c], r_yf.at[c], to_y)
        leaving = ([], [], [])


        def leave(i, value):
            before = leaving[PARTS[i][2]]
            place = len(before) % 2
            if len(before) > 1:
                gone(before[-2])
            before.append((i, place))
            mv.fin[i, place][...] = value
            mv.out[i, place].start()
            if i in BY_Y:
                mv.yf[i, place].start()

        def gone(what):
            mv.out[what].wait()
            if what[0] in BY_Y:
                mv.yf[what].wait_send()

        def t1(i):
            mv.core[i].wait_recv()
            out, col, kind = PARTS[i]
            a, own = acc[kind].at[IN_KIND[i]], slot_of(i)

            @pl.loop(0, 8)
            def _(d):
                p, q, r = lax.div(d, 4), lax.rem(lax.div(d, 2), 2), lax.rem(d, 2)
                a[p, q, r] = a[p, q, r] + own[core, p, q, r]

            (mv.y[i] if i in BY_Y else mv.cut[0, i]).start()

        def ty(i):
            mv.y[i].wait_recv()
            a, c = mv.acc[i], BY_Y.index(i)

            @pl.loop(0, 8)
            def _(d):
                p, q, r = lax.div(d, 4), lax.rem(lax.div(d, 2), 2), lax.rem(d, 2)
                a[p, q, r] = a[p, q, r] + yr[c, p, q, r]

            mv.cut[0, i].start()

        def t2(i):
            mv.cut[0, i].wait_recv()
            a, r = mv.acc[i], mv.got[i][0]
            first = ORDER[i][0]

            @pl.loop(0, 4)
            def _(d):
                p, q = lax.div(d, 2), lax.rem(d, 2)
                at = [p, q]
                at.insert(first, here[first])
                at = tuple(at)
                a[at] = a[at] + r[p, q]

            mv.cut[1, i].start()

        def t3(i):
            mv.cut[1, i].wait_recv()
            a, r = mv.acc[i], mv.got[i][1]
            for p in range(2):
                at = list(here)
                at[ORDER[i][2]] = p
                at = tuple(at)
                a[at] = a[at] + r[p]
            mv.cut[2, i].start()

        def t4(i):
            mv.cut[2, i].wait_recv()
            whole = mv.acc[i][zh, zl, x].astype(F32) + mv.got[i][2][...].astype(F32)
            if i >= FIRST_CROSS and i not in BY_Y:
                ybf[late(i), 0] = whole.astype(BF)
                mv.yf[i, 0].start()
            else:
                leave(i, whole)

        def tf(i):
            mv.yf[i, 0].wait_recv()
            if i not in BY_Y:
                leave(i, ybf[late(i), 0].astype(F32) + ybf[late(i), 1].astype(F32))

        steps = (t1, t2, t3, t4, ty, tf)
    left = []
    for i in range(NP):
        left += [n * 100 + i for n in (1, 2, 3, 4) + (5,) * (i in BY_Y) + (6,) * (i >= FIRST_CROSS)]
    core_free = {}

    def serve(place):
        if fused:
            for t in SERVE.get(place, ()):
                left.remove(t)
                steps[t // 100 - 1](t % 100)

    def free_slot(i):
        if i in core_free:
            core_free.pop(i)()

    def push(i):
        if fused:
            mv.core[i].start()
            core_free[i] = mv.core[i].wait_send
        else:
            c = pltpu.make_async_copy(slot_of(i), parts_o[i], part_sems.at[i])
            c.start()
            core_free[i] = c.wait

    def same_slot(i):
        for j in range(i - 1, -1, -1):
            if (PARTS[j][2] == 0) == (PARTS[i][2] == 0) and j % 2 == i % 2:
                return j
        return None

    def weight_part(i, left, right, col0):
        serve(-1 - i)
        free_slot(same_slot(i))
        ref = slot_of(i)
        width = KINDS[PARTS[i][2]][1]

        @pl.loop(0, width // TILE)
        def _(j):
            src = right[:, pl.ds(pl.multiple_of(col0 + j * TILE, TILE), TILE)]
            w = tn(left[...], src).astype(BF)
            for d in range(16):
                ref[d % 2, d // 8, (d // 4) % 2, (d // 2) % 2, :, tile_at(j)] = w[d * BLK : (d + 1) * BLK, :]

        push(i)
        serve(i)

    for col in range(3):
        serve(-1 - col)
        free_slot(same_slot(col))
        ref = slot_of(col)

        @pl.loop(0, 4)
        def _(t):
            w = tn(active[:, tile_at(t, D)], cot[:, col * TILE : (col + 1) * TILE]).astype(BF)
            for d in range(4):
                ref[d % 2, lax.div(t, 2), lax.rem(t, 2), d // 2, :, :] = w[d * 4 * BLK : (d + 1) * 4 * BLK, :]

        push(col)
        serve(col)

    for r in range(3):
        @pl.loop(4 * r, 4 * r + 4)
        def _(j):
            at = tile_at(j)
            ga = nt(cot[...], wq[at, :])
            y = inner[:, at].astype(F32)
            slope = 0.5 * (1.0 + lax.erf(y * (0.5**0.5))) + y * jnp.exp(-0.5 * y * y) * 0.3989422804014327
            gi = (ga * slope).astype(BF)
            inner[:, at] = gi

        serve(20 + r)
    for r in range(4):
        vec[FINB + r : FINB + r + 1, :] = total(inner[:, r * D : (r + 1) * D])
    c_self = fetch_self()

    for col in range(3):
        weight_part(3 + col, settled, inner, col * 1024)

    @pl.loop(0, 3)
    def _(j):
        at = tile_at(j)
        res[:, at] += nt(inner[...], wp[at, :])

    serve(30)
    c_cqkv = fetch(1, cqkv_h, wp.at[:, 0 : 3 * D])
    c_cout = fetch(3, cout_h, wp.at[:, 3 * D :])
    norm_backward(res, sm.self_gain, hat2, columns, 2, g_low, vec, SGAIN, SSHIFT, SOUTB)
    serve(31)
    weight_part(6, satt, g_low, 0)
    for j in range(D // 128):
        by_slot(out_f[j], out_f, j)
        satt[:, j * 128 : (j + 1) * 128] = out_f[j].astype(BF)
    c_out = fetch(8, satt, out_o)
    for c in c_self:
        c.wait()

    @pl.loop(0, 3)
    def _(j):
        at = tile_at(j)
        w_at = pl.ds(pl.multiple_of(3 * D + j * TILE, TILE), TILE)
        store_pairs(gpad, nt(g_low[...], wq[w_at, :]), at)

    serve(32)

    def serve_each(place, g):
        for k in range(groups):
            if fused and SERVE.get(place + k):
                @pl.when(g == k)
                def _():
                    serve(place + k)

    @pl.loop(0, groups)
    def _(g):
        attention_backward(g, sqkv, gpad, columns, 3, gx)
        serve_each(40, g)

    for part in range(3):
        weight_part(7 + part, joined, gx, part * D)
    vec[SQB : SQB + 1, :] = total(gx[:, 0:D])
    vec[SVB : SVB + 1, :] = total(gx[:, 2 * D : 3 * D])

    @pl.loop(0, 3)
    def _(j):
        at = tile_at(j)
        g = res[:, at]
        for part in range(3):
            w_at = pl.ds(pl.multiple_of(part * D + j * TILE, TILE), TILE)
            g += nt(gx[:, part * D : (part + 1) * D], wq[w_at, :])
        res[:, at] = g

    serve(33)
    norm_backward(res, sm.cross_gain, hat1, columns, 1, g_low, vec, CGAIN, CSHIFT, COUTB)
    serve(34)
    weight_part(10, xatt, g_low, 0)
    c_cqkv.wait()
    c_cout.wait()

    @pl.loop(0, 3)
    def _(j):
        at = tile_at(j)
        store_pairs(gpad, nt(g_low[...], wp[at, 3 * D :]), at)

    serve(35)
    if fused:

        def back_to(g):
            at = pl.ds(pl.multiple_of(g * GR, GR), GR)
            return remote(g_low.at[at, :], back.at[at, :], s_m.at[groups + g], r_m.at[groups + g], to_y)

    @pl.loop(0, groups)
    def _(g):
        attention_backward(g, xqkv, gpad, columns, 4, gx)
        at = pl.ds(pl.multiple_of(g * GR, GR), GR)
        pair = gx[at, D : 3 * D]
        for j in range(3):
            w_at = slice(j * TILE, (j + 1) * TILE)
            g_low[at, w_at] = nt(pair, wp[w_at, D : 3 * D]).astype(BF)
        if fused:
            back_to(g).start()
        serve_each(50, g)

    vec[CQB : CQB + 1, :] = total(gx[:, 0:D])
    vec[CVB : CVB + 1, :] = total(gx[:, 2 * D : 3 * D])
    if fused:
        v_at = [
            remote(vbuf.at[j % 2], vbuf.at[2 + j], s_m.at[2 * groups + j], r_m.at[2 * groups + j], p)
            for j, p in enumerate((to_core, to_x, to_zl, to_zh))
        ]
        v_y = remote(vbuf.at[0], vbuf.at[6], s_m.at[2 * groups + 4], r_m.at[2 * groups + 4], to_y)

        def vec_step(j):
            v_at[j].wait_recv()
            if j > 0:
                v_at[j - 1].wait_send()
            vbuf[(j + 1) % 2] = vbuf[j % 2] + vbuf[2 + j]
            (v_at[j + 1] if j < 3 else v_y).start()

        v_at[0].start()
    weight_part(11, tok, gx, 0)
    weight_part(12, far, gx, D)
    if fused:
        vec_step(0)
    weight_part(13, far, gx, 2 * D)

    @pl.loop(0, 3)
    def _(j):
        at = tile_at(j)
        res[:, at] += nt(gx[:, 0:D], wp[at, 0:D])

    if not fused:
        for src, dst in ((g_low, back_o), (res, grad_o)):
            for j in range(D // 128):
                by_slot(src[:, j * 128 : (j + 1) * 128].astype(F32), out_f, j)
                fetch(0, out_f.at[j], dst.at[:, j * 128 : (j + 1) * 128]).wait()
        for done in core_free.values():
            done()
        c_out.wait()
        return

    serve(36)
    vec_step(1)
    serve(60)
    for g in range(groups):
        back_to(g).wait()

    c_grad = []
    for j in range(D // 128):
        cols = slice(j * 128, (j + 1) * 128)
        by_slot(res[:, cols] + back[:, cols].astype(F32), out_f, j)
        c_grad.append(pltpu.make_async_copy(out_f.at[j], grad_o.at[:, cols], sems.at[j]))
        c_grad[-1].start()
    serve(61)
    vec_step(2)
    serve(62)
    vec_step(3)
    serve(63)
    v_y.wait_recv()
    vec_o[...] = vbuf[0]
    vec_o[12:, :] = vbuf[0, 12:, :] + vbuf[6, 12:, :]
    for done in core_free.values():
        done()
    for i in range(NP):
        if i in BY_Y:
            mv.y[i].wait_send()
        for step in range(3):
            mv.cut[step, i].wait_send()
    for before in leaving:
        for what in before[-2:]:
            gone(what)
    for i in range(FIRST_CROSS, NP):
        if i not in BY_Y:
            mv.yf[i, 0].wait_send()
    v_at[3].wait_send()
    v_y.wait_send()
    for g in range(groups):
        tokens_to(g).wait_send()
    c_out.wait()
    for c in c_grad:
        c.wait()
    assert not left


def compute(rows, fused, arrays):
    any_space = pl.BlockSpec(memory_space=pl.ANY)
    vmem = pl.BlockSpec(memory_space=pltpu.VMEM)
    if fused:
        out_parts = [jax.ShapeDtypeStruct(o, F32) for o in OUTS]
    else:
        out_parts = [jax.ShapeDtypeStruct((2, 2, 2, 2, *KINDS[k]), BF) for _, _, k in PARTS]
    low = lambda n=D: pltpu.VMEM((rows, n), BF)
    wide = lambda n: pltpu.VMEM((rows // PAIR * PAD, n), BF)
    dma = lambda n: pltpu.SemaphoreType.DMA((n,))
    scratch = [
        low(), low(), low(),
        pltpu.VMEM((D, FF), BF), pltpu.VMEM((FF, D), BF),
        wide(3 * D), low(), low(), low(),
        wide(3 * D), low(), low(), low(),
        low(FF), low(FF),
        pltpu.VMEM((rows, D), F32), low(), wide(D),
        pltpu.VMEM((2 * PAD, PAD), F32),
        pltpu.VMEM((rows // PAIR * PAD, 128), F32),
        pltpu.VMEM((2, 2, 2, 2, 2, BLK, 1024), BF), pltpu.VMEM((2, 2, 2, 2, 2, 4 * BLK, TILE), BF),
        pltpu.VMEM((rows // PAIR, 1, PAD), F32), pltpu.VMEM((rows // PAIR, 1, PAD), F32),
        pltpu.VMEM((8, D), F32),
        pltpu.VMEM((D // 128, rows, 128), F32),
        dma(9), dma(NP),
    ]
    params = dict(vmem_limit_bytes=int(63.9 * 2**20))
    if fused:
        for lead in ((2, 2, 2), (2, 2), (2,), ()):
            scratch += [pltpu.VMEM((COUNT[k], *lead, *KINDS[k]), BF) for k in range(3)]
        scratch += [pltpu.VMEM((2, *KINDS[k]), F32) for k in range(3)]
        cross = NP - FIRST_CROSS
        scratch += [
            pltpu.VMEM((max(len(BY_Y), 1), 2, 2, 2, BLK, HALF), BF), low(), pltpu.VMEM((7, NV, D), F32),
            pltpu.VMEM((max(cross - len(BY_Y), 1), 2, BLK, D), BF),
            *([dma(NP)] * 8), *([dma(cross)] * 4), dma(2 * rows // GR + 5), dma(2 * rows // GR + 5),
        ]
        params.update(collective_id=0, has_side_effects=True)
    return pl.pallas_call(
        partial(body, fused),
        out_shape=[
            jax.ShapeDtypeStruct((rows, D), BF),
            jax.ShapeDtypeStruct((rows, D), F32),
            jax.ShapeDtypeStruct((8, 128) if fused else (rows, D), F32),
            jax.ShapeDtypeStruct((NV, D), F32),
            *out_parts,
        ],
        in_specs=[any_space] * 9 + [vmem] * (1 + NS),
        out_specs=[any_space] * 3 + [vmem] + [any_space] * len(out_parts),
        scratch_shapes=scratch,
        compiler_params=pltpu.CompilerParams(**params),
    )(*arrays)


VECTORS = (CQB, CVB, COUTB, CGAIN, CSHIFT, SQB, SVB, SOUTB, SGAIN, SSHIFT, FOUTB, FGAIN, FSHIFT)


def finish_body(n, *refs):
    vec, refs = refs[0], refs[1:]
    count = (len(refs) - len(VECTORS) - 2) // 3
    given, refs = refs[:count], refs[count:]
    vectors, finb, refs = refs[: len(VECTORS)], refs[len(VECTORS)], refs[len(VECTORS) + 1 :]
    out, sems, held = refs[:count], refs[count], refs[count + 1 :]
    into = [pltpu.make_async_copy(a, b, sems.at[i]) for i, (a, b) in enumerate(zip(given, held))]
    away = [pltpu.make_async_copy(a, b, sems.at[i]) for i, (a, b) in enumerate(zip(held, out))]
    for c in into:
        c.start()
    me = lax.axis_index("dp")
    share = D // n
    mine = pltpu.roll(vec[...], lax.rem(D - me * share, D), 1)
    for r, v in zip(VECTORS, vectors):
        v[...] = mine[r : r + 1, 0:share].reshape(v.shape)
    share = FF // n
    a_row = D // share
    v = vec[FINB : FINB + 8, :]
    at = lax.broadcasted_iota(jnp.int32, v.shape, 0) == lax.div(me, a_row)
    line = jnp.broadcast_to(jnp.sum(jnp.where(at, v, 0.0), axis=0, keepdims=True), v.shape)
    finb[...] = pltpu.roll(line, lax.rem(D - lax.rem(me, a_row) * share, D), 1)[0:1, 0:share]
    for a, b in zip(into, away):
        a.wait()
        b.start()
    for b in away:
        b.wait()


def finish(n, vec, arrays):
    any_space = pl.BlockSpec(memory_space=pl.ANY)
    vmem = pl.BlockSpec(memory_space=pltpu.VMEM)
    share = D // n
    shapes = [(share,)] * 5 + [(1, share)] * 8 + [(1, FF // n)]
    return pl.pallas_call(
        partial(finish_body, n),
        out_shape=[
            *(jax.ShapeDtypeStruct(s, F32) for s in shapes),
            *(jax.ShapeDtypeStruct(x.shape, x.dtype) for x in arrays),
        ],
        in_specs=[vmem] + [any_space] * len(arrays),
        out_specs=[vmem] * len(shapes) + [any_space] * len(arrays),
        scratch_shapes=[
            pltpu.SemaphoreType.DMA((max(len(arrays), 1),)),
            *(pltpu.VMEM(x.shape, x.dtype) for x in arrays),
        ],
        compiler_params=pltpu.CompilerParams(vmem_limit_bytes=int(63.9 * 2**20)),
    )(vec, *arrays)


def partner(block):
    return lax.ppermute(block, "stream", [(0, 1), (1, 0)])


def reduce_parts(parts, vec):
    def natural(some):
        done = []
        for p in some:
            r, n = p.shape[-2:]
            done.append(p.transpose(1, 2, 3, 0, 4, 5).reshape(16 * r, n))
        return jnp.concatenate(done, axis=1)

    def scatter(some, shared=False):
        x = natural(some)
        if shared:
            x = lax.psum(x, "stream")
        return lax.psum_scatter(x, "dp", scatter_dimension=0, tiled=True).astype(F32)

    sums = [
        scatter(parts[0:3]), scatter(parts[3:6]), scatter(parts[6:7]), scatter(parts[7:10]),
        scatter(parts[10:11], True), scatter(parts[11:14], True),
    ]
    own = lax.psum(vec[:CGAIN], "dp")
    return sums, jnp.concatenate([own, lax.psum(vec[CGAIN:], ("stream", "dp"))])


def local(*args):
    a = dict(zip(NAMES, args))
    n = lax.axis_size("dp")
    fused = n == 16
    shape = a["tokens"].shape
    items = shape[1]

    def to_slots(v):
        return v[0].transpose(1, 0, 2).reshape(items * LR, D)

    def back_to_items(v):
        return v.reshape(LR, items, D).transpose(1, 0, 2).reshape(shape)

    tok, cot = to_slots(a["tokens"]), to_slots(a["cotangent"])
    far = tok if fused else partner(tok)
    outs = compute(
        items * LR,
        fused,
        [tok, far, cot, a["cross_qkv"], a["cross_out"], a["self_qkv"][0], a["self_out"][0],
         a["ffn_in"][0], a["ffn_out"][0], a["region_mask"], *(a[k] for k in SMALL)],
    )
    stream, grad, back, vec = outs[:4]
    sums = outs[4:]
    if not fused:
        grad = grad + partner(back.astype(BF)).astype(F32)
        sums, vec = reduce_parts(sums, vec)
    done = finish(n, vec, [stream, grad, *sums] if fused else [])
    if fused:
        stream, grad, *sums = done[14:]
    fout, fin, sout, sqkv, cout, cqkv = sums
    cqb, cvb, coutb, cgain, cshift, sqb, svb, soutb, sgain, sshift, foutb, fgain, fshift, finb = done[:14]
    return (
        back_to_items(stream), back_to_items(grad),
        cqkv, cqb, cvb, cout, coutb, cgain, cshift,
        sqkv[None], sqb, svb, sout[None], soutb, sgain, sshift,
        fin[None], finb, fout[None], foutb, fgain, fshift,
    )


def solution(mesh):
    both = P("stream", "dp")
    one = P("stream")
    specs = {n: one for n in NAMES}
    specs.update({n: P() for n in NAMES if n.startswith("cross")})
    specs.update(tokens=both, cotangent=both, region_mask=P("dp"))
    return jax.shard_map(
        local,
        mesh=mesh,
        in_specs=tuple(specs[n] for n in NAMES),
        out_specs=(both, both) + (P("dp"),) * 7 + (both,) * 13,
        check_vma=False,
    )
```

```python
from functools import partial
from types import SimpleNamespace

import jax
import jax.numpy as jnp
from jax import lax
from jax.experimental import pallas as pl
from jax.experimental.pallas import tpu as pltpu
from jax.sharding import PartitionSpec as P

D = 768
H = 12
HD = 64
FF = 3072
LW = 20
LR = 36
BF = jnp.bfloat16
F32 = jnp.float32
GROUP = 4
GR = GROUP * LR
PAIR = 2 * LR
PAD = 80
TILE = 256
BLK = 48
NH = 2
LNB = 144
FGAIN, FSHIFT, FOUTB, SGAIN, SSHIFT, SOUTB, SQB, SVB, FINB = 0, 1, 2, 3, 4, 5, 6, 7, 8
CGAIN, CSHIFT, COUTB, CQB, CVB = 12, 13, 14, 15, 16
NV = 24


def nn(a, b):
    return lax.dot_general(a, b, (((1,), (0,)), ((), ())), preferred_element_type=F32)


def nt(a, b):
    return lax.dot_general(a, b, (((1,), (1,)), ((), ())), preferred_element_type=F32)


def tn(a, b):
    return lax.dot_general(a, b, (((0,), (0,)), ((), ())), preferred_element_type=F32)


def tile_at(i, size=TILE):
    return pl.ds(pl.multiple_of(i * size, size), size)


def total(x):
    return jnp.sum(x.astype(F32), axis=0, keepdims=True)


def norm_forward(res, gain, shift, hat, columns, col, y_low, first, count):
    @pl.loop(0, count // LNB)
    def _(i):
        at = pl.ds(pl.multiple_of(first + i * LNB, 16), LNB)
        r = res[at, :]
        centre = r - jnp.mean(r, axis=-1, keepdims=True)
        rs = lax.rsqrt(jnp.mean(centre * centre, axis=-1, keepdims=True) + 1e-12)
        xh = centre * rs
        y = xh * gain[...] + shift[...]
        hat[at, :] = xh.astype(BF)
        columns[at, col : col + 1] = rs
        res[at, :] = y
        y_low[at, :] = y.astype(BF)


def norm_grad(dy, xh, rs, gain):
    dx = dy * gain
    return rs * (
        dx - jnp.mean(dx, axis=-1, keepdims=True) - xh * jnp.mean(dx * xh, axis=-1, keepdims=True)
    )


def norm_backward(res, gain, hat, columns, col, g_low, vec, at_gain, at_shift, at_bias):
    rows = res.shape[0]

    @pl.loop(0, rows // LNB)
    def _(i):
        at = tile_at(i, LNB)
        dy = res[at, :]
        xh = hat[at, :].astype(F32)
        g = norm_grad(dy, xh, columns[at, col : col + 1], gain[...])
        low = g.astype(BF)
        res[at, :] = g
        g_low[at, :] = low
        vec[at_gain : at_gain + 1, :] += total(dy * xh)
        vec[at_shift : at_shift + 1, :] += total(dy)
        vec[at_bias : at_bias + 1, :] += total(low)


def head_masks():
    lane = lax.broadcasted_iota(jnp.int32, (1, 128), 1)
    first = (lane < HD).astype(BF)
    return first, (1 - first).astype(BF)


def stack_heads(x, masks):
    return jnp.concatenate([x * masks[0], x * masks[1]], axis=0)


def pick_heads(x):
    lane = lax.broadcasted_iota(jnp.int32, (PAIR, 128), 1)
    return jnp.where(lane < HD, x[:PAIR], x[PAD : PAD + PAIR])


def store_pairs(dst, x, at, first=0):
    zeros = jnp.zeros((PAD - PAIR, x.shape[1]), F32)
    for p in range(x.shape[0] // PAIR):
        block = jnp.concatenate([x[p * PAIR : (p + 1) * PAIR], zeros], axis=0)
        dst[pl.ds(pl.multiple_of((first + p) * PAD, 16), PAD), at] = block.astype(BF)


def probabilities(q2, k, rid, kid):
    s = nt(q2, k) * (1.0 / HD**0.5)
    s = jnp.where(rid == kid, s, -1000000000.0)
    e = jnp.exp(s - jnp.max(s, axis=-1, keepdims=True))
    return e * (1.0 / jnp.sum(e, axis=-1, keepdims=True))


def attention_forward(g, qkv, rid, kids, out):
    masks = head_masks()
    group = pl.ds(pl.multiple_of(g * GR, GR), GR)
    for p in range(H // 2):
        done = []
        for half in range(2):
            rows = pl.ds(pl.multiple_of((2 * g + half) * PAD, 16), PAD)
            q2 = stack_heads(qkv[rows, p * 128 : p * 128 + 128], masks)
            prob = probabilities(q2, qkv[rows, D + p * 128 : D + p * 128 + 128], rid[...], kids[2 * g + half])
            done.append(pick_heads(nn(prob.astype(BF), qkv[rows, 2 * D + p * 128 : 2 * D + p * 128 + 128])))
        out[group, p * 128 : p * 128 + 128] = jnp.concatenate(done, axis=0).astype(BF)


def attention_backward(g, qkv, grad_out, columns, col, out):
    masks = head_masks()
    group = pl.ds(pl.multiple_of(g * GR, GR), GR)
    query = lax.broadcasted_iota(jnp.int32, (1, 2 * PAD), 1)
    second = ((query >= LR) & (query < PAD)) | (query >= PAD + LR)
    query_item = second.astype(F32)
    for p in range(H // 2):
        done = [[], [], []]
        for half in range(2):
            rows = pl.ds(pl.multiple_of((2 * g + half) * PAD, 16), PAD)
            q2 = stack_heads(qkv[rows, p * 128 : p * 128 + 128], masks)
            k = qkv[rows, D + p * 128 : D + p * 128 + 128]
            v = qkv[rows, 2 * D + p * 128 : 2 * D + p * 128 + 128]
            g2 = stack_heads(grad_out[rows, p * 128 : p * 128 + 128], masks)
            s = nt(k, q2) * (1.0 / HD**0.5)
            s = jnp.where(columns[rows, col : col + 1] == query_item, s, -1000000000.0)
            e = jnp.exp(s - jnp.max(s, axis=0, keepdims=True))
            prob = e * (1.0 / jnp.sum(e, axis=0, keepdims=True))
            gp = nt(v, g2)
            gv = nn(prob.astype(BF), g2)
            s = prob * (gp - jnp.sum(gp * prob, axis=0, keepdims=True))
            s = s.astype(BF)
            done[0].append(pick_heads(tn(s, k)) * (1.0 / HD**0.5))
            done[1].append(nn(s, q2)[:PAIR] * (1.0 / HD**0.5))
            done[2].append(gv[:PAIR])
        for part in range(3):
            at = part * D + p * 128
            out[group, at : at + 128] = jnp.concatenate(done[part], axis=0).astype(BF)


def by_item(wide, dst, g):
    items = wide.shape[1] // LR
    for j in range(D // 128):
        got = [wide[j, pl.ds(g * GROUP + i, LR, stride=items), :] for i in range(GROUP)]
        dst[g * GR : (g + 1) * GR, j * 128 : (j + 1) * 128] = jnp.concatenate(got, axis=0).astype(BF)


def by_slot(value, wide, j):
    items = value.shape[0] // LR
    for i in range(items):
        wide[j, pl.ds(i, LR, stride=items), :] = value[i * LR : (i + 1) * LR]


def widen(src, wide):
    @pl.loop(0, src.shape[0] // BLK)
    def _(i):
        at = tile_at(i, BLK)
        for j in range(D // 128):
            wide[j, at, :] = src[at, j * 128 : (j + 1) * 128].astype(F32)


NAMES = (
    "tokens", "region_mask", "cotangent", "cross_qkv", "cross_q_bias", "cross_v_bias",
    "cross_out", "cross_out_bias", "cross_gain", "cross_shift", "self_qkv", "self_q_bias",
    "self_v_bias", "self_out", "self_out_bias", "self_gain", "self_shift", "ffn_in",
    "ffn_in_bias", "ffn_out", "ffn_out_bias", "ffn_gain", "ffn_shift",
)
SMALL = tuple(n for n in NAMES if n.endswith(("bias", "gain", "shift")))
NS = len(SMALL)
KINDS = ((4 * BLK, TILE), (BLK, 1024), (BLK, D))
PARTS = (
    *((0, TILE * i, 0) for i in range(3)),
    *((1, 1024 * i, 1) for i in range(3)),
    (2, 0, 2),
    *((3, D * i, 2) for i in range(3)),
    (4, 0, 2),
    *((5, D * i, 2) for i in range(3)),
)
NP = len(PARTS)
FIRST_CROSS = 10
OUTS = ((4 * BLK, D), (BLK, FF), (BLK, D), (BLK, 3 * D), (BLK, D), (BLK, 3 * D))
HALF = D // 2
IN_KIND = [sum(p[2] == PARTS[i][2] for p in PARTS[:i]) for i in range(NP)]
COUNT = [sum(p[2] == k for p in PARTS) for k in range(3)]


BY_Y = (10, 12,)
ORDER = (
    (2, 1, 0),
    (1, 2, 0),
    (2, 1, 0),
    (1, 0, 2),
    (2, 1, 0),
    (2, 1, 0),
    (2, 1, 0),
    (2, 1, 0),
    (2, 1, 0),
    (2, 1, 0),
    (2, 1, 0),
    (2, 1, 0),
    (2, 1, 0),
    (2, 1, 0),
)
SERVE = {
    -3: (100,),
    20: (101,),
    21: (102,),
    -6: (103,),
    5: (200,),
    30: (104, 201,),
    31: (105,),
    6: (202,),
    40: (106, 203,),
    42: (300, 204,),
    43: (302,),
    7: (301,),
    -10: (107,),
    33: (108, 303,),
    34: (109, 205, 400,),
    50: (304, 110, 206,),
    51: (402, 401,),
    52: (207, 305,),
    11: (404,),
    12: (306, 208,),
    -14: (111,),
    36: (510, 403, 307, 112,),
    60: (113, 405, 209, 406, 308, 407,),
    61: (211, 309, 210, 408, 311, 512, 213,),
    62: (409, 310, 411, 212, 313, 611,),
    63: (410, 312, 413, 610, 412, 613, 612,),
}


def body(fused, *refs):
    refs = list(refs)

    def take(n):
        got = refs[:n]
        del refs[:n]
        return got

    tok_h, far_h, cot_h, cqkv_h, cout_h, sqkv_h, sout_h, fin_h, fout_h = take(9)
    (mask_in,) = take(1)
    given = dict(zip(SMALL, take(NS)))
    out_o, grad_o, back_o, vec_o = take(4)
    parts_o = take(len(OUTS) if fused else NP)
    (tok, far, cot, wp, wq, xqkv, xatt, joined, hat1, sqkv, satt, settled, hat2, active, inner,
     res, g_low, gpad, rid, columns, slot_a, slot_b, kid_own, kid_far, sv,
     out_f, sems, part_sems) = take(28)
    rows = tok.shape[0]
    groups = rows // GR
    gx = active
    side = lax.axis_index("stream")

    def fetch(i, src, dst):
        c = pltpu.make_async_copy(src, dst, sems.at[i])
        c.start()
        return c

    if fused:
        acc, xr, za, zb, fin = take(3), take(3), take(3), take(3), take(3)
        yr, back, vbuf, ybf = take(4)
        s_core, r_core, s_x, r_x, s_za, r_za, s_zb, r_zb, s_y, r_y, s_yf, r_yf, s_m, r_m = take(14)
        me = lax.axis_index("dp")
        core, x = lax.rem(me, 2), lax.rem(lax.div(me, 2), 2)
        zl, zh = lax.rem(lax.div(me, 4), 2), lax.div(me, 8)
        to_y, to_core = (1 - side, me), (side, me + 1 - 2 * core)
        to_x, to_zl, to_zh = (side, me + 2 - 4 * x), (side, me + 4 - 8 * zl), (side, me + 8 - 16 * zh)
        peers = (to_y, to_core, to_x, to_zl, to_zh)
        barrier = pltpu.get_barrier_semaphore()
        for p in peers:
            pl.semaphore_signal(barrier, inc=1, device_id=p, device_id_type=pl.DeviceIdType.MESH)

        def remote(src, dst, send, recv, peer):
            return pltpu.make_async_remote_copy(
                src_ref=src, dst_ref=dst, send_sem=send, recv_sem=recv,
                device_id=peer, device_id_type=pl.DeviceIdType.MESH,
            )

    c_tok = fetch(0, tok_h, g_low)
    def fetch_self():
        return [
            *(fetch(4 + j, sqkv_h.at[:, j * D : (j + 1) * D], wq.at[j * D : (j + 1) * D, :]) for j in range(3)),
            fetch(7, sout_h, wq.at[3 * D :, :]),
        ]

    c_tok.wait()
    c_cqkv = fetch(1, cqkv_h, wp.at[:, 0 : 3 * D])
    c_cot = fetch(8, cot_h, settled)
    c_cout = fetch(3, cout_h, wp.at[:, 3 * D :])
    if not fused:
        c_far = fetch(2, far_h, satt)

    c_self = fetch_self()
    widen(g_low, out_f)
    if fused:
        pl.semaphore_wait(barrier, len(peers))

        def tokens_to(g):
            at = pl.ds(pl.multiple_of(g * GR, GR), GR)
            return remote(tok.at[at, :], far.at[at, :], s_m.at[g], r_m.at[g], to_y)

    for g in range(groups):
        by_item(out_f, tok, g)
        if fused:
            tokens_to(g).start()

    sm = SimpleNamespace()
    for i, n in enumerate(SMALL):
        row_of = given[n]
        if len(given[n].shape) == 1:
            sv[i : i + 1, :] = given[n][...].reshape(1, D)
            row_of = sv.at[i : i + 1, :]
        setattr(sm, n, row_of)
    vec = vbuf.at[0] if fused else vec_o
    vec[...] = jnp.zeros(vec.shape, F32)
    edge = lax.broadcasted_iota(jnp.int32, (2 * PAD, PAD), 0)
    second = ((edge >= LR) & (edge < PAD)) | (edge >= PAD + LR)
    rid[...] = second.astype(F32)
    items = rows // LR
    present = (mask_in[...] > 0).astype(F32)
    word = (lax.broadcasted_iota(jnp.int32, (items, LR), 1) < LW).astype(F32)
    slot = lax.broadcasted_iota(jnp.int32, (LR, GR), 0)
    lane = lax.broadcasted_iota(jnp.int32, (1, GR), 1)
    lane_item = sum((lane >= LR * i).astype(jnp.int32) for i in range(1, GROUP))
    spread_slots = (slot == lane - LR * lane_item).astype(BF)
    row = lax.broadcasted_iota(jnp.int32, (GR, GR), 0)
    diagonal = row == lax.broadcasted_iota(jnp.int32, (GR, GR), 1)

    def lay_masks(mask, kid, col, own):
        spread = nn(mask.astype(BF), spread_slots)
        for g in range(groups):
            line = jnp.zeros((1, GR), F32)
            for i in range(GROUP):
                line += jnp.where(lane_item == i, spread[g * GROUP + i : g * GROUP + i + 1, :], 0.0)
            ids = jnp.where(line > 0.5, (lane_item % 2).astype(F32), -1.0)
            for half in range(2):
                kid[2 * g + half, :, 0:PAIR] = ids[:, half * PAIR : (half + 1) * PAIR]
                kid[2 * g + half, :, PAIR:] = jnp.full((1, PAD - PAIR), -1.0, F32)
            if own:
                column = jnp.sum(jnp.where(diagonal, line, 0.0), axis=-1, keepdims=True)
                columns[g * GR : (g + 1) * GR, 0:1] = column
            column = jnp.sum(jnp.where(diagonal, ids, 0.0), axis=-1, keepdims=True)
            none = jnp.full((PAD - PAIR, 1), -1.0, F32)
            for half in range(2):
                padded = jnp.concatenate([column[half * PAIR : (half + 1) * PAIR], none], axis=0)
                columns[(2 * g + half) * PAD : (2 * g + half + 1) * PAD, col : col + 1] = padded

    lay_masks(jnp.where(side == 0, word, present), kid_own, 3, True)
    lay_masks(jnp.where(side == 0, present, word), kid_far, 4, False)

    c_cqkv.wait()

    @pl.loop(0, 3)
    def _(j):
        at = tile_at(j)
        store_pairs(xqkv, nn(tok[...], wp[:, at]) + sm.cross_q_bias[:, at], at)

    c_cot.wait()
    widen(settled, out_f)
    for g in range(groups):
        by_item(out_f, cot, g)
    if not fused:
        c_far.wait()
        widen(satt, out_f)
        for g in range(groups):
            by_item(out_f, far, g)

    c_cout.wait()
    for c in c_self:
        c.wait()
    part_rows, part_groups = rows // NH, groups // NH

    @pl.loop(0, NH)
    def _(h):
        first = h * part_rows
        at_h = pl.ds(pl.multiple_of(first, 16), part_rows)

        for q in range(part_groups):
            g = h * part_groups + q
            at_g = pl.ds(pl.multiple_of(g * GR, GR), GR)
            if fused:
                tokens_to(g).wait_recv()
            far_g = far[at_g, :]
            for j in range(3, 9):
                y = nn(far_g, wp[:, j * TILE : (j + 1) * TILE])
                if j >= 6:
                    y = y + sm.cross_v_bias[:, (j - 6) * TILE : (j - 5) * TILE]
                store_pairs(xqkv, y, slice(j * TILE, (j + 1) * TILE), 2 * g)
            attention_forward(g, xqkv, rid, kid_far, xatt)

        res[at_h, :] = tok[at_h, :].astype(F32) + nn(xatt[at_h, :], wp[:, 3 * D :]) + sm.cross_out_bias[...]

        @pl.when(h == NH - 1)
        def _():
            fetch(1, fin_h, wp)

        norm_forward(res, sm.cross_gain, sm.cross_shift, hat1, columns, 1, joined, first, part_rows)
        for part in range(3):
            y = nn(joined[at_h, :], wq[part * D : (part + 1) * D, :])
            if part == 0:
                y = y + sm.self_q_bias[...]
            if part == 2:
                y = y + sm.self_v_bias[...]
            store_pairs(sqkv, y, slice(part * D, (part + 1) * D), 2 * part_groups * h)

        for q in range(part_groups):
            attention_forward(h * part_groups + q, sqkv, rid, kid_own, satt)

        res[at_h, :] += nn(satt[at_h, :], wq[3 * D :, :]) + sm.self_out_bias[...]

        @pl.when(h == NH - 1)
        def _():
            fetch(3, fout_h, wq)

        norm_forward(res, sm.self_gain, sm.self_shift, hat2, columns, 2, settled, first, part_rows)

    pltpu.make_async_copy(fin_h, wp, sems.at[1]).wait()

    @pl.loop(0, FF // TILE)
    def _(j):
        at = tile_at(j)
        x = nn(settled[...], wp[:, at]) + sm.ffn_in_bias[:, at]
        half = 0.5 * (1.0 + lax.erf(x * (0.5**0.5)))
        active[:, at] = (x * half).astype(BF)
        inner[:, at] = x.astype(BF)

    pltpu.make_async_copy(fout_h, wq, sems.at[3]).wait()

    for j in range(3):
        at = slice(j * TILE, (j + 1) * TILE)
        res[:, at] += nn(active[...], wq[:, at]) + sm.ffn_out_bias[:, at]

    @pl.loop(0, rows // LNB)
    def _(i):
        at = tile_at(i, LNB)
        r = res[at, :]
        ok = columns[at, 0:1]
        gain = sm.ffn_gain[...]
        centre = r - jnp.mean(r, axis=-1, keepdims=True)
        rs = lax.rsqrt(jnp.mean(centre * centre, axis=-1, keepdims=True) + 1e-12)
        xh = centre * rs
        y = xh * gain + sm.ffn_shift[...]
        for j in range(D // 128):
            out_f[j, at, :] = y[:, j * 128 : (j + 1) * 128] * ok
        dy = cot[at, :].astype(F32) * ok
        g = norm_grad(dy, xh, rs, gain)
        low = g.astype(BF)
        res[at, :] = g
        cot[at, :] = low
        vec[FGAIN : FGAIN + 1, :] += total(dy * xh)
        vec[FSHIFT : FSHIFT + 1, :] += total(dy)
        vec[FOUTB : FOUTB + 1, :] += total(low)

    def slot_of(i):
        kind = PARTS[i][2]
        if kind == 0:
            return slot_b.at[i % 2]
        ref = slot_a.at[i % 2]
        return ref if kind == 1 else ref.at[:, :, :, :, :, 0:D]

    mv = SimpleNamespace(core={}, y={}, cut={}, yf={}, out={}, acc={}, got={}, fin={})
    if fused:
        here = (zh, zl, x)

        def late(i):
            return [j for j in range(FIRST_CROSS, NP) if j not in BY_Y].index(i)

        over = (to_zh, to_zl, to_x)

        def cut(ref, places, *after):
            return ref.at[(*(places.get(d, slice(None)) for d in range(3)), *after)]

        for i in range(NP):
            out, col, kind = PARTS[i]
            n, width = IN_KIND[i], KINDS[kind][1]
            a = acc[kind].at[n]
            mv.core[i] = remote(slot_of(i).at[1 - core], a, s_core.at[i], r_core.at[i], to_core)
            got = [xr[kind].at[n], za[kind].at[n], zb[kind].at[n]]
            c = i - FIRST_CROSS
            if i in BY_Y:
                mine = pl.ds(pl.multiple_of(side * HALF, HALF), HALF)
                other = pl.ds(pl.multiple_of((1 - side) * HALF, HALF), HALF)
                mv.y[i] = remote(a.at[:, :, :, :, other], yr.at[BY_Y.index(i)], s_y.at[c], r_y.at[c], to_y)
                a = a.at[:, :, :, :, mine]
                short = pl.ds(0, HALF)
                got = [got[0].at[:, :, :, short], got[1].at[:, :, short], got[2].at[:, short]]
                width = HALF
            mv.acc[i], mv.got[i] = a, got
            places = {}
            sems_of = ((s_x, r_x), (s_za, r_za), (s_zb, r_zb))
            for step, d in enumerate(ORDER[i]):
                send, recv = sems_of[step]
                src = cut(a, {**places, d: 1 - here[d]})
                mv.cut[step, i] = remote(src, got[step], send.at[i], recv.at[i], over[d])
                places[d] = here[d]
            if i in BY_Y:
                col0 = pl.ds(pl.multiple_of(col + side * HALF, HALF), HALF)
            else:
                col0 = pl.ds(col, width)
            for place in range(2):
                f = fin[kind].at[place]
                if i in BY_Y:
                    f = f.at[:, 0:HALF]
                    mv.yf[i, place] = remote(f, parts_o[out].at[:, col0], s_yf.at[c], r_yf.at[c], to_y)
                mv.fin[i, place] = f
                mv.out[i, place] = pltpu.make_async_copy(f, parts_o[out].at[:, col0], part_sems.at[i])
            if i >= FIRST_CROSS and i not in BY_Y:
                mv.yf[i, 0] = remote(ybf.at[late(i), 0], ybf.at[late(i), 1], s_yf.at[c], r_yf.at[c], to_y)
        leaving = ([], [], [])


        def leave(i, value):
            before = leaving[PARTS[i][2]]
            place = len(before) % 2
            if len(before) > 1:
                gone(before[-2])
            before.append((i, place))
            mv.fin[i, place][...] = value
            mv.out[i, place].start()
            if i in BY_Y:
                mv.yf[i, place].start()

        def gone(what):
            mv.out[what].wait()
            if what[0] in BY_Y:
                mv.yf[what].wait_send()

        def t1(i):
            mv.core[i].wait_recv()
            out, col, kind = PARTS[i]
            a, own = acc[kind].at[IN_KIND[i]], slot_of(i)

            @pl.loop(0, 8)
            def _(d):
                p, q, r = lax.div(d, 4), lax.rem(lax.div(d, 2), 2), lax.rem(d, 2)
                a[p, q, r] = a[p, q, r] + own[core, p, q, r]

            (mv.y[i] if i in BY_Y else mv.cut[0, i]).start()

        def ty(i):
            mv.y[i].wait_recv()
            a, c = mv.acc[i], BY_Y.index(i)

            @pl.loop(0, 8)
            def _(d):
                p, q, r = lax.div(d, 4), lax.rem(lax.div(d, 2), 2), lax.rem(d, 2)
                a[p, q, r] = a[p, q, r] + yr[c, p, q, r]

            mv.cut[0, i].start()

        def t2(i):
            mv.cut[0, i].wait_recv()
            a, r = mv.acc[i], mv.got[i][0]
            first = ORDER[i][0]

            @pl.loop(0, 4)
            def _(d):
                p, q = lax.div(d, 2), lax.rem(d, 2)
                at = [p, q]
                at.insert(first, here[first])
                at = tuple(at)
                a[at] = a[at] + r[p, q]

            mv.cut[1, i].start()

        def t3(i):
            mv.cut[1, i].wait_recv()
            a, r = mv.acc[i], mv.got[i][1]
            for p in range(2):
                at = list(here)
                at[ORDER[i][2]] = p
                at = tuple(at)
                a[at] = a[at] + r[p]
            mv.cut[2, i].start()

        def t4(i):
            mv.cut[2, i].wait_recv()
            whole = mv.acc[i][zh, zl, x].astype(F32) + mv.got[i][2][...].astype(F32)
            if i >= FIRST_CROSS and i not in BY_Y:
                ybf[late(i), 0] = whole.astype(BF)
                mv.yf[i, 0].start()
            else:
                leave(i, whole)

        def tf(i):
            mv.yf[i, 0].wait_recv()
            if i not in BY_Y:
                leave(i, ybf[late(i), 0].astype(F32) + ybf[late(i), 1].astype(F32))

        steps = (t1, t2, t3, t4, ty, tf)
    left = []
    for i in range(NP):
        left += [n * 100 + i for n in (1, 2, 3, 4) + (5,) * (i in BY_Y) + (6,) * (i >= FIRST_CROSS)]
    core_free = {}

    def serve(place):
        if fused:
            for t in SERVE.get(place, ()):
                left.remove(t)
                steps[t // 100 - 1](t % 100)

    def free_slot(i):
        if i in core_free:
            core_free.pop(i)()

    def push(i):
        if fused:
            mv.core[i].start()
            core_free[i] = mv.core[i].wait_send
        else:
            c = pltpu.make_async_copy(slot_of(i), parts_o[i], part_sems.at[i])
            c.start()
            core_free[i] = c.wait

    def same_slot(i):
        for j in range(i - 1, -1, -1):
            if (PARTS[j][2] == 0) == (PARTS[i][2] == 0) and j % 2 == i % 2:
                return j
        return None

    def weight_part(i, left, right, col0):
        serve(-1 - i)
        free_slot(same_slot(i))
        ref = slot_of(i)
        width = KINDS[PARTS[i][2]][1]

        @pl.loop(0, width // TILE)
        def _(j):
            src = right[:, pl.ds(pl.multiple_of(col0 + j * TILE, TILE), TILE)]
            w = tn(left[...], src).astype(BF)
            for d in range(16):
                ref[d % 2, d // 8, (d // 4) % 2, (d // 2) % 2, :, tile_at(j)] = w[d * BLK : (d + 1) * BLK, :]

        push(i)
        serve(i)

    for col in range(3):
        serve(-1 - col)
        free_slot(same_slot(col))
        ref = slot_of(col)

        @pl.loop(0, 4)
        def _(t):
            w = tn(active[:, tile_at(t, D)], cot[:, col * TILE : (col + 1) * TILE]).astype(BF)
            for d in range(4):
                ref[d % 2, lax.div(t, 2), lax.rem(t, 2), d // 2, :, :] = w[d * 4 * BLK : (d + 1) * 4 * BLK, :]

        push(col)
        serve(col)

    for r in range(3):
        @pl.loop(4 * r, 4 * r + 4)
        def _(j):
            at = tile_at(j)
            ga = nt(cot[...], wq[at, :])
            y = inner[:, at].astype(F32)
            slope = 0.5 * (1.0 + lax.erf(y * (0.5**0.5))) + y * jnp.exp(-0.5 * y * y) * 0.3989422804014327
            gi = (ga * slope).astype(BF)
            inner[:, at] = gi

        serve(20 + r)
    for r in range(4):
        vec[FINB + r : FINB + r + 1, :] = total(inner[:, r * D : (r + 1) * D])
    c_self = fetch_self()

    for col in range(3):
        weight_part(3 + col, settled, inner, col * 1024)

    @pl.loop(0, 3)
    def _(j):
        at = tile_at(j)
        res[:, at] += nt(inner[...], wp[at, :])

    serve(30)
    c_cqkv = fetch(1, cqkv_h, wp.at[:, 0 : 3 * D])
    c_cout = fetch(3, cout_h, wp.at[:, 3 * D :])
    norm_backward(res, sm.self_gain, hat2, columns, 2, g_low, vec, SGAIN, SSHIFT, SOUTB)
    serve(31)
    weight_part(6, satt, g_low, 0)
    for j in range(D // 128):
        by_slot(out_f[j], out_f, j)
        satt[:, j * 128 : (j + 1) * 128] = out_f[j].astype(BF)
    c_out = fetch(8, satt, out_o)
    for c in c_self:
        c.wait()

    @pl.loop(0, 3)
    def _(j):
        at = tile_at(j)
        w_at = pl.ds(pl.multiple_of(3 * D + j * TILE, TILE), TILE)
        store_pairs(gpad, nt(g_low[...], wq[w_at, :]), at)

    serve(32)

    def serve_each(place, g):
        for k in range(groups):
            if fused and SERVE.get(place + k):
                @pl.when(g == k)
                def _():
                    serve(place + k)

    @pl.loop(0, groups)
    def _(g):
        attention_backward(g, sqkv, gpad, columns, 3, gx)
        serve_each(40, g)

    for part in range(3):
        weight_part(7 + part, joined, gx, part * D)
    vec[SQB : SQB + 1, :] = total(gx[:, 0:D])
    vec[SVB : SVB + 1, :] = total(gx[:, 2 * D : 3 * D])

    @pl.loop(0, 3)
    def _(j):
        at = tile_at(j)
        g = res[:, at]
        for part in range(3):
            w_at = pl.ds(pl.multiple_of(part * D + j * TILE, TILE), TILE)
            g += nt(gx[:, part * D : (part + 1) * D], wq[w_at, :])
        res[:, at] = g

    serve(33)
    norm_backward(res, sm.cross_gain, hat1, columns, 1, g_low, vec, CGAIN, CSHIFT, COUTB)
    serve(34)
    weight_part(10, xatt, g_low, 0)
    c_cqkv.wait()
    c_cout.wait()

    @pl.loop(0, 3)
    def _(j):
        at = tile_at(j)
        store_pairs(gpad, nt(g_low[...], wp[at, 3 * D :]), at)

    serve(35)
    if fused:

        def back_to(g):
            at = pl.ds(pl.multiple_of(g * GR, GR), GR)
            return remote(g_low.at[at, :], back.at[at, :], s_m.at[groups + g], r_m.at[groups + g], to_y)

    @pl.loop(0, groups)
    def _(g):
        attention_backward(g, xqkv, gpad, columns, 4, gx)
        at = pl.ds(pl.multiple_of(g * GR, GR), GR)
        pair = gx[at, D : 3 * D]
        for j in range(3):
            w_at = slice(j * TILE, (j + 1) * TILE)
            g_low[at, w_at] = nt(pair, wp[w_at, D : 3 * D]).astype(BF)
        if fused:
            back_to(g).start()
        serve_each(50, g)

    vec[CQB : CQB + 1, :] = total(gx[:, 0:D])
    vec[CVB : CVB + 1, :] = total(gx[:, 2 * D : 3 * D])
    if fused:
        v_at = [
            remote(vbuf.at[j % 2], vbuf.at[2 + j], s_m.at[2 * groups + j], r_m.at[2 * groups + j], p)
            for j, p in enumerate((to_core, to_x, to_zl, to_zh))
        ]
        v_y = remote(vbuf.at[0], vbuf.at[6], s_m.at[2 * groups + 4], r_m.at[2 * groups + 4], to_y)

        def vec_step(j):
            v_at[j].wait_recv()
            if j > 0:
                v_at[j - 1].wait_send()
            vbuf[(j + 1) % 2] = vbuf[j % 2] + vbuf[2 + j]
            (v_at[j + 1] if j < 3 else v_y).start()

        v_at[0].start()
    weight_part(11, tok, gx, 0)
    weight_part(12, far, gx, D)
    if fused:
        vec_step(0)
    weight_part(13, far, gx, 2 * D)

    @pl.loop(0, 3)
    def _(j):
        at = tile_at(j)
        res[:, at] += nt(gx[:, 0:D], wp[at, 0:D])

    if not fused:
        for src, dst in ((g_low, back_o), (res, grad_o)):
            for j in range(D // 128):
                by_slot(src[:, j * 128 : (j + 1) * 128].astype(F32), out_f, j)
                fetch(0, out_f.at[j], dst.at[:, j * 128 : (j + 1) * 128]).wait()
        for done in core_free.values():
            done()
        c_out.wait()
        return

    serve(36)
    vec_step(1)
    serve(60)
    for g in range(groups):
        back_to(g).wait()

    c_grad = []
    for j in range(D // 128):
        cols = slice(j * 128, (j + 1) * 128)
        by_slot(res[:, cols] + back[:, cols].astype(F32), out_f, j)
        c_grad.append(pltpu.make_async_copy(out_f.at[j], grad_o.at[:, cols], sems.at[j]))
        c_grad[-1].start()
    serve(61)
    vec_step(2)
    serve(62)
    vec_step(3)
    serve(63)
    v_y.wait_recv()
    vec_o[...] = vbuf[0]
    vec_o[12:, :] = vbuf[0, 12:, :] + vbuf[6, 12:, :]
    for done in core_free.values():
        done()
    for i in range(NP):
        if i in BY_Y:
            mv.y[i].wait_send()
        for step in range(3):
            mv.cut[step, i].wait_send()
    for before in leaving:
        for what in before[-2:]:
            gone(what)
    for i in range(FIRST_CROSS, NP):
        if i not in BY_Y:
            mv.yf[i, 0].wait_send()
    v_at[3].wait_send()
    v_y.wait_send()
    for g in range(groups):
        tokens_to(g).wait_send()
    c_out.wait()
    for c in c_grad:
        c.wait()
    assert not left


def compute(rows, fused, arrays):
    any_space = pl.BlockSpec(memory_space=pl.ANY)
    vmem = pl.BlockSpec(memory_space=pltpu.VMEM)
    if fused:
        out_parts = [jax.ShapeDtypeStruct(o, F32) for o in OUTS]
    else:
        out_parts = [jax.ShapeDtypeStruct((2, 2, 2, 2, *KINDS[k]), BF) for _, _, k in PARTS]
    low = lambda n=D: pltpu.VMEM((rows, n), BF)
    wide = lambda n: pltpu.VMEM((rows // PAIR * PAD, n), BF)
    dma = lambda n: pltpu.SemaphoreType.DMA((n,))
    scratch = [
        low(), low(), low(),
        pltpu.VMEM((D, FF), BF), pltpu.VMEM((FF, D), BF),
        wide(3 * D), low(), low(), low(),
        wide(3 * D), low(), low(), low(),
        low(FF), low(FF),
        pltpu.VMEM((rows, D), F32), low(), wide(D),
        pltpu.VMEM((2 * PAD, PAD), F32),
        pltpu.VMEM((rows // PAIR * PAD, 128), F32),
        pltpu.VMEM((2, 2, 2, 2, 2, BLK, 1024), BF), pltpu.VMEM((2, 2, 2, 2, 2, 4 * BLK, TILE), BF),
        pltpu.VMEM((rows // PAIR, 1, PAD), F32), pltpu.VMEM((rows // PAIR, 1, PAD), F32),
        pltpu.VMEM((8, D), F32),
        pltpu.VMEM((D // 128, rows, 128), F32),
        dma(9), dma(NP),
    ]
    params = dict(vmem_limit_bytes=int(63.9 * 2**20))
    if fused:
        for lead in ((2, 2, 2), (2, 2), (2,), ()):
            scratch += [pltpu.VMEM((COUNT[k], *lead, *KINDS[k]), BF) for k in range(3)]
        scratch += [pltpu.VMEM((2, *KINDS[k]), F32) for k in range(3)]
        cross = NP - FIRST_CROSS
        scratch += [
            pltpu.VMEM((max(len(BY_Y), 1), 2, 2, 2, BLK, HALF), BF), low(), pltpu.VMEM((7, NV, D), F32),
            pltpu.VMEM((max(cross - len(BY_Y), 1), 2, BLK, D), BF),
            *([dma(NP)] * 8), *([dma(cross)] * 4), dma(2 * rows // GR + 5), dma(2 * rows // GR + 5),
        ]
        params.update(collective_id=0, has_side_effects=True)
    return pl.pallas_call(
        partial(body, fused),
        out_shape=[
            jax.ShapeDtypeStruct((rows, D), BF),
            jax.ShapeDtypeStruct((rows, D), F32),
            jax.ShapeDtypeStruct((8, 128) if fused else (rows, D), F32),
            jax.ShapeDtypeStruct((NV, D), F32),
            *out_parts,
        ],
        in_specs=[any_space] * 9 + [vmem] * (1 + NS),
        out_specs=[any_space] * 3 + [vmem] + [any_space] * len(out_parts),
        scratch_shapes=scratch,
        compiler_params=pltpu.CompilerParams(**params),
    )(*arrays)


VECTORS = (CQB, CVB, COUTB, CGAIN, CSHIFT, SQB, SVB, SOUTB, SGAIN, SSHIFT, FOUTB, FGAIN, FSHIFT)


def finish_body(n, *refs):
    vec, refs = refs[0], refs[1:]
    count = (len(refs) - len(VECTORS) - 2) // 3
    given, refs = refs[:count], refs[count:]
    vectors, finb, refs = refs[: len(VECTORS)], refs[len(VECTORS)], refs[len(VECTORS) + 1 :]
    out, sems, held = refs[:count], refs[count], refs[count + 1 :]
    into = [pltpu.make_async_copy(a, b, sems.at[i]) for i, (a, b) in enumerate(zip(given, held))]
    away = [pltpu.make_async_copy(a, b, sems.at[i]) for i, (a, b) in enumerate(zip(held, out))]
    for c in into:
        c.start()
    me = lax.axis_index("dp")
    share = D // n
    mine = pltpu.roll(vec[...], lax.rem(D - me * share, D), 1)
    for r, v in zip(VECTORS, vectors):
        v[...] = mine[r : r + 1, 0:share].reshape(v.shape)
    share = FF // n
    a_row = D // share
    v = vec[FINB : FINB + 8, :]
    at = lax.broadcasted_iota(jnp.int32, v.shape, 0) == lax.div(me, a_row)
    line = jnp.broadcast_to(jnp.sum(jnp.where(at, v, 0.0), axis=0, keepdims=True), v.shape)
    finb[...] = pltpu.roll(line, lax.rem(D - lax.rem(me, a_row) * share, D), 1)[0:1, 0:share]
    for a, b in zip(into, away):
        a.wait()
        b.start()
    for b in away:
        b.wait()


def finish(n, vec, arrays):
    any_space = pl.BlockSpec(memory_space=pl.ANY)
    vmem = pl.BlockSpec(memory_space=pltpu.VMEM)
    share = D // n
    shapes = [(share,)] * 5 + [(1, share)] * 8 + [(1, FF // n)]
    return pl.pallas_call(
        partial(finish_body, n),
        out_shape=[
            *(jax.ShapeDtypeStruct(s, F32) for s in shapes),
            *(jax.ShapeDtypeStruct(x.shape, x.dtype) for x in arrays),
        ],
        in_specs=[vmem] + [any_space] * len(arrays),
        out_specs=[vmem] * len(shapes) + [any_space] * len(arrays),
        scratch_shapes=[
            pltpu.SemaphoreType.DMA((max(len(arrays), 1),)),
            *(pltpu.VMEM(x.shape, x.dtype) for x in arrays),
        ],
        compiler_params=pltpu.CompilerParams(vmem_limit_bytes=int(63.9 * 2**20)),
    )(vec, *arrays)


def partner(block):
    return lax.ppermute(block, "stream", [(0, 1), (1, 0)])


def reduce_parts(parts, vec):
    def natural(some):
        done = []
        for p in some:
            r, n = p.shape[-2:]
            done.append(p.transpose(1, 2, 3, 0, 4, 5).reshape(16 * r, n))
        return jnp.concatenate(done, axis=1)

    def scatter(some, shared=False):
        x = natural(some)
        if shared:
            x = lax.psum(x, "stream")
        return lax.psum_scatter(x, "dp", scatter_dimension=0, tiled=True).astype(F32)

    sums = [
        scatter(parts[0:3]), scatter(parts[3:6]), scatter(parts[6:7]), scatter(parts[7:10]),
        scatter(parts[10:11], True), scatter(parts[11:14], True),
    ]
    own = lax.psum(vec[:CGAIN], "dp")
    return sums, jnp.concatenate([own, lax.psum(vec[CGAIN:], ("stream", "dp"))])


def local(*args):
    a = dict(zip(NAMES, args))
    n = lax.axis_size("dp")
    fused = n == 16
    shape = a["tokens"].shape
    items = shape[1]

    def to_slots(v):
        return v[0].transpose(1, 0, 2).reshape(items * LR, D)

    def back_to_items(v):
        return v.reshape(LR, items, D).transpose(1, 0, 2).reshape(shape)

    tok, cot = to_slots(a["tokens"]), to_slots(a["cotangent"])
    far = tok if fused else partner(tok)
    outs = compute(
        items * LR,
        fused,
        [tok, far, cot, a["cross_qkv"], a["cross_out"], a["self_qkv"][0], a["self_out"][0],
         a["ffn_in"][0], a["ffn_out"][0], a["region_mask"], *(a[k] for k in SMALL)],
    )
    stream, grad, back, vec = outs[:4]
    sums = outs[4:]
    if not fused:
        grad = grad + partner(back.astype(BF)).astype(F32)
        sums, vec = reduce_parts(sums, vec)
    done = finish(n, vec, [stream, grad, *sums] if fused else [])
    if fused:
        stream, grad, *sums = done[14:]
    fout, fin, sout, sqkv, cout, cqkv = sums
    cqb, cvb, coutb, cgain, cshift, sqb, svb, soutb, sgain, sshift, foutb, fgain, fshift, finb = done[:14]
    return (
        back_to_items(stream), back_to_items(grad),
        cqkv, cqb, cvb, cout, coutb, cgain, cshift,
        sqkv[None], sqb, svb, sout[None], soutb, sgain, sshift,
        fin[None], finb, fout[None], foutb, fgain, fshift,
    )


def solution(mesh):
    both = P("stream", "dp")
    one = P("stream")
    specs = {n: one for n in NAMES}
    specs.update({n: P() for n in NAMES if n.startswith("cross")})
    specs.update(tokens=both, cotangent=both, region_mask=P("dp"))
    return jax.shard_map(
        local,
        mesh=mesh,
        in_specs=tuple(specs[n] for n in NAMES),
        out_specs=(both, both) + (P("dp"),) * 7 + (both,) * 13,
        check_vma=False,
    )
```
